32 devices in a mesh: tm: 4 (over y, core), space: 8 (over z, x).
Axes of the slice: x: 2, y: 2, z: 4, core: 2. Of those that a mesh axis runs over, the one named last changes fastest.
Arguments:
- queries: bfloat16 [4, 8, 384, 1536], P('tm', 'space'), may hold values from -7 to 7
- keys: bfloat16 [4, 8, 384, 1536], P('tm', 'space'), may hold values from -7 to 7
- values: bfloat16 [4, 8, 384, 1536], P('tm', 'space'), may hold values from -2 to 2
- outputs: bfloat16 [4, 8, 384, 1536], P('tm', 'space'), may hold values from -2 to 2
- out_grads: bfloat16 [4, 8, 384, 1536], P('tm', 'space'), may hold values from -6 to 6
- log_sums: float32 [4, 8, 12, 384], P('tm', 'space'), may hold values from 8 to 9.5
- window_mask: int32 [4, 8, 9], P('tm', 'space'), may hold values 0 or 1
Outputs:
- query_grads: bfloat16 [4, 8, 384, 1536], P('tm', 'space')
- key_grads: bfloat16 [4, 8, 384, 1536], P('tm', 'space')
- value_grads: bfloat16 [4, 8, 384, 1536], P('tm', 'space')
The draws below stay inside these ranges and needn't reach their ends.
All inputs are finite; a program needn't handle non-finite values. No bound on the sum of `window_mask` on one device may be relied on, other than what follows from the above.
Results may differ from the reference program's by a relative error of at most 0.0065.
Values may be sent and summed in bfloat16 or wider, within the bound.
No kernel may reach another device: no remote copies, remote signals or barrier semaphores. Data moves between devices by JAX's collectives and lax.ppermute only.
A program may use at most 192 MiB of HBM per device.

```python
import jax
import jax.numpy as jnp
from jax import lax

HEADS = 12
HEAD_DIM = 128
TILE = 384
WINDOW = 3
NT = 4
NR = 8


def place_ends(drawn, key, low, top_value):
    extent = drawn.shape
    place = [jax.random.randint(jax.random.fold_in(key, axis), (), 0, extent[axis]) for axis in range(len(extent))]
    drawn = drawn.at[tuple(place)].set(low)
    longest = extent.index(max(extent))
    place[longest] = (place[longest] + 1) % extent[longest]
    return drawn.at[tuple(place)].set(top_value)


def level_of(own_key, extent, cuts, smallest, high):
    factor_of, own = 1.0, jax.random.fold_in(own_key, 6)
    for position, blocks in cuts:
        steps = jnp.exp(jax.random.uniform(jax.random.fold_in(own, position), (blocks,), jnp.float32, smallest / len(cuts), high / len(cuts)))
        factor_of = factor_of * jnp.repeat(steps, extent[position] // blocks).reshape([-1 if axis == position else 1 for axis in range(len(extent))])
    return factor_of


def bell_draw(rng, extent, width, limit, shards=(), kind=jnp.bfloat16):
    entries = width * jax.random.normal(rng, extent, jnp.float32)
    if shards:
        entries = entries * level_of(rng, extent, shards, -0.22, 0.18)
    return jnp.clip(entries, -limit, limit).astype(kind)


def setup_inputs(seed: int = 0) -> dict:
    arg_keys = jax.random.split(jax.random.key(seed), 8)
    return {
        "queries": bell_draw(arg_keys[0], (NT, NR, TILE, HEADS * HEAD_DIM), 1.2, 7.0, ((0, 4), (1, 8))),
        "keys": bell_draw(arg_keys[1], (NT, NR, TILE, HEADS * HEAD_DIM), 1.2, 7.0, ((0, 4), (1, 8))),
        "values": bell_draw(arg_keys[2], (NT, NR, TILE, HEADS * HEAD_DIM), 0.3, 2.0, ((0, 4), (1, 8))),
        "outputs": bell_draw(arg_keys[3], (NT, NR, TILE, HEADS * HEAD_DIM), 0.3, 2.0, ((0, 4), (1, 8))),
        "out_grads": bell_draw(arg_keys[4], (NT, NR, TILE, HEADS * HEAD_DIM), 1.0, 6.0, ((0, 4), (1, 8))),
        "log_sums": jnp.clip(8.0 + 1.5 * jax.random.uniform(arg_keys[5], (NT, NR, HEADS, TILE), jnp.float32) ** level_of(arg_keys[5], (NT, NR, HEADS, TILE), ((0, 4), (1, 8)), -0.2, 0.2), 8.0, 9.5),
        "window_mask": place_ends((jax.random.randint(arg_keys[6], (NT, NR, WINDOW * WINDOW), 0, 4) < 3).astype(jnp.int32), jax.random.fold_in(arg_keys[6], 1), 0, 1),
    }


def round_keep(value):
    return lax.optimization_barrier(value.astype(jnp.bfloat16)).astype(jnp.float32)


def pair_terms(query_rows, grad_rows, sum_rows, delta_rows, flags, key_rows, value_rows):
    num_tiles = query_rows.shape[0]
    shape_four = (num_tiles, TILE, HEADS, HEAD_DIM)
    factor = HEAD_DIM ** -0.5
    query_heads = query_rows.reshape(shape_four).astype(jnp.float32)
    grad_heads = grad_rows.reshape(shape_four).astype(jnp.float32)
    key_heads = key_rows.reshape(shape_four).astype(jnp.float32)
    value_heads = value_rows.reshape(shape_four).astype(jnp.float32)
    scores = jnp.einsum("nqhd,nkhd->nhqk", query_heads, key_heads) * factor
    weights = jnp.exp(scores - sum_rows[..., None]) * flags[:, None, None, None]
    weights_low = round_keep(weights)
    grad_prob = jnp.einsum("nqhd,nkhd->nhqk", grad_heads, value_heads)
    grad_score = round_keep(weights * (grad_prob - delta_rows[..., None]))
    query_term = jnp.einsum("nhqk,nkhd->nqhd", grad_score, key_heads) * factor
    key_term = jnp.einsum("nhqk,nqhd->nkhd", grad_score, query_heads) * factor
    value_term = jnp.einsum("nhqk,nqhd->nkhd", weights_low, grad_heads)
    flat = (num_tiles, TILE, HEADS * HEAD_DIM)
    return query_term.reshape(flat), key_term.reshape(flat), value_term.reshape(flat)


def reference(queries, keys, values, outputs, out_grads, log_sums, window_mask):
    full_width = HEADS * HEAD_DIM
    padding = ((1, 1), (1, 1), (0, 0), (0, 0))
    keys_pad = jnp.pad(keys, padding)
    values_pad = jnp.pad(values, padding)
    products = out_grads.astype(jnp.float32) * outputs.astype(jnp.float32)
    deltas = products.reshape(NT, NR, TILE, HEADS, HEAD_DIM).sum(-1).transpose(0, 1, 3, 2)
    row_ids = jnp.arange(NR)

    def per_time(time_id):
        query_rows = lax.dynamic_index_in_dim(queries, time_id, 0, False)
        grad_rows = lax.dynamic_index_in_dim(out_grads, time_id, 0, False)
        sum_rows = lax.dynamic_index_in_dim(log_sums, time_id, 0, False)
        delta_rows = lax.dynamic_index_in_dim(deltas, time_id, 0, False)
        mask_rows = lax.dynamic_index_in_dim(window_mask, time_id, 0, False)
        query_total = jnp.zeros((NR, TILE, full_width), jnp.float32)
        grouped = []
        for time_off in (-1, 0, 1):
            inner = jnp.zeros((2, NR + 2, TILE, full_width), jnp.float32)
            key_plane = lax.dynamic_index_in_dim(keys_pad, time_id + 1 + time_off, 0, False)
            value_plane = lax.dynamic_index_in_dim(values_pad, time_id + 1 + time_off, 0, False)
            time_inside = jnp.logical_and(time_id + time_off >= 0, time_id + time_off < NT)
            for row_off in (-1, 0, 1):
                slot_index = (time_off + 1) * 3 + row_off + 1
                row_inside = jnp.logical_and(row_ids + row_off >= 0, row_ids + row_off < NR)
                if slot_index == 4:
                    picked = jnp.ones((NR,), jnp.float32)
                else:
                    picked = (mask_rows[:, slot_index] > 0).astype(jnp.float32)
                flags = picked * jnp.logical_and(row_inside, time_inside).astype(jnp.float32)
                key_rows = key_plane[1 + row_off:1 + row_off + NR]
                value_rows = value_plane[1 + row_off:1 + row_off + NR]
                query_term, key_term, value_term = pair_terms(query_rows, grad_rows, sum_rows, delta_rows, flags, key_rows, value_rows)
                query_total = query_total + query_term
                parts = round_keep(jnp.stack((key_term, value_term)))
                inner = inner.at[:, 1 + row_off:1 + row_off + NR].add(parts)
            grouped.append(inner[:, 1:NR + 1].astype(jnp.bfloat16))
        return query_total.astype(jnp.bfloat16), jnp.stack(grouped)

    query_grads, groups = lax.map(per_time, jnp.arange(NT))
    total = jnp.zeros((2, NT + 2, NR, TILE, full_width), jnp.float32)
    for time_off in (-1, 0, 1):
        piece = groups[:, time_off + 1].transpose(1, 0, 2, 3, 4).astype(jnp.float32)
        total = total.at[:, 1 + time_off:1 + time_off + NT].add(piece)
    key_grads = total[0, 1:NT + 1].astype(jnp.bfloat16)
    value_grads = total[1, 1:NT + 1].astype(jnp.bfloat16)
    return query_grads, key_grads, value_grads
```

```python
import functools
import math

import jax
import jax.numpy as jnp
from jax import lax
from jax.experimental import pallas as pl
from jax.experimental.pallas import tpu as pltpu
from jax.sharding import PartitionSpec as P

F32 = jnp.float32
BF16 = jnp.bfloat16
LOG2E = math.log2(math.e)
FAR = 1e30
CHUNKS = (4, 4, 4)


def dot(a, b, dims):
    return lax.dot_general(a, b, (dims, ((), ())), preferred_element_type=F32)


def prep_kernel(chunks, q_ref, g_ref, o_ref, lse_ref, flag_ref, *outs):
    stat_ref = outs[-1]
    h = pl.program_id(0)
    heads = pl.num_programs(0)
    prod = g_ref[...].astype(F32) * o_ref[...].astype(F32)
    stat_ref[h, 1:2, :] = jnp.sum(prod.T, axis=0, keepdims=True)
    stat_ref[h, 0:1, :] = lse_ref[pl.ds(h, 1), :] * LOG2E

    @pl.when(h == 0)
    def _():
        stat_ref[heads, :, :] = flag_ref[...]

    first = 0
    for count, out in zip(chunks, outs):

        @pl.when((h >= first) & (h < first + count))
        def _(out=out):
            out[0] = q_ref[...]
            out[1] = g_ref[...]

        first += count


def prep(chunks, head_width, q, g, o, lse, flags):
    tile, full = q.shape
    heads = full // head_width
    cols = pl.BlockSpec((tile, head_width), lambda h: (0, h))

    def chunk_spec(first, count):
        return pl.BlockSpec(
            (2, tile, head_width), lambda h: (0, 0, jnp.clip(h - first, 0, count - 1))
        )

    specs, shapes, first = ([], [], 0)
    for count in chunks:
        specs.append(chunk_spec(first, count))
        shapes.append(jax.ShapeDtypeStruct((2, tile, count * head_width), BF16))
        first += count
    return pl.pallas_call(
        functools.partial(prep_kernel, chunks),
        grid=(heads,),
        in_specs=[
            cols,
            cols,
            cols,
            pl.BlockSpec((heads, tile), lambda h: (0, 0)),
            pl.BlockSpec((2, tile), lambda h: (0, 0)),
        ],
        out_specs=specs + [pl.BlockSpec((heads + 1, 2, tile), lambda h: (0, 0, 0))],
        out_shape=shapes + [jax.ShapeDtypeStruct((heads + 1, 2, tile), F32)],
        cost_estimate=pl.CostEstimate(
            flops=2 * tile * full, bytes_accessed=10 * tile * full, transcendentals=0
        ),
        name="prep",
    )(q, g, o, lse, flags)


def pair_kernel(
    first, heads, factor, far_ref,
    q_ref, g_ref, x_ref, z_ref, k_ref, v_ref, kn_ref, vn_ref, kf_ref, vf_ref,
    so_ref, sx_ref, sz_ref,
    dq_own, dq_partner, dq_outer, dkv_own, dkv_near, dkv_far, acc,
):
    h = pl.program_id(0) + first
    queries = (z_ref.at[0], q_ref, x_ref.at[0])
    grads = (z_ref.at[1], g_ref, x_ref.at[1])
    stats = (sz_ref, so_ref, sx_ref)

    def key_slot(slot, key, value):
        dk = None
        dv = None
        for j in range(3):
            qj = queries[j][...]
            gj = grads[j][...]
            lane = 3 * j + slot
            flag = stats[j][heads, 0:1, lane : lane + 1]
            shift = jnp.where(flag > 0, stats[j][h, 0:1, :], FAR)
            delta = stats[j][h, 1:2, :]
            scores = dot(key, qj, ((1,), (1,)))
            weights = jnp.exp2(scores * (factor * LOG2E) - shift)
            grad_prob = dot(value, gj, ((1,), (1,)))
            grad_score = (weights * (grad_prob - delta)).astype(BF16)
            term_v = dot(weights.astype(BF16), gj, ((1,), (0,)))
            term_k = dot(grad_score, qj, ((1,), (0,)))
            term_q = dot(grad_score, key, ((0,), (0,)))
            dv = term_v if dv is None else dv + term_v
            dk = term_k if dk is None else dk + term_k
            acc[j] = term_q if slot == 0 else acc[j] + term_q
        return (dk * factor, dv)

    dk, dv = key_slot(0, k_ref[...], v_ref[...])
    dkv_own[0] = dk
    dkv_own[1] = dv
    dk, dv = key_slot(1, kn_ref[...], vn_ref[...])
    dkv_near[0] = dk.astype(BF16)
    dkv_near[1] = dv.astype(BF16)

    @pl.when(far_ref[0] > 0)
    def _():
        dk, dv = key_slot(2, kf_ref[...], vf_ref[...])
        dkv_far[0] = dk.astype(BF16)
        dkv_far[1] = dv.astype(BF16)

    @pl.when(far_ref[0] == 0)
    def _():
        dkv_far[...] = jnp.zeros_like(dkv_far)

    dq_outer[...] = (acc[0] * factor).astype(BF16)
    dq_own[...] = acc[1] * factor
    dq_partner[...] = acc[2] * factor


def pair_call(first, count, head_width, far, q, g, x, z, kv, near, far_kv, so, sx, sz):
    tile, full = q.shape
    heads = full // head_width
    wide = count * head_width
    cols = pl.BlockSpec((tile, head_width), lambda h, *_: (0, h + first))
    part = pl.BlockSpec((2, tile, head_width), lambda h, *_: (0, 0, h))
    stat = pl.BlockSpec((heads + 1, 2, tile), lambda h, *_: (0, 0, 0))
    one = pl.BlockSpec((tile, head_width), lambda h, *_: (0, h))
    two = lambda kind: jax.ShapeDtypeStruct((2, tile, wide), kind)
    single = lambda kind: jax.ShapeDtypeStruct((tile, wide), kind)
    pairs = 9 * count
    return pl.pallas_call(
        functools.partial(pair_kernel, first, heads, head_width**-0.5),
        grid_spec=pltpu.PrefetchScalarGridSpec(
            num_scalar_prefetch=1,
            grid=(count,),
            in_specs=[cols, cols, part, part] + [cols] * 6 + [stat] * 3,
            out_specs=[one, one, one, part, part, part],
            scratch_shapes=[pltpu.VMEM((3, tile, head_width), F32)],
        ),
        out_shape=[single(F32), single(F32), single(BF16), two(F32), two(BF16), two(BF16)],
        compiler_params=pltpu.CompilerParams(vmem_limit_bytes=40 * 1024 * 1024),
        cost_estimate=pl.CostEstimate(
            flops=20 * pairs * tile * tile * head_width,
            bytes_accessed=40 * tile * wide,
            transcendentals=pairs * tile * tile,
        ),
        name="pairs",
    )(far, q, g, x, z, *kv, *near, *far_kv, so, sx, sz)


def finish_kernel(own_q, back_q, own_kv, near, far, *rest):
    out_q, out_k, out_v = rest[-3:]
    out_q[...] = (own_q[...] + back_q[...].astype(F32)).astype(BF16)
    sums = own_kv[...] + near[...].astype(F32) + far[...].astype(F32)
    out_k[...] = sums[0].astype(BF16)
    out_v[...] = sums[1].astype(BF16)


def finish(first, count, head_width, full, parts, so_far):
    tile = parts[0].shape[0]
    one = pl.BlockSpec((tile, head_width), lambda h: (0, h))
    two = pl.BlockSpec((2, tile, head_width), lambda h: (0, 0, h))
    cols = pl.BlockSpec((tile, head_width), lambda h: (0, h + first))
    kept = [] if so_far is None else list(so_far)
    return pl.pallas_call(
        finish_kernel,
        grid=(count,),
        in_specs=[one, one, two, two, two] + [pl.BlockSpec(memory_space=pl.ANY)] * len(kept),
        out_specs=[cols] * 3,
        out_shape=[jax.ShapeDtypeStruct((tile, full), BF16)] * 3,
        input_output_aliases={5 + i: i for i in range(len(kept))},
        cost_estimate=pl.CostEstimate(
            flops=8 * tile * count * head_width,
            bytes_accessed=30 * tile * count * head_width,
            transcendentals=0,
        ),
        name="finish",
    )(*parts, *kept)


def pair_flags(window_mask, tile):
    mask = window_mask.reshape(9)
    frames, rows = (lax.axis_size("tm"), lax.axis_size("space"))
    frame, row = (lax.axis_index("tm"), lax.axis_index("space"))
    toward = 1 - 2 * lax.rem(row, 2)
    near = 1 - 2 * lax.rem(frame, 2)
    lane = jnp.arange(9, dtype=jnp.int32)
    row_off = (lane // 3 - 1) * toward
    slot = lane % 3
    frame_off = jnp.where(slot == 1, near, jnp.where(slot == 2, -near, 0))
    inside = (
        (row + row_off >= 0)
        & (row + row_off < rows)
        & (frame + frame_off >= 0)
        & (frame + frame_off < frames)
    )
    index = 3 * (frame_off + 1) + row_off + 1
    picked = jnp.sum(
        jnp.where(index[:, None] == lane[None, :], mask[None, :], 0), axis=1
    )
    flags = (inside & ((picked > 0) | (index == 4))).astype(F32)
    return jnp.zeros((2, tile), F32).at[0, :9].set(flags)


def per_device(queries, keys, values, outputs, out_grads, log_sums, window_mask):
    tile, full = queries.shape[2:]
    heads = log_sums.shape[2]
    head_width = full // heads
    frames, rows = (lax.axis_size("tm"), lax.axis_size("space"))
    q, k, v, o, g = (
        a.reshape(tile, full) for a in (queries, keys, values, outputs, out_grads)
    )
    partner = [(i, i ^ 1) for i in range(rows)]
    onward = [(i, i + 2) for i in range(0, rows - 2, 2)]
    onward += [(i, i - 2) for i in range(3, rows, 2)]
    homeward = [(b, a) for a, b in onward]
    near_pairs = [(i, i ^ 1) for i in range(frames)]
    far_pairs = [(i, i + 1) for i in range(1, frames - 1, 2)]
    far_pairs += [(b, a) for a, b in far_pairs]

    frame = lax.axis_index("tm")
    far_frame = frame - 1 + 2 * lax.rem(frame, 2)
    has_far = ((far_frame >= 0) & (far_frame < frames)).astype(jnp.int32).reshape(1)

    flags = pair_flags(window_mask, tile)
    *packed, stats = prep(
        CHUNKS, head_width, q, g, o, log_sums.reshape(heads, tile), flags
    )
    near_kv = [lax.ppermute(a, "tm", near_pairs) for a in (k, v)]
    far_kv = [lax.ppermute(a, "tm", far_pairs) for a in (k, v)]
    stats_x = lax.ppermute(stats, "space", partner)
    stats_z = lax.ppermute(stats_x, "space", onward)
    from_partner = [lax.ppermute(a, "space", partner) for a in packed]
    from_outer = [lax.ppermute(a, "space", onward) for a in from_partner]

    out = None
    first = 0
    for count, x, z in zip(CHUNKS, from_partner, from_outer):
        dq_own, dq_partner, dq_outer, dkv_own, dkv_near, dkv_far = pair_call(
            first, count, head_width, has_far, q, g, x, z,
            (k, v), near_kv, far_kv, stats, stats_x, stats_z,
        )
        home = lax.ppermute(dq_outer, "space", homeward)
        dq_back = lax.ppermute(
            (dq_partner + home.astype(F32)).astype(BF16), "space", partner
        )
        near_back = lax.ppermute(dkv_near, "tm", near_pairs)
        far_back = lax.ppermute(dkv_far, "tm", far_pairs)
        out = finish(
            first, count, head_width, full,
            (dq_own, dq_back, dkv_own, near_back, far_back), out,
        )
        first += count
    return tuple(a.reshape(queries.shape) for a in out)


def solution(mesh):
    tile = P("tm", "space", None, None)
    return jax.shard_map(
        per_device,
        mesh=mesh,
        in_specs=(tile,) * 6 + (P("tm", "space", None),),
        out_specs=(tile,) * 3,
        check_vma=False,
    )
```

```python
import functools
import math

import jax
import jax.numpy as jnp
from jax import lax
from jax.experimental import pallas as pl
from jax.experimental.pallas import tpu as pltpu
from jax.sharding import PartitionSpec as P

F32 = jnp.float32
BF16 = jnp.bfloat16
LOG2E = math.log2(math.e)
FAR_AWAY = 1e30

OUTER, OWN, PARTNER = (0, 1, 2)
HERE, NEAR, FAR = (0, 1, 2)
CHUNKS = (3, 3, 3, 3)
STAGES = (
    ((HERE, (OWN, PARTNER)), (NEAR, (OWN, PARTNER))),
    ((HERE, (OUTER,)), (NEAR, (OUTER,)), (FAR, (OWN, PARTNER, OUTER))),
)
EXTRA = 32


def dot(a, b, dims):
    return lax.dot_general(a, b, (dims, ((), ())), preferred_element_type=F32)


def three_terms(row):
    terms = []
    for _ in range(3):
        term = row.astype(BF16).astype(F32)
        terms.append(term)
        row = row - term
    return terms


def fold(row):
    lanes = 128
    return [row[:, i : i + lanes] for i in range(0, row.shape[1], lanes)]


def prep_kernel(first, count, q_ref, g_ref, o_ref, lse_ref, flag_ref, out):
    tile = q_ref.shape[0]
    width = q_ref.shape[1] // count
    out[0:tile, :] = q_ref[...]
    out[tile : 2 * tile, :] = g_ref[...]
    ones = jnp.ones((8, width), BF16)
    for h in range(count):
        cols = slice(h * width, (h + 1) * width)
        prod = g_ref[:, cols].astype(F32) * o_ref[:, cols].astype(F32)
        high = prod.astype(BF16)
        low = (prod - high.astype(F32)).astype(BF16)
        delta = dot(ones, high, ((1,), (1,))) + dot(ones, low, ((1,), (1,)))
        rows = []
        for row in (lse_ref[first + h : first + h + 1, :] * LOG2E, delta[0:1, :]):
            for term in three_terms(row):
                rows += fold(term)
        rows.append(flag_ref[...])
        rows.append(jnp.zeros((EXTRA - len(rows), width), F32))
        out[2 * tile : 2 * tile + EXTRA, cols] = jnp.concatenate(rows, axis=0).astype(BF16)


def prep(first, count, head_width, q, g, o, lse, flags):
    tile, full = q.shape
    wide = count * head_width
    offset = first * head_width
    cols = pl.BlockSpec((pl.Element(tile), pl.Element(wide)), lambda i: (0, offset))
    return pl.pallas_call(
        functools.partial(prep_kernel, first, count),
        grid=(1,),
        in_specs=[
            cols,
            cols,
            cols,
            pl.BlockSpec(lse.shape, lambda i: (0, 0)),
            pl.BlockSpec(flags.shape, lambda i: (0, 0)),
        ],
        out_specs=pl.BlockSpec((2 * tile + EXTRA, wide), lambda i: (0, 0)),
        out_shape=jax.ShapeDtypeStruct((2 * tile + EXTRA, wide), BF16),
        cost_estimate=pl.CostEstimate(
            flops=2 * tile * wide, bytes_accessed=10 * tile * wide, transcendentals=0
        ),
        name="prep",
    )(q, g, o, lse, flags)


def row_stats(message, tile):
    extra = message[2 * tile : 2 * tile + EXTRA, :].astype(F32)
    parts = tile // 128
    rows = []
    for base in (0, 3 * parts):
        pieces = []
        for p in range(parts):
            a, b, c = (extra[base + i * parts + p : base + i * parts + p + 1] for i in range(3))
            pieces.append(a + b + c)
        rows.append(jnp.concatenate(pieces, axis=1))
    return (rows[0], rows[1], extra[6 * parts : 6 * parts + 1])


def stage_kernel(work, names, carried, factor, far_ref, *refs):
    env = dict(zip(names, refs))
    tile = env["message%d" % work[0][1][0]].shape[0] - EXTRA
    tile //= 2
    used = sorted({j for _, js in work for j in js})
    stats = {j: row_stats(env["message%d" % j], tile) for j in used}
    started = set()

    def add_q(j, term):
        name = "q%d" % j
        if name in started:
            env["sum_" + name][...] += term
        elif "acc_" + name in env:
            env["sum_" + name][...] = env["acc_" + name][...] + term
        else:
            env["sum_" + name][...] = term
        started.add(name)

    def key_frame(slot, js):
        key = env["k%d" % slot][...]
        value = env["v%d" % slot][...]
        name = "acc_kv%d" % slot
        dk, dv = (env[name][0], env[name][1]) if name in env else (None, None)
        for j in js:
            message = env["message%d" % j]
            qj = message[0:tile, :]
            gj = message[tile : 2 * tile, :]
            shift, delta, flags = stats[j]
            lane = 3 * j + slot
            shift = jnp.where(flags[:, lane : lane + 1] > 0, shift, FAR_AWAY)
            scores = dot(key, qj, ((1,), (1,)))
            weights = jnp.exp2(scores * (factor * LOG2E) - shift)
            grad_prob = dot(value, gj, ((1,), (1,)))
            grad_score = (weights * (grad_prob - delta)).astype(BF16)
            term_v = dot(weights.astype(BF16), gj, ((1,), (0,)))
            term_k = dot(grad_score, qj, ((1,), (0,))) * factor
            add_q(j, dot(grad_score, key, ((0,), (0,))))
            dv = term_v if dv is None else dv + term_v
            dk = term_k if dk is None else dk + term_k
        out = env["out_kv%d" % slot]
        out[0] = dk.astype(out.dtype)
        out[1] = dv.astype(out.dtype)

    for slot, js in work:
        if slot != FAR:
            key_frame(slot, js)
    for slot, js in work:
        if slot == FAR:
            pl.when(far_ref[0] > 0)(functools.partial(key_frame, slot, js))

            @pl.when(far_ref[0] == 0)
            def _():
                out = env["out_kv%d" % FAR]
                out[...] = jnp.zeros_like(out)
                for j in js:
                    name = "q%d" % j
                    if name not in carried:
                        continue
                    env["sum_" + name][...] = env["acc_" + name][...]

    for j in used:
        out = env["out_q%d" % j]
        out[...] = (env["sum_q%d" % j][...]).astype(out.dtype)


def run_stage(work, last, first, count, head_width, far, keys, messages, sums):
    rows, wide = next(iter(messages.values())).shape
    tile = (rows - EXTRA) // 2
    one = pl.BlockSpec((tile, head_width), lambda h, *_: (0, h))
    two = pl.BlockSpec((2, tile, head_width), lambda h, *_: (0, 0, h))
    cols = pl.BlockSpec((tile, head_width), lambda h, *_: (0, h + first))
    whole = pl.BlockSpec((rows, head_width), lambda h, *_: (0, h))
    used = sorted({j for _, js in work for j in js})
    slots = [slot for slot, _ in work]
    names, args, specs = ([], [], [])

    def give(name, arg, spec):
        names.append(name)
        args.append(arg)
        specs.append(spec)

    for j in used:
        give("message%d" % j, messages[j], whole)
    for slot in slots:
        give("k%d" % slot, keys[slot][0], cols)
        give("v%d" % slot, keys[slot][1], cols)
    touched = [("q%d" % j, one) for j in used] + [("kv%d" % s, two) for s in slots]
    carried = [name for name, _ in touched if name in sums]
    for name, spec in touched:
        if name in sums:
            give("acc_" + name, sums[name], spec)
    out_specs, out_shapes = ([], [])
    for name, spec in touched:
        names.append("out_" + name)
        out_specs.append(spec)
        shape = (tile, wide) if name.startswith("q") else (2, tile, wide)
        out_shapes.append(jax.ShapeDtypeStruct(shape, BF16 if name in last else F32))
    names += ["sum_q%d" % j for j in used]
    pairs = count * sum(len(js) for _, js in work)
    results = pl.pallas_call(
        functools.partial(stage_kernel, work, names, carried, head_width**-0.5),
        grid_spec=pltpu.PrefetchScalarGridSpec(
            num_scalar_prefetch=1,
            grid=(count,),
            in_specs=specs,
            out_specs=out_specs,
            scratch_shapes=[pltpu.VMEM((tile, head_width), F32)] * len(used),
        ),
        out_shape=out_shapes,
        compiler_params=pltpu.CompilerParams(vmem_limit_bytes=40 * 1024 * 1024),
        cost_estimate=pl.CostEstimate(
            flops=20 * pairs * tile * tile * head_width,
            bytes_accessed=40 * tile * wide,
            transcendentals=pairs * tile * tile,
        ),
        name="pairs",
    )(far, *args)
    return {**sums, **{name: value for (name, _), value in zip(touched, results)}}


def finish_kernel(factor, own_q, back_q, own_kv, near, far, *rest):
    out_q, out_k, out_v = rest[-3:]
    out_q[...] = (own_q[...] * factor + back_q[...].astype(F32)).astype(BF16)
    sums = own_kv[...] + near[...].astype(F32) + far[...].astype(F32)
    out_k[...] = sums[0].astype(BF16)
    out_v[...] = sums[1].astype(BF16)


def finish(first, count, head_width, full, parts, so_far):
    tile = parts[0].shape[0]
    one = pl.BlockSpec((tile, head_width), lambda h: (0, h))
    two = pl.BlockSpec((2, tile, head_width), lambda h: (0, 0, h))
    cols = pl.BlockSpec((tile, head_width), lambda h: (0, h + first))
    kept = [] if so_far is None else list(so_far)
    return pl.pallas_call(
        functools.partial(finish_kernel, head_width**-0.5),
        grid=(count,),
        in_specs=[one, one, two, two, two] + [pl.BlockSpec(memory_space=pl.ANY)] * len(kept),
        out_specs=[cols] * 3,
        out_shape=[jax.ShapeDtypeStruct((tile, full), BF16)] * 3,
        input_output_aliases={5 + i: i for i in range(len(kept))},
        cost_estimate=pl.CostEstimate(
            flops=8 * tile * count * head_width,
            bytes_accessed=30 * tile * count * head_width,
            transcendentals=0,
        ),
        name="finish",
    )(*parts, *kept)


def pair_flags(window_mask, lanes):
    mask = window_mask.reshape(9)
    frames, rows = (lax.axis_size("tm"), lax.axis_size("space"))
    frame, row = (lax.axis_index("tm"), lax.axis_index("space"))
    toward = 1 - 2 * lax.rem(row, 2)
    near = 1 - 2 * lax.rem(frame, 2)
    lane = jnp.arange(9, dtype=jnp.int32)
    row_off = (lane // 3 - 1) * toward
    slot = lane % 3
    frame_off = jnp.where(slot == NEAR, near, jnp.where(slot == FAR, -near, 0))
    inside = (
        (row + row_off >= 0)
        & (row + row_off < rows)
        & (frame + frame_off >= 0)
        & (frame + frame_off < frames)
    )
    index = 3 * (frame_off + 1) + row_off + 1
    picked = jnp.sum(jnp.where(index[:, None] == lane[None, :], mask[None, :], 0), axis=1)
    flags = (inside & ((picked > 0) | (index == 4))).astype(F32)
    return jnp.pad(flags, (0, lanes - 9)).reshape(1, lanes)


def after(value, *earlier):
    return lax.optimization_barrier((value, *earlier))[0]


def per_device(queries, keys, values, outputs, out_grads, log_sums, window_mask):
    tile, full = queries.shape[2:]
    heads = log_sums.shape[2]
    width = full // heads
    frames, rows = (lax.axis_size("tm"), lax.axis_size("space"))
    q, k, v, o, g = (a.reshape(tile, full) for a in (queries, keys, values, outputs, out_grads))
    partner = [(i, i ^ 1) for i in range(rows)]
    onward = [(i, i + 2) for i in range(0, rows - 2, 2)]
    onward += [(i, i - 2) for i in range(3, rows, 2)]
    homeward = [(b, a) for a, b in onward]
    near_pairs = [(i, i ^ 1) for i in range(frames)]
    far_pairs = [(i, i + 1) for i in range(1, frames - 1, 2)]
    far_pairs += [(b, a) for a, b in far_pairs]

    frame = lax.axis_index("tm")
    far_frame = frame - 1 + 2 * lax.rem(frame, 2)
    has_far = ((far_frame >= 0) & (far_frame < frames)).astype(jnp.int32).reshape(1)

    firsts = [sum(CHUNKS[:c]) for c in range(len(CHUNKS))]
    flags = pair_flags(window_mask, width)
    lse = log_sums.reshape(heads, tile)
    near_kv = [lax.ppermute(a, "tm", near_pairs) for a in (k, v)]
    far_kv = [lax.ppermute(a, "tm", far_pairs) for a in (k, v)]
    mine, theirs, outers = ([], [], [])
    for c, count in enumerate(CHUNKS):
        source = q
        if c == 1:
            source = after(q, *near_kv)
        if c >= 2:
            source = after(q, theirs[c - 2])
        mine.append(prep(firsts[c], count, width, source, g, o, lse, flags))
        theirs.append(lax.ppermute(mine[c], "space", partner))
        outers.append(lax.ppermute(theirs[c], "space", onward))
    frames_kv = {HERE: (k, v), NEAR: near_kv, FAR: far_kv}

    out = None
    for c, count in enumerate(CHUNKS):
        messages = {OUTER: outers[c], OWN: mine[c], PARTNER: theirs[c]}
        sums = {}
        for step, work in enumerate(STAGES):
            last = ("q0", "kv1", "kv2") if step + 1 == len(STAGES) else ()
            needed = {j: messages[j] for _, js in work for j in js}
            sums = run_stage(
                work, last, firsts[c], count, width, has_far, frames_kv, needed, sums
            )
        home = lax.ppermute(sums["q0"], "space", homeward)
        total = (sums["q2"] + home.astype(F32)) * (width**-0.5)
        dq_back = lax.ppermute(total.astype(BF16), "space", partner)
        near_back = lax.ppermute(sums["kv1"], "tm", near_pairs)
        far_back = lax.ppermute(sums["kv2"], "tm", far_pairs)
        out = finish(
            firsts[c], count, width, full,
            (sums["q1"], dq_back, sums["kv0"], near_back, far_back), out,
        )
    return tuple(a.reshape(queries.shape) for a in out)


def solution(mesh):
    tile = P("tm", "space", None, None)
    return jax.shard_map(
        per_device,
        mesh=mesh,
        in_specs=(tile,) * 6 + (P("tm", "space", None),),
        out_specs=(tile,) * 3,
        check_vma=False,
    )
```

```python
import functools
import math

import jax
import jax.numpy as jnp
from jax import lax
from jax.experimental import pallas as pl
from jax.experimental.pallas import tpu as pltpu
from jax.sharding import PartitionSpec as P

F32 = jnp.float32
BF16 = jnp.bfloat16
LOG2E = math.log2(math.e)
FAR_AWAY = 1e30

EVEN_ROW, ODD_ROW, OUTER = (0, 1, 2)
EVEN, ODD, FAR = (0, 1, 2)
BOTH = (EVEN_ROW, ODD_ROW)
CHUNKS = (2, 3, 4, 3)
STAGES = (
    ((EVEN, BOTH), (ODD, BOTH)),
    ((EVEN, (OUTER,)), (ODD, (OUTER,)), (FAR, (EVEN_ROW, ODD_ROW, OUTER))),
)
EXTRA = 32
VMEM_LIMIT = 16 * 1024 * 1024


def dot(a, b, dims):
    return lax.dot_general(a, b, (dims, ((), ())), preferred_element_type=F32)


def three_terms(row):
    terms = []
    for _ in range(3):
        term = row.astype(BF16).astype(F32)
        terms.append(term)
        row = row - term
    return terms


def fold(row):
    lanes = 128
    return [row[:, i : i + lanes] for i in range(0, row.shape[1], lanes)]


def prep_kernel(first, count, q_ref, g_ref, o_ref, lse_ref, flag_ref, out):
    tile = q_ref.shape[0]
    width = q_ref.shape[1] // count
    out[0:tile, :] = q_ref[...]
    out[tile : 2 * tile, :] = g_ref[...]
    ones = jnp.ones((8, width), BF16)
    for h in range(count):
        cols = slice(h * width, (h + 1) * width)
        prod = g_ref[:, cols].astype(F32) * o_ref[:, cols].astype(F32)
        high = prod.astype(BF16)
        low = (prod - high.astype(F32)).astype(BF16)
        delta = dot(ones, high, ((1,), (1,))) + dot(ones, low, ((1,), (1,)))
        rows = []
        for row in (lse_ref[first + h : first + h + 1, :] * LOG2E, delta[0:1, :]):
            for term in three_terms(row):
                rows += fold(term)
        rows.append(flag_ref[...])
        rows.append(jnp.zeros((EXTRA - len(rows), width), F32))
        out[2 * tile : 2 * tile + EXTRA, cols] = jnp.concatenate(rows, axis=0).astype(BF16)


def prep(first, count, head_width, q, g, o, lse, flags):
    tile, full = q.shape
    wide = count * head_width
    offset = first * head_width
    cols = pl.BlockSpec((pl.Element(tile), pl.Element(wide)), lambda i: (0, offset))
    return pl.pallas_call(
        functools.partial(prep_kernel, first, count),
        grid=(1,),
        in_specs=[
            cols,
            cols,
            cols,
            pl.BlockSpec(lse.shape, lambda i: (0, 0)),
            pl.BlockSpec(flags.shape, lambda i: (0, 0)),
        ],
        out_specs=pl.BlockSpec((2 * tile + EXTRA, wide), lambda i: (0, 0)),
        out_shape=jax.ShapeDtypeStruct((2 * tile + EXTRA, wide), BF16),
        cost_estimate=pl.CostEstimate(
            flops=2 * tile * wide, bytes_accessed=10 * tile * wide, transcendentals=0
        ),
        name="prep",
    )(q, g, o, lse, flags)


def row_stats(message, parity):
    tile = (message.shape[0] - EXTRA) // 2
    extra = message[2 * tile : 2 * tile + EXTRA, :].astype(F32)
    parts = tile // 128
    rows = []
    for base in (0, 3 * parts):
        pieces = []
        for p in range(parts):
            a, b, c = (extra[base + i * parts + p : base + i * parts + p + 1] for i in range(3))
            pieces.append(a + b + c)
        rows.append(jnp.concatenate(pieces, axis=1))
    flags = extra[6 * parts : 6 * parts + 1]
    lanes = [flags[:, i : i + 1] for i in range(9)]
    if parity is None:
        chosen = lanes[6:9]
    else:
        chosen = [jnp.where(parity == 0, lanes[i], lanes[3 + i]) for i in range(3)]
    return (rows[0], rows[1], chosen)


def stage_kernel(work, names, factor, place_ref, *refs):
    env = dict(zip(names, refs))
    has_far, parity = (place_ref[0], place_ref[1])
    used = sorted({j for _, js in work for j in js})
    messages = {j: env["outer"] if j == OUTER else env["pair"].at[j] for j in used}
    stats = {j: row_stats(messages[j], None if j == OUTER else parity) for j in used}
    tile = (messages[used[0]].shape[0] - EXTRA) // 2
    sums = {j: env["sum%d" % j] for j in used}
    started = set()

    def before(j):
        if j == OUTER or "acc_pair" not in env:
            return None
        return env["acc_pair"][j]

    def add_q(j, term):
        if j in started:
            sums[j][...] += term
        else:
            earlier = before(j)
            sums[j][...] = term if earlier is None else earlier + term
        started.add(j)

    def key_frame(slot, js):
        key, value = (
            (env["far_k"][...], env["far_v"][...])
            if slot == FAR
            else (env["k"][slot], env["v"][slot])
        )
        dk, dv = (None, None)
        if slot != FAR and "acc_keys" in env:
            dk, dv = (env["acc_keys"][slot, 0], env["acc_keys"][slot, 1])
        for j in js:
            qj = messages[j][0:tile, :]
            gj = messages[j][tile : 2 * tile, :]
            shift, delta, flags = stats[j]
            shift = jnp.where(flags[slot] > 0, shift, FAR_AWAY)
            scores = dot(key, qj, ((1,), (1,)))
            weights = jnp.exp2(scores * (factor * LOG2E) - shift)
            grad_prob = dot(value, gj, ((1,), (1,)))
            grad_score = (weights * (grad_prob - delta)).astype(BF16)
            term_v = dot(weights.astype(BF16), gj, ((1,), (0,)))
            term_k = dot(grad_score, qj, ((1,), (0,))) * factor
            add_q(j, dot(grad_score, key, ((0,), (0,))) * factor)
            dv = term_v if dv is None else dv + term_v
            dk = term_k if dk is None else dk + term_k
        out = env["out_far"] if slot == FAR else env["out_keys"].at[slot]
        out[0] = dk.astype(out.dtype)
        out[1] = dv.astype(out.dtype)

    for slot, js in work:
        if slot != FAR:
            key_frame(slot, js)
    for slot, js in work:
        if slot == FAR:
            fresh = [j for j in js if j not in started]
            pl.when(has_far > 0)(functools.partial(key_frame, slot, js))

            @pl.when(has_far == 0)
            def _():
                out = env["out_far"]
                out[...] = jnp.zeros_like(out)
                for j in fresh:
                    earlier = before(j)
                    sums[j][...] = jnp.zeros_like(sums[j]) if earlier is None else earlier

    for j in used:
        out = env["out_outer"] if j == OUTER else env["out_pair"].at[j]
        out[...] = sums[j][...].astype(out.dtype)


def run_stage(work, final, first, count, head_width, place, operands, sums):
    rows, wide = operands["pair"].shape[1:]
    tile = (rows - EXTRA) // 2
    used = sorted({j for _, js in work for j in js})
    slots = [slot for slot, _ in work]
    specs = {
        "pair": pl.BlockSpec((2, rows, head_width), lambda h, *_: (0, 0, h)),
        "outer": pl.BlockSpec((rows, head_width), lambda h, *_: (0, h)),
        "k": pl.BlockSpec((2, tile, head_width), lambda h, *_: (0, 0, h + first)),
        "far_k": pl.BlockSpec((tile, head_width), lambda h, *_: (0, h + first)),
    }
    specs.update(v=specs["k"], far_v=specs["far_k"])
    sum_specs = {
        "pair": pl.BlockSpec((2, tile, head_width), lambda h, *_: (0, 0, h)),
        "outer": pl.BlockSpec((tile, head_width), lambda h, *_: (0, h)),
        "keys": pl.BlockSpec((2, 2, tile, head_width), lambda h, *_: (0, 0, 0, h)),
        "far": pl.BlockSpec((2, tile, head_width), lambda h, *_: (0, 0, h)),
    }
    shapes = {
        "pair": (2, tile, wide),
        "outer": (tile, wide),
        "keys": (2, 2, tile, wide),
        "far": (2, tile, wide),
    }
    names = []
    if set(used) & set(BOTH):
        names.append("pair")
    if OUTER in used:
        names.append("outer")
    if EVEN in slots or ODD in slots:
        names += ["k", "v"]
    if FAR in slots:
        names += ["far_k", "far_v"]
    args = [operands[name] for name in names]
    in_specs = [specs[name] for name in names]
    touched = [name for name in ("pair", "outer") if name in names]
    touched += ["keys"] if "k" in names else []
    touched += ["far"] if "far_k" in names else []
    for name in touched:
        if name in sums:
            names.append("acc_" + name)
            args.append(sums[name])
            in_specs.append(sum_specs[name])
    names += ["out_" + name for name in touched]
    names += ["sum%d" % j for j in used]
    pairs = count * sum(len(js) for _, js in work)
    results = pl.pallas_call(
        functools.partial(stage_kernel, work, names, head_width**-0.5),
        grid_spec=pltpu.PrefetchScalarGridSpec(
            num_scalar_prefetch=1,
            grid=(count,),
            in_specs=in_specs,
            out_specs=[sum_specs[name] for name in touched],
            scratch_shapes=[pltpu.VMEM((tile, head_width), F32)] * len(used),
        ),
        out_shape=[
            jax.ShapeDtypeStruct(shapes[name], BF16 if name in final else F32)
            for name in touched
        ],
        compiler_params=pltpu.CompilerParams(vmem_limit_bytes=VMEM_LIMIT),
        cost_estimate=pl.CostEstimate(
            flops=20 * pairs * tile * tile * head_width,
            bytes_accessed=40 * tile * wide,
            transcendentals=pairs * tile * tile,
        ),
        name="pairs",
    )(place, *args)
    return {**sums, **dict(zip(touched, results))}


def finish_kernel(q, keys, far, *rest):
    out_q, out_k, out_v = rest[-3:]
    out_q[...] = q[...]
    sums = keys[...].astype(F32) + far[...].astype(F32)
    out_k[...] = sums[0].astype(BF16)
    out_v[...] = sums[1].astype(BF16)


def finish(first, count, head_width, full, parts, so_far):
    tile = parts[0].shape[0]
    one = pl.BlockSpec((tile, head_width), lambda h: (0, h))
    two = pl.BlockSpec((2, tile, head_width), lambda h: (0, 0, h))
    cols = pl.BlockSpec((tile, head_width), lambda h: (0, h + first))
    kept = [] if so_far is None else list(so_far)
    return pl.pallas_call(
        finish_kernel,
        grid=(count,),
        in_specs=[one, two, two] + [pl.BlockSpec(memory_space=pl.ANY)] * len(kept),
        out_specs=[cols] * 3,
        out_shape=[jax.ShapeDtypeStruct((tile, full), BF16)] * 3,
        input_output_aliases={3 + i: i for i in range(len(kept))},
        cost_estimate=pl.CostEstimate(
            flops=4 * tile * count * head_width,
            bytes_accessed=16 * tile * count * head_width,
            transcendentals=0,
        ),
        name="finish",
    )(*parts, *kept)


def pair_flags(window_mask, lanes):
    mask = window_mask.reshape(9)
    frames, rows = (lax.axis_size("tm"), lax.axis_size("space"))
    frame, row = (lax.axis_index("tm"), lax.axis_index("space"))
    row_odd, frame_odd = (lax.rem(row, 2), lax.rem(frame, 2))
    lane = jnp.arange(9, dtype=jnp.int32)
    role, slot = (lane // 3, lane % 3)
    row_off = jnp.where(role == OUTER, 2 * row_odd - 1, role - row_odd)
    frame_off = jnp.where(slot == FAR, 2 * frame_odd - 1, slot - frame_odd)
    inside = (
        (row + row_off >= 0)
        & (row + row_off < rows)
        & (frame + frame_off >= 0)
        & (frame + frame_off < frames)
    )
    index = 3 * (frame_off + 1) + row_off + 1
    picked = jnp.sum(jnp.where(index[:, None] == lane[None, :], mask[None, :], 0), axis=1)
    flags = (inside & ((picked > 0) | (index == 4))).astype(F32)
    return jnp.pad(flags, (0, lanes - 9)).reshape(1, lanes)


def after(value, *earlier):
    return lax.optimization_barrier((value, *earlier))[0]


def per_device(queries, keys, values, outputs, out_grads, log_sums, window_mask):
    tile, full = queries.shape[2:]
    heads = log_sums.shape[2]
    width = full // heads
    frames, rows = (lax.axis_size("tm"), lax.axis_size("space"))
    q, k, v, o, g = (a.reshape(tile, full) for a in (queries, keys, values, outputs, out_grads))
    row_pairs = [[i, i + 1] for i in range(0, rows, 2)]
    frame_pairs = [[i, i + 1] for i in range(0, frames, 2)]
    onward = [(i, i + 2) for i in range(0, rows - 2, 2)]
    onward += [(i, i - 2) for i in range(3, rows, 2)]
    homeward = [(b, a) for a, b in onward]
    far_pairs = [(i, i + 1) for i in range(1, frames - 1, 2)]
    far_pairs += [(b, a) for a, b in far_pairs]

    frame, row = (lax.axis_index("tm"), lax.axis_index("space"))
    far_frame = frame - 1 + 2 * lax.rem(frame, 2)
    has_far = ((far_frame >= 0) & (far_frame < frames)).astype(jnp.int32)
    parity = lax.rem(row, 2)
    place = jnp.stack([has_far, parity])

    firsts = [sum(CHUNKS[:c]) for c in range(len(CHUNKS))]
    flags = pair_flags(window_mask, width)
    lse = log_sums.reshape(heads, tile)
    pair_k, pair_v = (
        lax.all_gather(a, "tm", axis_index_groups=frame_pairs) for a in (k, v)
    )
    far_k, far_v = (lax.ppermute(a, "tm", far_pairs) for a in (k, v))
    pairs, outers = ([], [])
    for c, count in enumerate(CHUNKS):
        source = q
        if c >= 2:
            source = after(q, pairs[c - 2])
        message = prep(firsts[c], count, width, source, g, o, lse, flags)
        pairs.append(lax.all_gather(message, "space", axis_index_groups=row_pairs))
        theirs = lax.dynamic_index_in_dim(pairs[c], 1 - parity, 0, False)
        outers.append(lax.ppermute(theirs, "space", onward))

    out = None
    for c, count in enumerate(CHUNKS):
        operands = {
            "pair": pairs[c],
            "outer": outers[c],
            "k": pair_k,
            "v": pair_v,
            "far_k": far_k,
            "far_v": far_v,
        }
        sums = {}
        for step, work in enumerate(STAGES):
            final = ("outer", "keys", "far") if step + 1 == len(STAGES) else ()
            sums = run_stage(work, final, firsts[c], count, width, place, operands, sums)
        home = lax.ppermute(sums["outer"], "space", homeward)
        theirs = jnp.arange(2).reshape(2, 1, 1) == 1 - parity
        total = sums["pair"] + jnp.where(theirs, home.astype(F32)[None], 0.0)
        back_q = lax.psum_scatter(
            total.astype(BF16), "space", axis_index_groups=row_pairs
        )
        back_keys = lax.psum_scatter(sums["keys"], "tm", axis_index_groups=frame_pairs)
        back_far = lax.ppermute(sums["far"], "tm", far_pairs)
        out = finish(firsts[c], count, width, full, (back_q, back_keys, back_far), out)
    return tuple(a.reshape(queries.shape) for a in out)


def solution(mesh):
    tile = P("tm", "space", None, None)
    return jax.shard_map(
        per_device,
        mesh=mesh,
        in_specs=(tile,) * 6 + (P("tm", "space", None),),
        out_specs=(tile,) * 3,
        check_vma=False,
    )
```

```python
import functools
import math

import jax
import jax.numpy as jnp
from jax import lax
from jax.experimental import pallas as pl
from jax.experimental.pallas import tpu as pltpu
from jax.sharding import PartitionSpec as P

F32 = jnp.float32
BF16 = jnp.bfloat16
LOG2E = math.log2(math.e)
FAR_AWAY = 1e30

OUTER, OWN, PARTNER = (0, 1, 2)
HERE, NEAR, FAR = (0, 1, 2)
CHUNKS = (4, 5, 3)
STAGES = (
    ((HERE, (OWN,)), (NEAR, (OWN,))),
    ((HERE, (PARTNER,)), (NEAR, (PARTNER,))),
    ((HERE, (OUTER,)), (NEAR, (OUTER,)), (FAR, (OWN, PARTNER, OUTER))),
)
EXTRA = 32
VMEM_LIMIT = 16 * 1024 * 1024


def dot(a, b, dims):
    return lax.dot_general(a, b, (dims, ((), ())), preferred_element_type=F32)


def three_terms(row):
    terms = []
    for _ in range(3):
        term = row.astype(BF16).astype(F32)
        terms.append(term)
        row = row - term
    return terms


def fold(row):
    lanes = 128
    return [row[:, i : i + lanes] for i in range(0, row.shape[1], lanes)]


def flag_row(frames, rows, frame, row, mask_ref, lanes):
    toward = 1 - 2 * lax.rem(row, 2)
    near = 1 - 2 * lax.rem(frame, 2)
    lane = lax.broadcasted_iota(jnp.int32, (1, lanes), 1)
    flags = jnp.zeros((1, lanes), F32)
    for role in (OUTER, OWN, PARTNER):
        for slot in (HERE, NEAR, FAR):
            row_off = (role - 1) * toward
            frame_off = (0, near, -near)[slot]
            inside = (
                (row + row_off >= 0)
                & (row + row_off < rows)
                & (frame + frame_off >= 0)
                & (frame + frame_off < frames)
            )
            index = 3 * (frame_off + 1) + row_off + 1
            on = inside & ((mask_ref[index] > 0) | (index == 4))
            flags = jnp.where(lane == 3 * role + slot, on.astype(F32), flags)
    return flags


def prep_kernel(
    counts, frames, rows, frame_ref, row_ref, mask_ref, q_ref, g_ref, o_ref, lse_ref, *outs
):
    tile = q_ref.shape[0]
    width = q_ref.shape[1] // sum(counts)
    flags = flag_row(frames, rows, frame_ref[0], row_ref[0], mask_ref, width)
    ones = jnp.ones((8, width), BF16)
    head = 0
    for out, count in zip(outs, counts):
        for h in range(count):
            source = slice(head * width, (head + 1) * width)
            cols = slice(h * width, (h + 1) * width)
            grad = g_ref[:, source]
            out[0:tile, cols] = q_ref[:, source]
            out[tile : 2 * tile, cols] = grad
            prod = grad.astype(F32) * o_ref[:, source].astype(F32)
            high = prod.astype(BF16)
            low = (prod - high.astype(F32)).astype(BF16)
            delta = dot(ones, high, ((1,), (1,))) + dot(ones, low, ((1,), (1,)))
            lines = []
            for line in (lse_ref[head] * LOG2E, delta[0:1, :]):
                for term in three_terms(line):
                    lines += fold(term)
            lines.append(flags)
            lines.append(jnp.zeros((EXTRA - len(lines), width), F32))
            extra = jnp.concatenate(lines, axis=0).astype(BF16)
            out[2 * tile : 2 * tile + EXTRA, cols] = extra
            head += 1


def prep(first, counts, head_width, sizes, place, mask, q, g, o, lse):
    tile, full = q.shape
    count = sum(counts)
    offset = first * head_width
    cols = pl.BlockSpec(
        (pl.Element(tile), pl.Element(count * head_width)), lambda i, *_: (0, offset)
    )
    shapes = [(2 * tile + EXTRA, n * head_width) for n in counts]
    return pl.pallas_call(
        functools.partial(prep_kernel, counts, *sizes),
        grid_spec=pltpu.PrefetchScalarGridSpec(
            num_scalar_prefetch=3,
            grid=(1,),
            in_specs=[
                cols,
                cols,
                cols,
                pl.BlockSpec(
                    (pl.Element(count), pl.Element(1), pl.Element(tile)),
                    lambda i, *_: (first, 0, 0),
                ),
            ],
            out_specs=[pl.BlockSpec(shape, lambda i, *_: (0, 0)) for shape in shapes],
        ),
        out_shape=[jax.ShapeDtypeStruct(shape, BF16) for shape in shapes],
        compiler_params=pltpu.CompilerParams(vmem_limit_bytes=VMEM_LIMIT),
        cost_estimate=pl.CostEstimate(
            flops=2 * tile * count * head_width,
            bytes_accessed=10 * tile * count * head_width,
            transcendentals=0,
        ),
        name="prep",
    )(*place, mask, q, g, o, lse)


def row_stats(message, tile):
    extra = message[2 * tile : 2 * tile + EXTRA, :].astype(F32)
    parts = tile // 128
    rows = []
    for base in (0, 3 * parts):
        pieces = []
        for p in range(parts):
            a, b, c = (extra[base + i * parts + p : base + i * parts + p + 1] for i in range(3))
            pieces.append(a + b + c)
        rows.append(jnp.concatenate(pieces, axis=1))
    return (rows[0], rows[1], extra[6 * parts : 6 * parts + 1])


def stage_kernel(work, names, carried, factor, far_ref, *refs):
    env = dict(zip(names, refs))
    tile = env["message%d" % work[0][1][0]].shape[0] - EXTRA
    tile //= 2
    used = sorted({j for _, js in work for j in js})
    stats = {j: row_stats(env["message%d" % j], tile) for j in used}
    started = set()

    def add_q(j, term):
        name = "q%d" % j
        if name in started:
            env["sum_" + name][...] += term
        elif "acc_" + name in env:
            env["sum_" + name][...] = env["acc_" + name][...] + term
        else:
            env["sum_" + name][...] = term
        started.add(name)

    def key_frame(slot, js):
        key = env["k%d" % slot][...]
        value = env["v%d" % slot][...]
        name = "acc_kv%d" % slot
        dk, dv = (env[name][0], env[name][1]) if name in env else (None, None)
        for j in js:
            message = env["message%d" % j]
            qj = message[0:tile, :]
            gj = message[tile : 2 * tile, :]
            shift, delta, flags = stats[j]
            lane = 3 * j + slot
            shift = jnp.where(flags[:, lane : lane + 1] > 0, shift, FAR_AWAY)
            scores = dot(key, qj, ((1,), (1,)))
            weights = jnp.exp2(scores * (factor * LOG2E) - shift)
            grad_prob = dot(value, gj, ((1,), (1,)))
            grad_score = (weights * (grad_prob - delta)).astype(BF16)
            term_v = dot(weights.astype(BF16), gj, ((1,), (0,)))
            term_k = dot(grad_score, qj, ((1,), (0,))) * factor
            add_q(j, dot(grad_score, key, ((0,), (0,))))
            dv = term_v if dv is None else dv + term_v
            dk = term_k if dk is None else dk + term_k
        out = env["out_kv%d" % slot]
        out[0] = dk.astype(out.dtype)
        out[1] = dv.astype(out.dtype)

    for slot, js in work:
        if slot != FAR:
            key_frame(slot, js)
    for slot, js in work:
        if slot == FAR:
            pl.when(far_ref[0] > 0)(functools.partial(key_frame, slot, js))

            @pl.when(far_ref[0] == 0)
            def _():
                out = env["out_kv%d" % FAR]
                out[...] = jnp.zeros_like(out)
                for j in js:
                    name = "q%d" % j
                    if name not in carried:
                        continue
                    env["sum_" + name][...] = env["acc_" + name][...]

    for j in used:
        out = env["out_q%d" % j]
        out[...] = (env["sum_q%d" % j][...]).astype(out.dtype)


def run_stage(work, last, first, count, head_width, far, keys, messages, sums):
    rows, wide = next(iter(messages.values())).shape
    tile = (rows - EXTRA) // 2
    one = pl.BlockSpec((tile, head_width), lambda h, *_: (0, h))
    two = pl.BlockSpec((2, tile, head_width), lambda h, *_: (0, 0, h))
    cols = pl.BlockSpec((tile, head_width), lambda h, *_: (0, h + first))
    whole = pl.BlockSpec((rows, head_width), lambda h, *_: (0, h))
    used = sorted({j for _, js in work for j in js})
    slots = [slot for slot, _ in work]
    names, args, specs = ([], [], [])

    def give(name, arg, spec):
        names.append(name)
        args.append(arg)
        specs.append(spec)

    for j in used:
        give("message%d" % j, messages[j], whole)
    for slot in slots:
        give("k%d" % slot, keys[slot][0], cols)
        give("v%d" % slot, keys[slot][1], cols)
    touched = [("q%d" % j, one) for j in used] + [("kv%d" % s, two) for s in slots]
    carried = [name for name, _ in touched if name in sums]
    for name, spec in touched:
        if name in sums:
            give("acc_" + name, sums[name], spec)
    out_specs, out_shapes = ([], [])
    for name, spec in touched:
        names.append("out_" + name)
        out_specs.append(spec)
        shape = (tile, wide) if name.startswith("q") else (2, tile, wide)
        out_shapes.append(jax.ShapeDtypeStruct(shape, BF16 if name in last else F32))
    names += ["sum_q%d" % j for j in used]
    pairs = count * sum(len(js) for _, js in work)
    results = pl.pallas_call(
        functools.partial(stage_kernel, work, names, carried, head_width**-0.5),
        grid_spec=pltpu.PrefetchScalarGridSpec(
            num_scalar_prefetch=1,
            grid=(count,),
            in_specs=specs,
            out_specs=out_specs,
            scratch_shapes=[pltpu.VMEM((tile, head_width), F32)] * len(used),
        ),
        out_shape=out_shapes,
        compiler_params=pltpu.CompilerParams(vmem_limit_bytes=VMEM_LIMIT),
        cost_estimate=pl.CostEstimate(
            flops=20 * pairs * tile * tile * head_width,
            bytes_accessed=40 * tile * wide,
            transcendentals=pairs * tile * tile,
        ),
        name="pairs",
    )(far, *args)
    return {**sums, **{name: value for (name, _), value in zip(touched, results)}}


def finish_kernel(factor, own_q, back_q, own_kv, near, far, *rest):
    out_q, out_k, out_v = rest[-3:]
    out_q[...] = (own_q[...] * factor + back_q[...].astype(F32)).astype(BF16)
    sums = own_kv[...] + near[...].astype(F32) + far[...].astype(F32)
    out_k[...] = sums[0].astype(BF16)
    out_v[...] = sums[1].astype(BF16)


def finish(first, count, head_width, full, parts, so_far):
    tile = parts[0].shape[0]
    wide = count * head_width
    one = pl.BlockSpec((tile, wide), lambda i: (0, 0))
    two = pl.BlockSpec((2, tile, wide), lambda i: (0, 0, 0))
    cols = pl.BlockSpec(
        (pl.Element(tile), pl.Element(wide)), lambda i: (0, first * head_width)
    )
    kept = [] if so_far is None else list(so_far)
    return pl.pallas_call(
        functools.partial(finish_kernel, head_width**-0.5),
        grid=(1,),
        in_specs=[one, one, two, two, two] + [pl.BlockSpec(memory_space=pl.ANY)] * len(kept),
        out_specs=[cols] * 3,
        out_shape=[jax.ShapeDtypeStruct((tile, full), BF16)] * 3,
        input_output_aliases={5 + i: i for i in range(len(kept))},
        compiler_params=pltpu.CompilerParams(vmem_limit_bytes=VMEM_LIMIT),
        cost_estimate=pl.CostEstimate(
            flops=8 * tile * count * head_width,
            bytes_accessed=30 * tile * count * head_width,
            transcendentals=0,
        ),
        name="finish",
    )(*parts, *kept)


def after(value, *earlier):
    return lax.optimization_barrier((value, *earlier))[0]


def per_device(queries, keys, values, outputs, out_grads, log_sums, window_mask):
    tile, full = queries.shape[2:]
    heads = log_sums.shape[2]
    width = full // heads
    frames, rows = (lax.axis_size("tm"), lax.axis_size("space"))
    q, k, v, o, g = (a.reshape(tile, full) for a in (queries, keys, values, outputs, out_grads))
    partner = [(i, i ^ 1) for i in range(rows)]
    onward = [(i, (i + 2) % rows) for i in range(0, rows, 2)]
    onward += [(i, (i - 2) % rows) for i in range(1, rows, 2)]
    homeward = [(b, a) for a, b in onward]
    near_pairs = [(i, i ^ 1) for i in range(frames)]
    far_pairs = [(0, 0), (frames - 1, frames - 1)]
    for i in range(1, frames - 1, 2):
        far_pairs += [(i, i + 1), (i + 1, i)]

    frame, row = (lax.axis_index("tm"), lax.axis_index("space"))
    far_frame = frame - 1 + 2 * lax.rem(frame, 2)
    has_far = ((far_frame >= 0) & (far_frame < frames)).astype(jnp.int32).reshape(1)
    place = (frame.reshape(1), row.reshape(1))

    firsts = [sum(CHUNKS[:c]) for c in range(len(CHUNKS))]
    lse = log_sums.reshape(heads, 1, tile)
    mask = window_mask.reshape(9)
    near_kv = [lax.ppermute(a, "tm", near_pairs) for a in (k, v)]
    make = lambda first, counts, source: prep(
        first, counts, width, (frames, rows), place, mask, source, g, o, lse
    )
    mine = make(0, CHUNKS[:1], q)
    theirs = {0: lax.ppermute(mine[0], "space", partner)}
    mine += make(firsts[1], CHUNKS[1:], after(q, mine[0]))
    far_kv = [lax.ppermute(after(a, mine[1]), "tm", far_pairs) for a in (k, v)]
    frames_kv = {HERE: (k, v), NEAR: near_kv, FAR: far_kv}
    outers = {}
    sums = [{} for _ in CHUNKS]
    backs = {}
    done = []
    out = None

    def stage(c, step):
        messages = {OUTER: outers.get(c), OWN: mine[c], PARTNER: theirs.get(c)}
        work = STAGES[step]
        needed = {j: messages[j] for _, js in work for j in js}
        first_used = min(needed)
        needed[first_used] = after(needed[first_used], *done[-1:])
        last = ("q0", "kv1", "kv2") if step + 1 == len(STAGES) else ()
        sums[c] = run_stage(
            work, last, firsts[c], CHUNKS[c], width, has_far, frames_kv, needed, sums[c]
        )
        done.append(sums[c]["kv0"])

    def hand_on(c):
        outers[c] = lax.ppermute(after(theirs[c], *done[-1:]), "space", onward)

    def send_home(c):
        backs[c] = [
            lax.ppermute(sums[c]["q0"], "space", homeward),
            lax.ppermute(sums[c]["kv1"], "tm", near_pairs),
            lax.ppermute(sums[c]["kv2"], "tm", far_pairs),
        ]

    def send_back(c):
        home = after(backs[c][0], *done[-1:])
        total = (sums[c]["q2"] + home.astype(F32)) * (width**-0.5)
        backs[c][0] = lax.ppermute(total.astype(BF16), "space", partner)

    def complete(c, so_far):
        back_q, back_near, back_far = backs[c]
        back_q = after(back_q, *done[-1:])
        return finish(
            firsts[c], CHUNKS[c], width, full,
            (sums[c]["q1"], back_q, sums[c]["kv0"], back_near, back_far), so_far,
        )

    last = len(CHUNKS) - 1
    theirs[1] = lax.ppermute(mine[1], "space", partner)
    stage(0, 0)
    stage(1, 0)
    for c in range(2, len(CHUNKS)):
        theirs[c] = lax.ppermute(after(mine[c], theirs[c - 2]), "space", partner)
    hand_on(0)
    for c in range(2, len(CHUNKS)):
        stage(c, 0)
    stage(0, 1)
    for c in range(len(CHUNKS)):
        if c < last:
            hand_on(c + 1)
        stage(c, 2)
        send_home(c)
        if c < last:
            stage(c + 1, 1)
            send_back(c)
        if c >= 2:
            out = complete(c - 2, out)
    send_back(last)
    if last >= 1:
        out = complete(last - 1, out)
    out = complete(last, out)
    return tuple(a.reshape(queries.shape) for a in out)


def solution(mesh):
    tile = P("tm", "space", None, None)
    return jax.shard_map(
        per_device,
        mesh=mesh,
        in_specs=(tile,) * 6 + (P("tm", "space", None),),
        out_specs=(tile,) * 3,
        check_vma=False,
    )
```

```python
import functools
import math

import jax
import jax.numpy as jnp
from jax import lax
from jax.experimental import pallas as pl
from jax.experimental.pallas import tpu as pltpu
from jax.sharding import PartitionSpec as P

F32 = jnp.float32
BF16 = jnp.bfloat16
LOG2E = math.log2(math.e)
FAR_AWAY = 1e30

OUTER, OWN, PARTNER = (0, 1, 2)
HERE, NEAR, FAR = (0, 1, 2)
CHUNKS = (4, 5, 3)
STAGES = (
    ((HERE, (OWN,)), (NEAR, (OWN,))),
    ((HERE, (PARTNER,)), (NEAR, (PARTNER,))),
    ((HERE, (OUTER,)), (NEAR, (OUTER,)), (FAR, (OWN, PARTNER, OUTER))),
)
LATER_STAGES = (
    STAGES[0],
    STAGES[1] + ((FAR, (PARTNER,)),),
    ((HERE, (OUTER,)), (NEAR, (OUTER,)), (FAR, (OWN, OUTER))),
)
ORDER = (('stage', 0, 0), ('stage', 1, 0), ('hand', 0), ('stage', 2, 0), ('stage', 0, 1), ('hand', 1), ('stage', 1, 1), ('stage', 0, 2), ('hand', 2), ('stage', 2, 1), ('stage', 1, 2, (0, 'q0')), ('stage', 2, 2, (0, 'q2'), (0, 'kv1')), ('finish', 0), ('finish', 1), ('finish', 2))
JOINED = ()
WEIGHTS = ((40, 40, 20), (20, 10, 20), (20, 40, 40))
EXTRA = 32
VMEM_LIMIT = 16 * 1024 * 1024


def dot(a, b, dims):
    return lax.dot_general(a, b, (dims, ((), ())), preferred_element_type=F32)


def three_terms(row):
    terms = []
    for _ in range(3):
        term = row.astype(BF16).astype(F32)
        terms.append(term)
        row = row - term
    return terms


def fold(row):
    lanes = 128
    return [row[:, i : i + lanes] for i in range(0, row.shape[1], lanes)]


def flag_row(frames, rows, frame, row, mask_ref, lanes):
    toward = 1 - 2 * lax.rem(row, 2)
    near = 1 - 2 * lax.rem(frame, 2)
    lane = lax.broadcasted_iota(jnp.int32, (1, lanes), 1)
    flags = jnp.zeros((1, lanes), F32)
    for role in (OUTER, OWN, PARTNER):
        for slot in (HERE, NEAR, FAR):
            row_off = (role - 1) * toward
            frame_off = (0, near, -near)[slot]
            inside = (
                (row + row_off >= 0)
                & (row + row_off < rows)
                & (frame + frame_off >= 0)
                & (frame + frame_off < frames)
            )
            index = 3 * (frame_off + 1) + row_off + 1
            on = inside & ((mask_ref[index] > 0) | (index == 4))
            flags = jnp.where(lane == 3 * role + slot, on.astype(F32), flags)
    return flags


def prep_kernel(
    counts, frames, rows, frame_ref, row_ref, mask_ref, q_ref, g_ref, o_ref, lse_ref, *outs
):
    tile = q_ref.shape[0]
    width = q_ref.shape[1] // sum(counts)
    flags = flag_row(frames, rows, frame_ref[0], row_ref[0], mask_ref, width)
    ones = jnp.ones((8, width), BF16)
    head = 0
    for out, count in zip(outs, counts):
        for h in range(count):
            source = slice(head * width, (head + 1) * width)
            cols = slice(h * width, (h + 1) * width)
            grad = g_ref[:, source]
            out[0:tile, cols] = q_ref[:, source]
            out[tile : 2 * tile, cols] = grad
            prod = grad.astype(F32) * o_ref[:, source].astype(F32)
            high = prod.astype(BF16)
            low = (prod - high.astype(F32)).astype(BF16)
            delta = dot(ones, high, ((1,), (1,))) + dot(ones, low, ((1,), (1,)))
            lines = []
            for line in (lse_ref[head] * LOG2E, delta[0:1, :]):
                for term in three_terms(line):
                    lines += fold(term)
            lines.append(flags)
            lines.append(jnp.zeros((EXTRA - len(lines), width), F32))
            extra = jnp.concatenate(lines, axis=0).astype(BF16)
            out[2 * tile : 2 * tile + EXTRA, cols] = extra
            head += 1


def prep(first, counts, head_width, sizes, place, mask, q, g, o, lse):
    tile, full = q.shape
    count = sum(counts)
    offset = first * head_width
    cols = pl.BlockSpec(
        (pl.Element(tile), pl.Element(count * head_width)), lambda i, *_: (0, offset)
    )
    shapes = [(2 * tile + EXTRA, n * head_width) for n in counts]
    return pl.pallas_call(
        functools.partial(prep_kernel, counts, *sizes),
        grid_spec=pltpu.PrefetchScalarGridSpec(
            num_scalar_prefetch=3,
            grid=(1,),
            in_specs=[
                cols,
                cols,
                cols,
                pl.BlockSpec(
                    (pl.Element(count), pl.Element(1), pl.Element(tile)),
                    lambda i, *_: (first, 0, 0),
                ),
            ],
            out_specs=[pl.BlockSpec(shape, lambda i, *_: (0, 0)) for shape in shapes],
        ),
        out_shape=[jax.ShapeDtypeStruct(shape, BF16) for shape in shapes],
        compiler_params=pltpu.CompilerParams(vmem_limit_bytes=VMEM_LIMIT),
        cost_estimate=pl.CostEstimate(
            flops=2 * tile * count * head_width,
            bytes_accessed=10 * tile * count * head_width,
            transcendentals=0,
        ),
        name="prep",
    )(*place, mask, *(pltpu.with_memory_space_constraint(a, pltpu.HBM) for a in (q, g, o)), lse)


def pack_kernel(k_ref, v_ref, out, sems):
    copies = [
        pltpu.make_async_copy(source, out.at[i], sems.at[i])
        for i, source in enumerate((k_ref, v_ref))
    ]
    for copy in copies:
        copy.start()
    for copy in copies:
        copy.wait()


def pack(k, v):
    anywhere = pl.BlockSpec(memory_space=pl.ANY)
    return pl.pallas_call(
        pack_kernel,
        in_specs=[anywhere, anywhere],
        out_specs=anywhere,
        out_shape=jax.ShapeDtypeStruct((2,) + k.shape, k.dtype),
        scratch_shapes=[pltpu.SemaphoreType.DMA((2,))],
        cost_estimate=pl.CostEstimate(flops=0, bytes_accessed=8 * k.size, transcendentals=0),
        name="pack",
    )(k, v)


def row_stats(message, tile):
    extra = message[2 * tile : 2 * tile + EXTRA, :].astype(F32)
    parts = tile // 128
    rows = []
    for base in (0, 3 * parts):
        pieces = []
        for p in range(parts):
            a, b, c = (extra[base + i * parts + p : base + i * parts + p + 1] for i in range(3))
            pieces.append(a + b + c)
        rows.append(jnp.concatenate(pieces, axis=1))
    return (rows[0], rows[1], extra[6 * parts : 6 * parts + 1])


def stage_kernel(work, names, carried, last, factor, far_ref, *refs):
    env = dict(zip(names, refs))
    tile = env["message%d" % work[0][1][0]].shape[0] - EXTRA
    tile //= 2
    width = env["both"].shape[2] // 2
    used = sorted({j for _, js in work for j in js})
    stats = {j: row_stats(env["message%d" % j], tile) for j in used}
    both = {j: env["both"].at[i] for i, j in enumerate(used)}

    @pl.when(pl.program_id(0) == 0)
    def _():
        env["both"][...] = jnp.zeros_like(env["both"])

    for j in used:
        both[j][0:tile, 0:width] = env["message%d" % j][0:tile, :]
        both[j][tile:, width:] = env["message%d" % j][tile : 2 * tile, :]
    started = set()

    def add_q(j, term):
        name = "q%d" % j
        if name in started:
            env["sum_" + name][...] += term
        elif "acc_" + name in env:
            env["sum_" + name][...] = env["acc_" + name][...] + term
        else:
            env["sum_" + name][...] = term
        started.add(name)

    def pair(slot, j):
        shift, delta, flags = stats[j]
        lane = 3 * j + slot
        shift = jnp.where(flags[:, lane : lane + 1] > 0, shift, FAR_AWAY)
        keys = jnp.concatenate((env["keys%d" % slot][0], env["keys%d" % slot][1]), axis=1)
        products = dot(keys, both[j][...], ((1,), (1,)))
        weights = jnp.exp2(products[:, :tile] * (factor * LOG2E) - shift)
        grad_score = (weights * (products[:, tile:] - delta)).astype(BF16)
        joint = jnp.concatenate((grad_score, weights.astype(BF16)), axis=1)
        return (grad_score, dot(joint, both[j][...], ((1,), (0,))))

    def put_keys(slot, terms):
        name = "kv%d" % slot
        dk, dv = (terms[:, :width], terms[:, width:])
        if "acc_" + name in env:
            dk, dv = (dk + env["acc_" + name][0], dv + env["acc_" + name][1])
        out = env["out_" + name]
        out[0] = (dk * factor if name in last else dk).astype(out.dtype)
        out[1] = dv.astype(out.dtype)

    def frames(slots, js):
        terms = {}
        for j in js:
            scores = []
            for slot in slots:
                grad_score, term = pair(slot, j)
                terms[slot] = term if slot not in terms else terms[slot] + term
                scores.append(grad_score)
            keys = [env["keys%d" % slot][0] for slot in slots]
            joint = [jnp.concatenate(a, axis=0) if len(slots) > 1 else a[0] for a in (scores, keys)]
            add_q(j, dot(*joint, ((0,), (0,))))
        for slot in slots:
            put_keys(slot, terms[slot])

    near = [slot for slot, _ in work if slot != FAR]
    frames(near, work[0][1])
    for slot, js in work:
        if slot == FAR:
            pl.when(far_ref[0] > 0)(functools.partial(frames, [slot], js))

            @pl.when(far_ref[0] == 0)
            def _():
                out = env["out_kv%d" % FAR]
                out[...] = jnp.zeros_like(out)
                for j in js:
                    name = "q%d" % j
                    if name not in carried:
                        continue
                    env["sum_" + name][...] = env["acc_" + name][...]

    for j in used:
        out = env["out_q%d" % j]
        out[...] = (env["sum_q%d" % j][...]).astype(out.dtype)


def run_stage(work, weight, last, joined, first, count, head_width, far, keys, messages, sums):
    rows, wide = next(iter(messages.values())).shape
    tile = (rows - EXTRA) // 2
    one = pl.BlockSpec((tile, head_width), lambda h, *_: (0, h))
    two = pl.BlockSpec((2, tile, head_width), lambda h, *_: (0, 0, h))
    cols = pl.BlockSpec((2, tile, head_width), lambda h, *_: (0, 0, h + first))
    whole = pl.BlockSpec((rows, head_width), lambda h, *_: (0, h))
    used = sorted({j for _, js in work for j in js})
    slots = [slot for slot, _ in work]
    names, args, specs = ([], [], [])

    def give(name, arg, spec):
        names.append(name)
        args.append(arg)
        specs.append(spec)

    for j in used:
        give("message%d" % j, messages[j], whole)
    for slot in slots:
        give("keys%d" % slot, keys[slot], cols)
    touched = [("q%d" % j, one) for j in used] + [("kv%d" % s, two) for s in slots]
    carried = [name for name, _ in touched if name in sums]
    for name, spec in touched:
        if name in sums:
            give("acc_" + name, sums[name], spec)
    out_specs, out_shapes, aliases = ([], [], {})
    for name, spec in touched:
        shape = (tile, wide) if name.startswith("q") else (2, tile, wide)
        if name in last and name in joined:
            total, begun = joined[name]
            spec = cols
            shape = (2, tile, total)
            if begun is not None:
                aliases[1 + len(args)] = len(out_specs)
                give("begun_" + name, begun, pl.BlockSpec(memory_space=pl.ANY))
        out_specs.append(spec)
        out_shapes.append(jax.ShapeDtypeStruct(shape, BF16 if name in last else F32))
    names += ["out_" + name for name, _ in touched]
    names += ["both"] + ["sum_q%d" % j for j in used]
    pairs = count * sum(len(js) for _, js in work)
    results = pl.pallas_call(
        functools.partial(stage_kernel, work, names, carried, last, head_width**-0.5),
        grid_spec=pltpu.PrefetchScalarGridSpec(
            num_scalar_prefetch=1,
            grid=(count,),
            in_specs=specs,
            out_specs=out_specs,
            scratch_shapes=[pltpu.VMEM((len(used), 2 * tile, 2 * head_width), BF16)]
            + [pltpu.VMEM((tile, head_width), F32)] * len(used),
        ),
        out_shape=out_shapes,
        input_output_aliases=aliases,
        compiler_params=pltpu.CompilerParams(vmem_limit_bytes=VMEM_LIMIT),
        cost_estimate=pl.CostEstimate(
            flops=weight * pairs * tile * tile * head_width,
            bytes_accessed=20 * tile * wide,
            transcendentals=0,
        ),
        name="pairs",
    )(far, *args)
    return {**sums, **{name: value for (name, _), value in zip(touched, results)}}


def finish_kernel(factor, own_q, from_partner, from_outer, own_kv, near, far, *rest):
    out_q, out_k, out_v = rest[-3:]
    query = own_q[...] + from_partner[...].astype(F32) + from_outer[...].astype(F32)
    out_q[...] = (query * factor).astype(BF16)
    for i, (out, scale) in enumerate(((out_k, factor), (out_v, 1.0))):
        others = near[i].astype(F32) + far[i].astype(F32)
        out[...] = (own_kv[i] * scale + others).astype(BF16)


def finish(first, count, head_width, full, parts, so_far):
    tile = parts[0].shape[0]
    wide = count * head_width
    one = pl.BlockSpec((tile, wide), lambda i: (0, 0))
    two = pl.BlockSpec((2, tile, wide), lambda i: (0, 0, 0))

    def part(array):
        offset = first * head_width if array.shape[2] > wide else 0
        return pl.BlockSpec(
            (pl.Element(2), pl.Element(tile), pl.Element(wide)), lambda i: (0, 0, offset)
        )

    cols = pl.BlockSpec(
        (pl.Element(tile), pl.Element(wide)), lambda i: (0, first * head_width)
    )
    kept = [] if so_far is None else list(so_far)
    return pl.pallas_call(
        functools.partial(finish_kernel, head_width**-0.5),
        grid=(1,),
        in_specs=[one, one, one, two, part(parts[4]), part(parts[5])] + [pl.BlockSpec(memory_space=pl.ANY)] * len(kept),
        out_specs=[cols] * 3,
        out_shape=[jax.ShapeDtypeStruct((tile, full), BF16)] * 3,
        input_output_aliases={6 + i: i for i in range(len(kept))},
        compiler_params=pltpu.CompilerParams(vmem_limit_bytes=VMEM_LIMIT),
        cost_estimate=pl.CostEstimate(
            flops=8 * tile * count * head_width,
            bytes_accessed=30 * tile * count * head_width,
            transcendentals=0,
        ),
        name="finish",
    )(*parts, *kept)


def after(value, *earlier):
    return lax.optimization_barrier((value, *earlier))[0]


def per_device(queries, keys, values, outputs, out_grads, log_sums, window_mask):
    tile, full = queries.shape[2:]
    heads = log_sums.shape[2]
    width = full // heads
    frames, rows = (lax.axis_size("tm"), lax.axis_size("space"))
    q, k, v, o, g = (a.reshape(tile, full) for a in (queries, keys, values, outputs, out_grads))
    partner = [(i, i ^ 1) for i in range(rows)]
    onward = [(i, (i + 2) % rows) for i in range(0, rows, 2)]
    onward += [(i, (i - 2) % rows) for i in range(1, rows, 2)]
    owners = [(0, 0), (rows - 1, rows - 1)]
    for i in range(1, rows - 1, 2):
        owners += [(i, i + 1), (i + 1, i)]
    near_pairs = [(i, i ^ 1) for i in range(frames)]
    far_pairs = [(0, 0), (frames - 1, frames - 1)]
    for i in range(1, frames - 1, 2):
        far_pairs += [(i, i + 1), (i + 1, i)]

    frame, row = (lax.axis_index("tm"), lax.axis_index("space"))
    far_frame = frame - 1 + 2 * lax.rem(frame, 2)
    has_far = ((far_frame >= 0) & (far_frame < frames)).astype(jnp.int32).reshape(1)
    place = (frame.reshape(1), row.reshape(1))

    firsts = [sum(CHUNKS[:c]) for c in range(len(CHUNKS))]
    lse = log_sums.reshape(heads, 1, tile)
    mask = window_mask.reshape(9)
    own_kv = pack(k, v)
    near_kv = lax.ppermute(own_kv, "tm", near_pairs)
    far_kv = lax.ppermute(own_kv, "tm", far_pairs)
    make = lambda first, counts, source: prep(
        first, counts, width, (frames, rows), place, mask, source, g, o, lse
    )
    mine = make(0, CHUNKS[:1], q)
    theirs = {0: lax.ppermute(mine[0], "space", partner)}
    mine += make(firsts[1], CHUNKS[1:], after(q, mine[0]))
    frames_kv = {HERE: own_kv, NEAR: near_kv, FAR: far_kv}
    last = len(CHUNKS) - 1
    outers = {}
    sums = [{} for _ in CHUNKS]
    backs = [{} for _ in CHUNKS]
    done = []
    out = None

    def stage(c, step, *awaited):
        messages = {OUTER: outers.get(c), OWN: mine[c], PARTNER: theirs.get(c)}
        stages = LATER_STAGES if c else STAGES
        work = stages[step]
        needed = {j: messages[j] for _, js in work for j in js}
        first_used = min(needed)
        arrived = [backs[i][name] for i, name in awaited]
        needed[first_used] = after(needed[first_used], *done[-1:], *arrived)
        later = {j for other in stages[step + 1 :] for _, js in other for j in js}
        slots = {slot for other in stages[step + 1 :] for slot, _ in other}
        final = {"q%d" % j for j in (OUTER, PARTNER) if j not in later}
        final |= {"kv%d" % slot for slot in (NEAR, FAR) if slot not in slots}
        joined = {}
        if c < last and step + 1 == len(stages):
            for name in JOINED:
                joined[name] = (firsts[last] * width, sums[c - 1][name] if c else None)
        sums[c] = run_stage(
            work, WEIGHTS[c][step], final, joined, firsts[c], CHUNKS[c], width, has_far, frames_kv, needed, sums[c]
        )
        done.append(sums[c]["kv0"])
        for name, axis, pairs in (
            ("q0", "space", owners),
            ("q2", "space", partner),
            ("kv1", "tm", near_pairs),
            ("kv2", "tm", far_pairs),
        ):
            if name not in final or name not in sums[c] or name in backs[c]:
                continue
            if name in joined and c + 1 < last:
                continue
            backs[c][name] = lax.ppermute(sums[c][name], axis, pairs)
            if name in joined:
                for earlier in range(c):
                    backs[earlier][name] = backs[c][name]

    def hand_on(c):
        outers[c] = lax.ppermute(after(theirs[c], *done[-1:]), "space", onward)

    def complete(c, so_far):
        back = backs[c]
        own = after(sums[c]["q1"], *done[-1:])
        so_far = finish(
            firsts[c], CHUNKS[c], width, full,
            (own, back["q2"], back["q0"], sums[c]["kv0"], back["kv1"], back["kv2"]), so_far,
        )
        done.append(so_far[0])
        return so_far

    for c in range(1, len(CHUNKS)):
        theirs[c] = lax.ppermute(mine[c], "space", partner)
    for kind, c, *rest in ORDER:
        if kind == "stage":
            stage(c, *rest)
        elif kind == "hand":
            hand_on(c)
        else:
            out = complete(c, out)
    return tuple(a.reshape(queries.shape) for a in out)


def solution(mesh):
    tile = P("tm", "space", None, None)
    return jax.shard_map(
        per_device,
        mesh=mesh,
        in_specs=(tile,) * 6 + (P("tm", "space", None),),
        out_specs=(tile,) * 3,
        check_vma=False,
    )
```

```python
import functools
import math

import jax
import jax.numpy as jnp
from jax import lax
from jax.experimental import pallas as pl
from jax.experimental.pallas import tpu as pltpu
from jax.sharding import PartitionSpec as P

F32 = jnp.float32
BF16 = jnp.bfloat16
LOG2E = math.log2(math.e)
FAR_AWAY = 1e30

OUTER, OWN, PARTNER = (0, 1, 2)
HERE, NEAR, FAR = (0, 1, 2)
CHUNKS = (4, 5, 3)
STAGES = (
    ((HERE, (OWN,)), (NEAR, (OWN,))),
    ((HERE, (PARTNER,)), (NEAR, (PARTNER,))),
    ((HERE, (OUTER,)), (NEAR, (OUTER,)), (FAR, (OWN, PARTNER, OUTER))),
)
LATER_STAGES = (
    STAGES[0],
    STAGES[1] + ((FAR, (PARTNER,)),),
    ((HERE, (OUTER,)), (NEAR, (OUTER,)), (FAR, (OWN, OUTER))),
)
ORDER = (('stage', 0, 0), ('stage', 1, 0), ('hand', 0), ('stage', 2, 0), ('stage', 0, 1), ('hand', 1), ('stage', 1, 1), ('stage', 0, 2), ('hand', 2), ('stage', 2, 1), ('stage', 1, 2, (0, 'q0')), ('stage', 2, 2, (0, 'q2'), (0, 'kv1')), ('finish', 0), ('finish', 1), ('finish', 2))
JOINED = ()
WEIGHTS = ((40, 40, 20), (20, 10, 20), (20, 40, 40))
EXTRA = 32
VMEM_LIMIT = 16 * 1024 * 1024


def dot(a, b, dims):
    return lax.dot_general(a, b, (dims, ((), ())), preferred_element_type=F32)


def three_terms(row):
    terms = []
    for _ in range(3):
        term = row.astype(BF16).astype(F32)
        terms.append(term)
        row = row - term
    return terms


def fold(row):
    lanes = 128
    return [row[:, i : i + lanes] for i in range(0, row.shape[1], lanes)]


def flag_row(frames, rows, frame, row, mask_ref, lanes):
    toward = 1 - 2 * lax.rem(row, 2)
    near = 1 - 2 * lax.rem(frame, 2)
    lane = lax.broadcasted_iota(jnp.int32, (1, lanes), 1)
    flags = jnp.zeros((1, lanes), F32)
    for role in (OUTER, OWN, PARTNER):
        for slot in (HERE, NEAR, FAR):
            row_off = (role - 1) * toward
            frame_off = (0, near, -near)[slot]
            inside = (
                (row + row_off >= 0)
                & (row + row_off < rows)
                & (frame + frame_off >= 0)
                & (frame + frame_off < frames)
            )
            index = 3 * (frame_off + 1) + row_off + 1
            on = inside & ((mask_ref[index] > 0) | (index == 4))
            flags = jnp.where(lane == 3 * role + slot, on.astype(F32), flags)
    return flags


def prep_kernel(
    counts, frames, rows, frame_ref, row_ref, mask_ref, q_ref, g_ref, o_ref, lse_ref, *outs
):
    tile = q_ref.shape[0]
    width = q_ref.shape[1] // sum(counts)
    flags = flag_row(frames, rows, frame_ref[0], row_ref[0], mask_ref, width)
    ones = jnp.ones((8, width), BF16)
    head = 0
    for out, count in zip(outs, counts):
        for h in range(count):
            source = slice(head * width, (head + 1) * width)
            cols = slice(h * width, (h + 1) * width)
            grad = g_ref[:, source]
            out[0:tile, cols] = q_ref[:, source]
            out[tile : 2 * tile, cols] = grad
            prod = grad.astype(F32) * o_ref[:, source].astype(F32)
            high = prod.astype(BF16)
            low = (prod - high.astype(F32)).astype(BF16)
            delta = dot(ones, high, ((1,), (1,))) + dot(ones, low, ((1,), (1,)))
            lines = []
            for line in (lse_ref[head] * LOG2E, delta[0:1, :]):
                for term in three_terms(line):
                    lines += fold(term)
            lines.append(flags)
            lines.append(jnp.zeros((EXTRA - len(lines), width), F32))
            extra = jnp.concatenate(lines, axis=0).astype(BF16)
            out[2 * tile : 2 * tile + EXTRA, cols] = extra
            head += 1


def prep(first, counts, head_width, sizes, place, mask, q, g, o, lse):
    tile, full = q.shape
    count = sum(counts)
    offset = first * head_width
    cols = pl.BlockSpec(
        (pl.Element(tile), pl.Element(count * head_width)), lambda i, *_: (0, offset)
    )
    shapes = [(2 * tile + EXTRA, n * head_width) for n in counts]
    return pl.pallas_call(
        functools.partial(prep_kernel, counts, *sizes),
        grid_spec=pltpu.PrefetchScalarGridSpec(
            num_scalar_prefetch=3,
            grid=(1,),
            in_specs=[
                cols,
                cols,
                cols,
                pl.BlockSpec(
                    (pl.Element(count), pl.Element(1), pl.Element(tile)),
                    lambda i, *_: (first, 0, 0),
                ),
            ],
            out_specs=[pl.BlockSpec(shape, lambda i, *_: (0, 0)) for shape in shapes],
        ),
        out_shape=[jax.ShapeDtypeStruct(shape, BF16) for shape in shapes],
        compiler_params=pltpu.CompilerParams(vmem_limit_bytes=VMEM_LIMIT),
        cost_estimate=pl.CostEstimate(
            flops=2 * tile * count * head_width,
            bytes_accessed=10 * tile * count * head_width,
            transcendentals=0,
        ),
        name="prep",
    )(*place, mask, *(pltpu.with_memory_space_constraint(a, pltpu.HBM) for a in (q, g, o)), lse)


def pack_kernel(k_ref, v_ref, out):
    out[0] = k_ref[...]
    out[1] = v_ref[...]


def pack(k, v, steps=2):
    tile, full = k.shape
    cols = pl.BlockSpec((tile, full // steps), lambda i: (0, i))
    return pl.pallas_call(
        pack_kernel,
        grid=(steps,),
        in_specs=[cols, cols],
        out_specs=pl.BlockSpec((2, tile, full // steps), lambda i: (0, 0, i)),
        out_shape=jax.ShapeDtypeStruct((2, tile, full), k.dtype),
        compiler_params=pltpu.CompilerParams(vmem_limit_bytes=VMEM_LIMIT),
        cost_estimate=pl.CostEstimate(flops=0, bytes_accessed=8 * k.size, transcendentals=0),
        name="pack",
    )(*(pltpu.with_memory_space_constraint(a, pltpu.HBM) for a in (k, v)))


def row_stats(message, tile):
    extra = message[2 * tile : 2 * tile + EXTRA, :].astype(F32)
    parts = tile // 128
    rows = []
    for base in (0, 3 * parts):
        pieces = []
        for p in range(parts):
            a, b, c = (extra[base + i * parts + p : base + i * parts + p + 1] for i in range(3))
            pieces.append(a + b + c)
        rows.append(jnp.concatenate(pieces, axis=1))
    return (rows[0], rows[1], extra[6 * parts : 6 * parts + 1])


def stage_kernel(work, names, carried, last, factor, far_ref, *refs):
    env = dict(zip(names, refs))
    tile = env["message%d" % work[0][1][0]].shape[0] - EXTRA
    tile //= 2
    width = env["message%d" % work[0][1][0]].shape[1]
    used = sorted({j for _, js in work for j in js})
    stats = {j: row_stats(env["message%d" % j], tile) for j in used}
    started = set()

    def add_q(j, term):
        name = "q%d" % j
        if name in started:
            env["sum_" + name][...] += term
        elif "acc_" + name in env:
            env["sum_" + name][...] = env["acc_" + name][...] + term
        else:
            env["sum_" + name][...] = term
        started.add(name)

    def operands(slot, j):
        message = env["message%d" % j]
        return (message[0:tile, :], message[tile : 2 * tile, :], env["keys%d" % slot])

    def products(slot, j):
        qj, gj, keys = operands(slot, j)
        return (dot(keys[0], qj, ((1,), (1,))), dot(keys[1], gj, ((1,), (1,))))

    def terms_of(slot, j, scores, grad_prob):
        qj, gj, keys = operands(slot, j)
        shift, delta, flags = stats[j]
        lane = 3 * j + slot
        shift = jnp.where(flags[:, lane : lane + 1] > 0, shift, FAR_AWAY)
        weights = jnp.exp2(scores * (factor * LOG2E) - shift)
        grad_score = (weights * (grad_prob - delta)).astype(BF16)
        return (
            dot(grad_score, keys[0], ((0,), (0,))),
            dot(grad_score, qj, ((1,), (0,))),
            dot(weights.astype(BF16), gj, ((1,), (0,))),
        )

    def put_keys(slot, terms):
        name = "kv%d" % slot
        dk, dv = terms
        if "acc_" + name in env:
            dk, dv = (dk + env["acc_" + name][0], dv + env["acc_" + name][1])
        out = env["out_" + name]
        out[0] = (dk * factor if name in last else dk).astype(out.dtype)
        out[1] = dv.astype(out.dtype)

    def frames(slots, js):
        todo = [(slot, j) for slot in slots for j in js]
        sums = {}
        ahead = products(*todo[0])
        for i, (slot, j) in enumerate(todo):
            now, ahead = (ahead, products(*todo[i + 1]) if i + 1 < len(todo) else None)
            term_q, term_k, term_v = terms_of(slot, j, *now)
            add_q(j, term_q)
            if slot in sums:
                term_k, term_v = (term_k + sums[slot][0], term_v + sums[slot][1])
            sums[slot] = (term_k, term_v)
        for slot in slots:
            put_keys(slot, sums[slot])

    near = [slot for slot, _ in work if slot != FAR]
    frames(near, work[0][1])
    for slot, js in work:
        if slot == FAR:
            pl.when(far_ref[0] > 0)(functools.partial(frames, [slot], js))

            @pl.when(far_ref[0] == 0)
            def _():
                out = env["out_kv%d" % FAR]
                out[...] = jnp.zeros_like(out)
                for j in js:
                    name = "q%d" % j
                    if name not in carried:
                        continue
                    env["sum_" + name][...] = env["acc_" + name][...]

    for j in used:
        out = env["out_q%d" % j]
        out[...] = (env["sum_q%d" % j][...]).astype(out.dtype)


def run_stage(work, weight, last, joined, first, count, head_width, far, keys, messages, sums):
    rows, wide = next(iter(messages.values())).shape
    tile = (rows - EXTRA) // 2
    one = pl.BlockSpec((tile, head_width), lambda h, *_: (0, h))
    two = pl.BlockSpec((2, tile, head_width), lambda h, *_: (0, 0, h))
    cols = pl.BlockSpec((2, tile, head_width), lambda h, *_: (0, 0, h + first))
    whole = pl.BlockSpec((rows, head_width), lambda h, *_: (0, h))
    used = sorted({j for _, js in work for j in js})
    slots = [slot for slot, _ in work]
    names, args, specs = ([], [], [])

    def give(name, arg, spec):
        names.append(name)
        args.append(arg)
        specs.append(spec)

    for j in used:
        give("message%d" % j, messages[j], whole)
    for slot in slots:
        give("keys%d" % slot, keys[slot], cols)
    touched = [("q%d" % j, one) for j in used] + [("kv%d" % s, two) for s in slots]
    carried = [name for name, _ in touched if name in sums]
    for name, spec in touched:
        if name in sums:
            give("acc_" + name, sums[name], spec)
    out_specs, out_shapes, aliases = ([], [], {})
    for name, spec in touched:
        shape = (tile, wide) if name.startswith("q") else (2, tile, wide)
        if name in last and name in joined:
            total, begun = joined[name]
            spec = cols
            shape = (2, tile, total)
            if begun is not None:
                aliases[1 + len(args)] = len(out_specs)
                give("begun_" + name, begun, pl.BlockSpec(memory_space=pl.ANY))
        out_specs.append(spec)
        out_shapes.append(jax.ShapeDtypeStruct(shape, BF16 if name in last else F32))
    names += ["out_" + name for name, _ in touched]
    names += ["sum_q%d" % j for j in used]
    pairs = count * sum(len(js) for _, js in work)
    results = pl.pallas_call(
        functools.partial(stage_kernel, work, names, carried, last, head_width**-0.5),
        grid_spec=pltpu.PrefetchScalarGridSpec(
            num_scalar_prefetch=1,
            grid=(count,),
            in_specs=specs,
            out_specs=out_specs,
            scratch_shapes=[pltpu.VMEM((tile, head_width), F32)] * len(used),
        ),
        out_shape=out_shapes,
        input_output_aliases=aliases,
        compiler_params=pltpu.CompilerParams(vmem_limit_bytes=VMEM_LIMIT),
        cost_estimate=pl.CostEstimate(
            flops=weight * pairs * tile * tile * head_width,
            bytes_accessed=20 * tile * wide,
            transcendentals=0,
        ),
        name="pairs",
    )(far, *args)
    return {**sums, **{name: value for (name, _), value in zip(touched, results)}}


def finish_kernel(factor, own_q, from_partner, from_outer, own_kv, near, far, *rest):
    out_q, out_k, out_v = rest[-3:]
    query = own_q[...] + from_partner[...].astype(F32) + from_outer[...].astype(F32)
    out_q[...] = (query * factor).astype(BF16)
    for i, (out, scale) in enumerate(((out_k, factor), (out_v, 1.0))):
        others = near[i].astype(F32) + far[i].astype(F32)
        out[...] = (own_kv[i] * scale + others).astype(BF16)


def finish(first, count, head_width, full, parts, so_far):
    tile = parts[0].shape[0]
    wide = count * head_width
    one = pl.BlockSpec((tile, wide), lambda i: (0, 0))
    two = pl.BlockSpec((2, tile, wide), lambda i: (0, 0, 0))

    def part(array):
        offset = first * head_width if array.shape[2] > wide else 0
        return pl.BlockSpec(
            (pl.Element(2), pl.Element(tile), pl.Element(wide)), lambda i: (0, 0, offset)
        )

    cols = pl.BlockSpec(
        (pl.Element(tile), pl.Element(wide)), lambda i: (0, first * head_width)
    )
    kept = [] if so_far is None else list(so_far)
    return pl.pallas_call(
        functools.partial(finish_kernel, head_width**-0.5),
        grid=(1,),
        in_specs=[one, one, one, two, part(parts[4]), part(parts[5])] + [pl.BlockSpec(memory_space=pl.ANY)] * len(kept),
        out_specs=[cols] * 3,
        out_shape=[jax.ShapeDtypeStruct((tile, full), BF16)] * 3,
        input_output_aliases={6 + i: i for i in range(len(kept))},
        compiler_params=pltpu.CompilerParams(vmem_limit_bytes=VMEM_LIMIT),
        cost_estimate=pl.CostEstimate(
            flops=8 * tile * count * head_width,
            bytes_accessed=30 * tile * count * head_width,
            transcendentals=0,
        ),
        name="finish",
    )(*parts, *kept)


def after(value, *earlier):
    return lax.optimization_barrier((value, *earlier))[0]


def per_device(queries, keys, values, outputs, out_grads, log_sums, window_mask):
    tile, full = queries.shape[2:]
    heads = log_sums.shape[2]
    width = full // heads
    frames, rows = (lax.axis_size("tm"), lax.axis_size("space"))
    q, k, v, o, g = (a.reshape(tile, full) for a in (queries, keys, values, outputs, out_grads))
    partner = [(i, i ^ 1) for i in range(rows)]
    onward = [(i, (i + 2) % rows) for i in range(0, rows, 2)]
    onward += [(i, (i - 2) % rows) for i in range(1, rows, 2)]
    owners = [(0, 0), (rows - 1, rows - 1)]
    for i in range(1, rows - 1, 2):
        owners += [(i, i + 1), (i + 1, i)]
    near_pairs = [(i, i ^ 1) for i in range(frames)]
    far_pairs = [(0, 0), (frames - 1, frames - 1)]
    for i in range(1, frames - 1, 2):
        far_pairs += [(i, i + 1), (i + 1, i)]

    frame, row = (lax.axis_index("tm"), lax.axis_index("space"))
    far_frame = frame - 1 + 2 * lax.rem(frame, 2)
    has_far = ((far_frame >= 0) & (far_frame < frames)).astype(jnp.int32).reshape(1)
    place = (frame.reshape(1), row.reshape(1))

    firsts = [sum(CHUNKS[:c]) for c in range(len(CHUNKS))]
    lse = log_sums.reshape(heads, 1, tile)
    mask = window_mask.reshape(9)
    own_kv = pack(k, v)
    near_kv = lax.ppermute(own_kv, "tm", near_pairs)
    far_kv = lax.ppermute(own_kv, "tm", far_pairs)
    make = lambda first, counts, source: prep(
        first, counts, width, (frames, rows), place, mask, source, g, o, lse
    )
    mine = make(0, CHUNKS[:1], q)
    theirs = {0: lax.ppermute(mine[0], "space", partner)}
    mine += make(firsts[1], CHUNKS[1:], after(q, mine[0]))
    frames_kv = {HERE: own_kv, NEAR: near_kv, FAR: far_kv}
    last = len(CHUNKS) - 1
    outers = {}
    sums = [{} for _ in CHUNKS]
    backs = [{} for _ in CHUNKS]
    done = []
    out = None

    def stage(c, step, *awaited):
        messages = {OUTER: outers.get(c), OWN: mine[c], PARTNER: theirs.get(c)}
        stages = LATER_STAGES if c else STAGES
        work = stages[step]
        needed = {j: messages[j] for _, js in work for j in js}
        first_used = min(needed)
        arrived = [backs[i][name] for i, name in awaited]
        needed[first_used] = after(needed[first_used], *done[-1:], *arrived)
        later = {j for other in stages[step + 1 :] for _, js in other for j in js}
        slots = {slot for other in stages[step + 1 :] for slot, _ in other}
        final = {"q%d" % j for j in (OUTER, PARTNER) if j not in later}
        final |= {"kv%d" % slot for slot in (NEAR, FAR) if slot not in slots}
        joined = {}
        if c < last and step + 1 == len(stages):
            for name in JOINED:
                joined[name] = (firsts[last] * width, sums[c - 1][name] if c else None)
        sums[c] = run_stage(
            work, WEIGHTS[c][step], final, joined, firsts[c], CHUNKS[c], width, has_far, frames_kv, needed, sums[c]
        )
        done.append(sums[c]["kv0"])
        for name, axis, pairs in (
            ("q0", "space", owners),
            ("q2", "space", partner),
            ("kv1", "tm", near_pairs),
            ("kv2", "tm", far_pairs),
        ):
            if name not in final or name not in sums[c] or name in backs[c]:
                continue
            if name in joined and c + 1 < last:
                continue
            backs[c][name] = lax.ppermute(sums[c][name], axis, pairs)
            if name in joined:
                for earlier in range(c):
                    backs[earlier][name] = backs[c][name]

    def hand_on(c):
        outers[c] = lax.ppermute(after(theirs[c], *done[-1:]), "space", onward)

    def complete(c, so_far):
        back = backs[c]
        own = after(sums[c]["q1"], *done[-1:])
        so_far = finish(
            firsts[c], CHUNKS[c], width, full,
            (own, back["q2"], back["q0"], sums[c]["kv0"], back["kv1"], back["kv2"]), so_far,
        )
        done.append(so_far[0])
        return so_far

    for c in range(1, len(CHUNKS)):
        theirs[c] = lax.ppermute(mine[c], "space", partner)
    for kind, c, *rest in ORDER:
        if kind == "stage":
            stage(c, *rest)
        elif kind == "hand":
            hand_on(c)
        else:
            out = complete(c, out)
    return tuple(a.reshape(queries.shape) for a in out)


def solution(mesh):
    tile = P("tm", "space", None, None)
    return jax.shard_map(
        per_device,
        mesh=mesh,
        in_specs=(tile,) * 6 + (P("tm", "space", None),),
        out_specs=(tile,) * 3,
        check_vma=False,
    )
```

```python
import functools
import math

import jax
import jax.numpy as jnp
from jax import lax
from jax.experimental import pallas as pl
from jax.experimental.pallas import tpu as pltpu
from jax.sharding import PartitionSpec as P

F32 = jnp.float32
BF16 = jnp.bfloat16
FAR_AWAY = 1e30

OUTER, OWN, PARTNER = (0, 1, 2)
HERE, NEAR, FAR = (0, 1, 2)
CHUNKS = (4, 4, 4)
STAGES = (
    ((HERE, (OWN,)), (NEAR, (OWN,))),
    ((HERE, (PARTNER,)), (NEAR, (PARTNER,))),
    ((HERE, (OUTER,)), (NEAR, (OUTER,)), (FAR, (OWN, PARTNER, OUTER))),
)
LATER_STAGES = (
    STAGES[0],
    STAGES[1] + ((FAR, (PARTNER,)),),
    ((HERE, (OUTER,)), (NEAR, (OUTER,)), (FAR, (OWN, OUTER))),
)
ORDER = (('stage', 0, 0), ('stage', 1, 0), ('hand', 0), ('stage', 0, 1), ('stage', 2, 0), ('hand', 1), ('stage', 1, 1), ('stage', 0, 2), ('hand', 2), ('stage', 2, 1), ('stage', 1, 2, (0, 'q0')), ('stage', 2, 2, (1, 'q2'), (0, 'kv1')), ('finish', 0), ('finish', 1), ('finish', 2))
JOINED = ('kv2',)
WEIGHTS = ((20, 160, 40), (10, 448, 20), (224, 4, 80))
EXTRA = 32
VMEM_LIMIT = 20 * 1024 * 1024
GROUP = 2


def dot(a, b, dims):
    return lax.dot_general(a, b, (dims, ((), ())), preferred_element_type=F32)


def three_terms(row):
    terms = []
    for _ in range(3):
        term = row.astype(BF16).astype(F32)
        terms.append(term)
        row = row - term
    return terms


def fold(row):
    lanes = 128
    return [row[:, i : i + lanes] for i in range(0, row.shape[1], lanes)]


def flag_row(frames, rows, frame, row, mask_ref, lanes):
    toward = 1 - 2 * lax.rem(row, 2)
    near = 1 - 2 * lax.rem(frame, 2)
    lane = lax.broadcasted_iota(jnp.int32, (1, lanes), 1)
    flags = jnp.zeros((1, lanes), F32)
    for role in (OUTER, OWN, PARTNER):
        for slot in (HERE, NEAR, FAR):
            row_off = (role - 1) * toward
            frame_off = (0, near, -near)[slot]
            inside = (
                (row + row_off >= 0)
                & (row + row_off < rows)
                & (frame + frame_off >= 0)
                & (frame + frame_off < frames)
            )
            index = 3 * (frame_off + 1) + row_off + 1
            on = inside & ((mask_ref[index] > 0) | (index == 4))
            flags = jnp.where(lane == 3 * role + slot, on.astype(F32), flags)
    return flags


def prep_kernel(
    counts, frames, rows, frame_ref, row_ref, mask_ref, q_ref, g_ref, o_ref, lse_ref, *outs
):
    tile = q_ref.shape[0]
    width = q_ref.shape[1] // sum(counts)
    flags = flag_row(frames, rows, frame_ref[0], row_ref[0], mask_ref, width)
    ones = jnp.ones((8, width), BF16)
    head = 0
    for out, count in zip(outs, counts):
        for h in range(count):
            source = slice(head * width, (head + 1) * width)
            cols = slice(h * width, (h + 1) * width)
            grad = g_ref[:, source]
            out[0:tile, cols] = q_ref[:, source]
            out[tile : 2 * tile, cols] = grad
            prod = grad.astype(F32) * o_ref[:, source].astype(F32)
            high = prod.astype(BF16)
            low = (prod - high.astype(F32)).astype(BF16)
            delta = dot(ones, high, ((1,), (1,))) + dot(ones, low, ((1,), (1,)))
            lines = []
            for line in (lse_ref[head], delta[0:1, :]):
                for term in three_terms(line):
                    lines += fold(term)
            lines.append(flags)
            lines.append(jnp.zeros((EXTRA - len(lines), width), F32))
            extra = jnp.concatenate(lines, axis=0).astype(BF16)
            out[2 * tile : 2 * tile + EXTRA, cols] = extra
            head += 1


def prep(first, counts, head_width, sizes, place, mask, q, g, o, lse):
    tile, full = q.shape
    count = sum(counts)
    offset = first * head_width
    cols = pl.BlockSpec(
        (pl.Element(tile), pl.Element(count * head_width)), lambda i, *_: (0, offset)
    )
    shapes = [(2 * tile + EXTRA, n * head_width) for n in counts]
    return pl.pallas_call(
        functools.partial(prep_kernel, counts, *sizes),
        grid_spec=pltpu.PrefetchScalarGridSpec(
            num_scalar_prefetch=3,
            grid=(1,),
            in_specs=[
                cols,
                cols,
                cols,
                pl.BlockSpec(
                    (pl.Element(count), pl.Element(1), pl.Element(tile)),
                    lambda i, *_: (first, 0, 0),
                ),
            ],
            out_specs=[pl.BlockSpec(shape, lambda i, *_: (0, 0)) for shape in shapes],
        ),
        out_shape=[jax.ShapeDtypeStruct(shape, BF16) for shape in shapes],
        compiler_params=pltpu.CompilerParams(vmem_limit_bytes=VMEM_LIMIT),
        cost_estimate=pl.CostEstimate(
            flops=2 * tile * count * head_width,
            bytes_accessed=10 * tile * count * head_width,
            transcendentals=0,
        ),
        name="prep",
    )(*place, mask, *(pltpu.with_memory_space_constraint(a, pltpu.HBM) for a in (q, g, o)), lse)


def pack_kernel(k_ref, v_ref, out):
    out[0] = k_ref[...]
    out[1] = v_ref[...]


def pack(k, v, steps=2):
    tile, full = k.shape
    cols = pl.BlockSpec((tile, full // steps), lambda i: (0, i))
    return pl.pallas_call(
        pack_kernel,
        grid=(steps,),
        in_specs=[cols, cols],
        out_specs=pl.BlockSpec((2, tile, full // steps), lambda i: (0, 0, i)),
        out_shape=jax.ShapeDtypeStruct((2, tile, full), k.dtype),
        compiler_params=pltpu.CompilerParams(vmem_limit_bytes=VMEM_LIMIT),
        cost_estimate=pl.CostEstimate(flops=0, bytes_accessed=8 * k.size, transcendentals=0),
        name="pack",
    )(*(pltpu.with_memory_space_constraint(a, pltpu.HBM) for a in (k, v)))


def row_stats(message, tile):
    extra = message[2 * tile : 2 * tile + EXTRA, :].astype(F32)
    parts = tile // 128
    rows = []
    for base in (0, 3 * parts):
        pieces = []
        for p in range(parts):
            a, b, c = (extra[base + i * parts + p : base + i * parts + p + 1] for i in range(3))
            pieces.append(a + b + c)
        rows.append(jnp.concatenate(pieces, axis=1))
    return (rows[0], rows[1], extra[6 * parts : 6 * parts + 1])


def stage_kernel(work, names, carried, last, factor, group, far_ref, *refs):
    env = dict(zip(names, refs))
    tile, wide = env["message%d" % work[0][1][0]].shape
    tile = (tile - EXTRA) // 2
    width = wide // group
    heads = [slice(i * width, (i + 1) * width) for i in range(group)]
    used = sorted({j for _, js in work for j in js})
    stats = {
        (j, i): row_stats(env["message%d" % j].at[:, cols], tile)
        for j in used
        for i, cols in enumerate(heads)
    }
    started = set()

    def add_q(j, i, term):
        name, cols = ("q%d" % j, heads[i])
        if (j, i) in started:
            env["sum_" + name][:, cols] += term
        elif "acc_" + name in env:
            env["sum_" + name][:, cols] = env["acc_" + name][:, cols] + term
        else:
            env["sum_" + name][:, cols] = term
        started.add((j, i))

    def pair_terms(slot, j, i):
        cols = heads[i]
        message, keys = (env["message%d" % j], env["keys%d" % slot])
        queries, grads = (message[0:tile, cols], message[tile : 2 * tile, cols])
        key, value = (keys[0, :, cols], keys[1, :, cols])
        shift, delta, flags = stats[j, i]
        lane = 3 * j + slot
        shift = jnp.where(flags[:, lane : lane + 1] > 0, shift, FAR_AWAY)
        scores = dot(key, queries, ((1,), (1,)))
        weights = jnp.exp(scores * factor - shift)
        grad_prob = dot(value, grads, ((1,), (1,)))
        grad_score = (weights * (grad_prob - delta)).astype(BF16)
        add_q(j, i, dot(grad_score, key, ((0,), (0,))))
        return (
            dot(grad_score, queries, ((1,), (0,))),
            dot(weights.astype(BF16), grads, ((1,), (0,))),
        )

    def key_frames(slots_js):
        for slot, js in slots_js:
            name = "kv%d" % slot
            out = env["out_" + name]
            for i, cols in enumerate(heads):
                dk, dv = pair_terms(slot, js[0], i)
                for j in js[1:]:
                    more_k, more_v = pair_terms(slot, j, i)
                    dk, dv = (dk + more_k, dv + more_v)
                if "acc_" + name in env:
                    acc = env["acc_" + name]
                    dk, dv = (dk + acc[0, :, cols], dv + acc[1, :, cols])
                out[0, :, cols] = (dk * factor if name in last else dk).astype(out.dtype)
                out[1, :, cols] = dv.astype(out.dtype)

    key_frames([(slot, js) for slot, js in work if slot != FAR])
    for slot, js in work:
        if slot == FAR:
            fresh = [j for j in js if (j, 0) not in started]
            pl.when(far_ref[0] > 0)(functools.partial(key_frames, [(slot, js)]))

            @pl.when(far_ref[0] == 0)
            def _():
                out = env["out_kv%d" % FAR]
                out[...] = jnp.zeros_like(out)
                for j in fresh:
                    name = "q%d" % j
                    env["sum_" + name][...] = env["acc_" + name][...]

    for j in used:
        out = env["out_q%d" % j]
        out[...] = (env["sum_q%d" % j][...]).astype(out.dtype)


def run_stage(work, weight, last, joined, first, count, head_width, far, keys, messages, sums):
    rows, wide = next(iter(messages.values())).shape
    tile = (rows - EXTRA) // 2
    group = math.gcd(count, GROUP) if first % math.gcd(count, GROUP) == 0 else 1
    step, begin = (group * head_width, first // group)
    one = pl.BlockSpec((tile, step), lambda h, *_: (0, h))
    two = pl.BlockSpec((2, tile, step), lambda h, *_: (0, 0, h))
    cols = pl.BlockSpec((2, tile, step), lambda h, *_: (0, 0, h + begin))
    whole = pl.BlockSpec((rows, step), lambda h, *_: (0, h))
    used = sorted({j for _, js in work for j in js})
    slots = [slot for slot, _ in work]
    names, args, specs = ([], [], [])

    def give(name, arg, spec):
        names.append(name)
        args.append(arg)
        specs.append(spec)

    for j in used:
        give("message%d" % j, messages[j], whole)
    for slot in slots:
        give("keys%d" % slot, keys[slot], cols)
    touched = [("q%d" % j, one) for j in used] + [("kv%d" % s, two) for s in slots]
    carried = [name for name, _ in touched if name in sums]
    for name, spec in touched:
        if name in sums:
            give("acc_" + name, sums[name], spec)
    out_specs, out_shapes, aliases = ([], [], {})
    for name, spec in touched:
        shape = (tile, wide) if name.startswith("q") else (2, tile, wide)
        if name in last and name in joined:
            total, begun = joined[name]
            spec = cols
            shape = (2, tile, total)
            if begun is not None:
                aliases[1 + len(args)] = len(out_specs)
                give("begun_" + name, begun, pl.BlockSpec(memory_space=pl.ANY))
        out_specs.append(spec)
        out_shapes.append(jax.ShapeDtypeStruct(shape, BF16 if name in last else F32))
    names += ["out_" + name for name, _ in touched]
    names += ["sum_q%d" % j for j in used]
    pairs = count * sum(len(js) for _, js in work)
    results = pl.pallas_call(
        functools.partial(stage_kernel, work, names, carried, last, head_width**-0.5, group),
        grid_spec=pltpu.PrefetchScalarGridSpec(
            num_scalar_prefetch=1,
            grid=(count // group,),
            in_specs=specs,
            out_specs=out_specs,
            scratch_shapes=[pltpu.VMEM((tile, step), F32)] * len(used),
        ),
        out_shape=out_shapes,
        input_output_aliases=aliases,
        compiler_params=pltpu.CompilerParams(vmem_limit_bytes=VMEM_LIMIT),
        cost_estimate=pl.CostEstimate(
            flops=weight * pairs * tile * tile * head_width,
            bytes_accessed=20 * tile * wide,
            transcendentals=0,
        ),
        name="pairs",
    )(far, *args)
    return {**sums, **{name: value for (name, _), value in zip(touched, results)}}


def finish_kernel(factor, own_q, from_partner, from_outer, own_kv, near, far, *rest):
    out_q, out_k, out_v = rest[-3:]
    query = own_q[...] + from_partner[...].astype(F32) + from_outer[...].astype(F32)
    out_q[...] = (query * factor).astype(BF16)
    for i, (out, scale) in enumerate(((out_k, factor), (out_v, 1.0))):
        others = near[i].astype(F32) + far[i].astype(F32)
        out[...] = (own_kv[i] * scale + others).astype(BF16)


def finish(first, count, head_width, full, parts, so_far):
    tile = parts[0].shape[0]
    wide = count * head_width
    one = pl.BlockSpec((tile, wide), lambda i: (0, 0))
    two = pl.BlockSpec((2, tile, wide), lambda i: (0, 0, 0))

    def part(array):
        offset = first * head_width if array.shape[2] > wide else 0
        return pl.BlockSpec(
            (pl.Element(2), pl.Element(tile), pl.Element(wide)), lambda i: (0, 0, offset)
        )

    cols = pl.BlockSpec(
        (pl.Element(tile), pl.Element(wide)), lambda i: (0, first * head_width)
    )
    kept = [] if so_far is None else list(so_far)
    return pl.pallas_call(
        functools.partial(finish_kernel, head_width**-0.5),
        grid=(1,),
        in_specs=[one, one, one, two, part(parts[4]), part(parts[5])] + [pl.BlockSpec(memory_space=pl.ANY)] * len(kept),
        out_specs=[cols] * 3,
        out_shape=[jax.ShapeDtypeStruct((tile, full), BF16)] * 3,
        input_output_aliases={6 + i: i for i in range(len(kept))},
        compiler_params=pltpu.CompilerParams(vmem_limit_bytes=VMEM_LIMIT),
        cost_estimate=pl.CostEstimate(
            flops=8 * tile * count * head_width,
            bytes_accessed=30 * tile * count * head_width,
            transcendentals=0,
        ),
        name="finish",
    )(*parts, *kept)


def after(value, *earlier):
    return lax.optimization_barrier((value, *earlier))[0]


def per_device(queries, keys, values, outputs, out_grads, log_sums, window_mask):
    tile, full = queries.shape[2:]
    heads = log_sums.shape[2]
    width = full // heads
    frames, rows = (lax.axis_size("tm"), lax.axis_size("space"))
    q, k, v, o, g = (a.reshape(tile, full) for a in (queries, keys, values, outputs, out_grads))
    partner = [(i, i ^ 1) for i in range(rows)]
    onward = [(i, (i + 2) % rows) for i in range(0, rows, 2)]
    onward += [(i, (i - 2) % rows) for i in range(1, rows, 2)]
    owners = [(0, 0), (rows - 1, rows - 1)]
    for i in range(1, rows - 1, 2):
        owners += [(i, i + 1), (i + 1, i)]
    near_pairs = [(i, i ^ 1) for i in range(frames)]
    far_pairs = [(0, 0), (frames - 1, frames - 1)]
    for i in range(1, frames - 1, 2):
        far_pairs += [(i, i + 1), (i + 1, i)]

    frame, row = (lax.axis_index("tm"), lax.axis_index("space"))
    far_frame = frame - 1 + 2 * lax.rem(frame, 2)
    has_far = ((far_frame >= 0) & (far_frame < frames)).astype(jnp.int32).reshape(1)
    place = (frame.reshape(1), row.reshape(1))

    firsts = [sum(CHUNKS[:c]) for c in range(len(CHUNKS))]
    lse = log_sums.reshape(heads, 1, tile)
    mask = window_mask.reshape(9)
    own_kv = pack(k, v)
    near_kv = lax.ppermute(own_kv, "tm", near_pairs)
    far_kv = lax.ppermute(own_kv, "tm", far_pairs)
    make = lambda first, counts, source: prep(
        first, counts, width, (frames, rows), place, mask, source, g, o, lse
    )
    mine = make(0, CHUNKS[:1], q)
    theirs = {0: lax.ppermute(mine[0], "space", partner)}
    mine += make(firsts[1], CHUNKS[1:], after(q, mine[0]))
    frames_kv = {HERE: own_kv, NEAR: near_kv, FAR: far_kv}
    last = len(CHUNKS) - 1
    outers = {}
    sums = [{} for _ in CHUNKS]
    backs = [{} for _ in CHUNKS]
    done = []
    out = None

    def stage(c, step, *awaited):
        messages = {OUTER: outers.get(c), OWN: mine[c], PARTNER: theirs.get(c)}
        stages = LATER_STAGES if c else STAGES
        work = stages[step]
        needed = {j: messages[j] for _, js in work for j in js}
        first_used = min(needed)
        arrived = [backs[i][name] for i, name in awaited]
        needed[first_used] = after(needed[first_used], *done[-1:], *arrived)
        later = {j for other in stages[step + 1 :] for _, js in other for j in js}
        slots = {slot for other in stages[step + 1 :] for slot, _ in other}
        final = {"q%d" % j for j in (OUTER, PARTNER) if j not in later}
        final |= {"kv%d" % slot for slot in (NEAR, FAR) if slot not in slots}
        joined = {}
        if c < last and step + 1 == len(stages):
            for name in JOINED:
                joined[name] = (firsts[last] * width, sums[c - 1][name] if c else None)
        sums[c] = run_stage(
            work, WEIGHTS[c][step], final, joined, firsts[c], CHUNKS[c], width, has_far, frames_kv, needed, sums[c]
        )
        done.append(sums[c]["kv0"])
        for name, axis, pairs in (
            ("q0", "space", owners),
            ("q2", "space", partner),
            ("kv1", "tm", near_pairs),
            ("kv2", "tm", far_pairs),
        ):
            if name not in final or name not in sums[c] or name in backs[c]:
                continue
            if name in joined and c + 1 < last:
                continue
            backs[c][name] = lax.ppermute(sums[c][name], axis, pairs)
            if name in joined:
                for earlier in range(c):
                    backs[earlier][name] = backs[c][name]

    def hand_on(c):
        outers[c] = lax.ppermute(after(theirs[c], *done[-1:]), "space", onward)

    def complete(c, so_far):
        back = backs[c]
        own = after(sums[c]["q1"], *done[-1:])
        so_far = finish(
            firsts[c], CHUNKS[c], width, full,
            (own, back["q2"], back["q0"], sums[c]["kv0"], back["kv1"], back["kv2"]), so_far,
        )
        done.append(so_far[0])
        return so_far

    for c in range(1, len(CHUNKS)):
        theirs[c] = lax.ppermute(mine[c], "space", partner)
    for kind, c, *rest in ORDER:
        if kind == "stage":
            stage(c, *rest)
        elif kind == "hand":
            hand_on(c)
        else:
            out = complete(c, out)
    return tuple(a.reshape(queries.shape) for a in out)


def solution(mesh):
    tile = P("tm", "space", None, None)
    return jax.shard_map(
        per_device,
        mesh=mesh,
        in_specs=(tile,) * 6 + (P("tm", "space", None),),
        out_specs=(tile,) * 3,
        check_vma=False,
    )
```

```python
import functools
import math

import jax
import jax.numpy as jnp
from jax import lax
from jax.experimental import pallas as pl
from jax.experimental.pallas import tpu as pltpu
from jax.sharding import PartitionSpec as P

F32 = jnp.float32
BF16 = jnp.bfloat16
FAR_AWAY = 1e30

OUTER, OWN, PARTNER = (0, 1, 2)
HERE, NEAR, FAR = (0, 1, 2)
CHUNKS = (4, 4, 4)
STAGES = (
    ((HERE, (OWN,)), (NEAR, (OWN,))),
    ((HERE, (PARTNER,)), (NEAR, (PARTNER,))),
    ((HERE, (OUTER,)), (NEAR, (OUTER,)), (FAR, (OWN, PARTNER, OUTER))),
)
LATER_STAGES = (
    STAGES[0],
    STAGES[1] + ((FAR, (PARTNER,)),),
    ((HERE, (OUTER,)), (NEAR, (OUTER,)), (FAR, (OWN, OUTER))),
)
ORDER = (('stage', 0, 0), ('stage', 1, 0), ('hand', 0), ('stage', 0, 1), ('stage', 2, 0), ('hand', 1), ('stage', 1, 1), ('stage', 0, 2), ('hand', 2), ('stage', 2, 1), ('stage', 1, 2, (0, 'q0')), ('stage', 2, 2, (1, 'q2'), (0, 'kv1')), ('finish', 0), ('finish', 1), ('finish', 2))
JOINED = ('kv2',)
WEIGHTS = ((20, 160, 40), (10, 448, 20), (224, 4, 80))
EXTRA = 32
VMEM_LIMIT = 20 * 1024 * 1024
GROUP = 1


def dot(a, b, dims):
    return lax.dot_general(a, b, (dims, ((), ())), preferred_element_type=F32)


def three_terms(row):
    terms = []
    for _ in range(3):
        term = row.astype(BF16).astype(F32)
        terms.append(term)
        row = row - term
    return terms


def fold(row):
    lanes = 128
    return [row[:, i : i + lanes] for i in range(0, row.shape[1], lanes)]


def flag_row(frames, rows, frame, row, mask_ref, lanes):
    toward = 1 - 2 * lax.rem(row, 2)
    near = 1 - 2 * lax.rem(frame, 2)
    lane = lax.broadcasted_iota(jnp.int32, (1, lanes), 1)
    flags = jnp.zeros((1, lanes), F32)
    for role in (OUTER, OWN, PARTNER):
        for slot in (HERE, NEAR, FAR):
            row_off = (role - 1) * toward
            frame_off = (0, near, -near)[slot]
            inside = (
                (row + row_off >= 0)
                & (row + row_off < rows)
                & (frame + frame_off >= 0)
                & (frame + frame_off < frames)
            )
            index = 3 * (frame_off + 1) + row_off + 1
            on = inside & ((mask_ref[index] > 0) | (index == 4))
            flags = jnp.where(lane == 3 * role + slot, on.astype(F32), flags)
    return flags


def prep_kernel(
    counts, frames, rows, frame_ref, row_ref, mask_ref, q_ref, g_ref, o_ref, lse_ref, *outs
):
    tile = q_ref.shape[0]
    width = q_ref.shape[1] // sum(counts)
    flags = flag_row(frames, rows, frame_ref[0], row_ref[0], mask_ref, width)
    ones = jnp.ones((8, width), BF16)
    head = 0
    for out, count in zip(outs, counts):
        for h in range(count):
            source = slice(head * width, (head + 1) * width)
            cols = slice(h * width, (h + 1) * width)
            grad = g_ref[:, source]
            out[0:tile, cols] = q_ref[:, source]
            out[tile : 2 * tile, cols] = grad
            prod = grad.astype(F32) * o_ref[:, source].astype(F32)
            high = prod.astype(BF16)
            low = (prod - high.astype(F32)).astype(BF16)
            delta = dot(ones, high, ((1,), (1,))) + dot(ones, low, ((1,), (1,)))
            lines = []
            for line in (lse_ref[head], delta[0:1, :]):
                for term in three_terms(line):
                    lines += fold(term)
            lines.append(flags)
            lines.append(jnp.zeros((EXTRA - len(lines), width), F32))
            extra = jnp.concatenate(lines, axis=0).astype(BF16)
            out[2 * tile : 2 * tile + EXTRA, cols] = extra
            head += 1


def prep(first, counts, head_width, sizes, place, mask, q, g, o, lse):
    tile, full = q.shape
    count = sum(counts)
    offset = first * head_width
    cols = pl.BlockSpec(
        (pl.Element(tile), pl.Element(count * head_width)), lambda i, *_: (0, offset)
    )
    shapes = [(2 * tile + EXTRA, n * head_width) for n in counts]
    return pl.pallas_call(
        functools.partial(prep_kernel, counts, *sizes),
        grid_spec=pltpu.PrefetchScalarGridSpec(
            num_scalar_prefetch=3,
            grid=(1,),
            in_specs=[
                cols,
                cols,
                cols,
                pl.BlockSpec(
                    (pl.Element(count), pl.Element(1), pl.Element(tile)),
                    lambda i, *_: (first, 0, 0),
                ),
            ],
            out_specs=[pl.BlockSpec(shape, lambda i, *_: (0, 0)) for shape in shapes],
        ),
        out_shape=[jax.ShapeDtypeStruct(shape, BF16) for shape in shapes],
        compiler_params=pltpu.CompilerParams(vmem_limit_bytes=VMEM_LIMIT),
        cost_estimate=pl.CostEstimate(
            flops=2 * tile * count * head_width,
            bytes_accessed=10 * tile * count * head_width,
            transcendentals=0,
        ),
        name="prep",
    )(*place, mask, *(pltpu.with_memory_space_constraint(a, pltpu.HBM) for a in (q, g, o)), lse)


def pack_kernel(k_ref, v_ref, out):
    out[0] = k_ref[...]
    out[1] = v_ref[...]


def pack(k, v, steps=2):
    tile, full = k.shape
    cols = pl.BlockSpec((tile, full // steps), lambda i: (0, i))
    return pl.pallas_call(
        pack_kernel,
        grid=(steps,),
        in_specs=[cols, cols],
        out_specs=pl.BlockSpec((2, tile, full // steps), lambda i: (0, 0, i)),
        out_shape=jax.ShapeDtypeStruct((2, tile, full), k.dtype),
        compiler_params=pltpu.CompilerParams(vmem_limit_bytes=VMEM_LIMIT),
        cost_estimate=pl.CostEstimate(flops=0, bytes_accessed=8 * k.size, transcendentals=0),
        name="pack",
    )(*(pltpu.with_memory_space_constraint(a, pltpu.HBM) for a in (k, v)))


def row_stats(message, tile):
    extra = message[2 * tile : 2 * tile + EXTRA, :].astype(F32)
    parts = tile // 128
    rows = []
    for base in (0, 3 * parts):
        pieces = []
        for p in range(parts):
            a, b, c = (extra[base + i * parts + p : base + i * parts + p + 1] for i in range(3))
            pieces.append(a + b + c)
        rows.append(jnp.concatenate(pieces, axis=1))
    return (rows[0], rows[1], extra[6 * parts : 6 * parts + 1])


def stage_kernel(work, names, closing, last, factor, group, far_ref, *refs):
    env = dict(zip(names, refs))
    tile, wide = env["message%d" % work[0][1][0]].shape
    tile = (tile - EXTRA) // 2
    width = wide // group
    heads = [slice(i * width, (i + 1) * width) for i in range(group)]
    used = sorted({j for _, js in work for j in js})
    stats = {
        (j, i): row_stats(env["message%d" % j].at[:, cols], tile)
        for j in used
        for i, cols in enumerate(heads)
    }
    started = set()

    def add_q(j, i, term):
        name, cols = ("q%d" % j, heads[i])
        if (j, i) in started:
            env["sum_" + name][cols, :] += term
        elif "acc_" + name in env:
            env["sum_" + name][cols, :] = env["acc_" + name][cols, :] + term
        else:
            env["sum_" + name][cols, :] = term
        started.add((j, i))

    def pair_terms(slot, j, i):
        cols = heads[i]
        message, keys = (env["message%d" % j], env["keys%d" % slot])
        queries, grads = (message[0:tile, cols], message[tile : 2 * tile, cols])
        key, value = (keys[0, :, cols], keys[1, :, cols])
        shift, delta, flags = stats[j, i]
        lane = 3 * j + slot
        shift = jnp.where(flags[:, lane : lane + 1] > 0, shift, FAR_AWAY)
        scores = dot(key, queries, ((1,), (1,)))
        weights = jnp.exp(scores * factor - shift)
        grad_prob = dot(value, grads, ((1,), (1,)))
        grad_score = (weights * (grad_prob - delta)).astype(BF16)
        add_q(j, i, dot(key, grad_score, ((0,), (0,))))
        return (
            dot(grad_score, queries, ((1,), (0,))),
            dot(weights.astype(BF16), grads, ((1,), (0,))),
        )

    def key_frames(slots_js):
        for slot, js in slots_js:
            name = "kv%d" % slot
            out = env["out_" + name]
            for i, cols in enumerate(heads):
                dk, dv = pair_terms(slot, js[0], i)
                for j in js[1:]:
                    more_k, more_v = pair_terms(slot, j, i)
                    dk, dv = (dk + more_k, dv + more_v)
                if "acc_" + name in env:
                    acc = env["acc_" + name]
                    dk, dv = (dk + acc[0, :, cols], dv + acc[1, :, cols])
                out[0, :, cols] = (dk * factor if name in last else dk).astype(out.dtype)
                out[1, :, cols] = dv.astype(out.dtype)

    key_frames([(slot, js) for slot, js in work if slot != FAR])
    for slot, js in work:
        if slot == FAR:
            fresh = [j for j in js if (j, 0) not in started]
            pl.when(far_ref[0] > 0)(functools.partial(key_frames, [(slot, js)]))

            @pl.when(far_ref[0] == 0)
            def _():
                out = env["out_kv%d" % FAR]
                out[...] = jnp.zeros_like(out)
                for j in fresh:
                    name = "q%d" % j
                    env["sum_" + name][...] = env["acc_" + name][...]

    for j in used:
        out = env["out_q%d" % j]
        total = env["sum_q%d" % j][...]
        out[...] = (total.T if "q%d" % j in closing else total).astype(out.dtype)


def run_stage(work, weight, closing, last, joined, first, count, head_width, far, keys, messages, sums):
    rows, wide = next(iter(messages.values())).shape
    tile = (rows - EXTRA) // 2
    group = math.gcd(count, GROUP) if first % math.gcd(count, GROUP) == 0 else 1
    step, begin = (group * head_width, first // group)
    one = pl.BlockSpec((tile, step), lambda h, *_: (0, h))
    turned = pl.BlockSpec((step, tile), lambda h, *_: (h, 0))
    two = pl.BlockSpec((2, tile, step), lambda h, *_: (0, 0, h))
    cols = pl.BlockSpec((2, tile, step), lambda h, *_: (0, 0, h + begin))
    whole = pl.BlockSpec((rows, step), lambda h, *_: (0, h))
    used = sorted({j for _, js in work for j in js})
    slots = [slot for slot, _ in work]
    names, args, specs = ([], [], [])

    def give(name, arg, spec):
        names.append(name)
        args.append(arg)
        specs.append(spec)

    for j in used:
        give("message%d" % j, messages[j], whole)
    for slot in slots:
        give("keys%d" % slot, keys[slot], cols)
    touched = [("q%d" % j, one) for j in used] + [("kv%d" % s, two) for s in slots]
    for name, spec in touched:
        if name in sums:
            give("acc_" + name, sums[name], turned if spec is one else spec)
    out_specs, out_shapes, aliases = ([], [], {})
    for name, spec in touched:
        shape = (tile, wide) if spec is one else (2, tile, wide)
        if spec is one and name not in closing:
            spec, shape = (turned, (wide, tile))
        if name in last and name in joined:
            total, begun = joined[name]
            spec = cols
            shape = (2, tile, total)
            if begun is not None:
                aliases[1 + len(args)] = len(out_specs)
                give("begun_" + name, begun, pl.BlockSpec(memory_space=pl.ANY))
        out_specs.append(spec)
        out_shapes.append(jax.ShapeDtypeStruct(shape, BF16 if name in last else F32))
    names += ["out_" + name for name, _ in touched]
    names += ["sum_q%d" % j for j in used]
    pairs = count * sum(len(js) for _, js in work)
    results = pl.pallas_call(
        functools.partial(stage_kernel, work, names, closing, last, head_width**-0.5, group),
        grid_spec=pltpu.PrefetchScalarGridSpec(
            num_scalar_prefetch=1,
            grid=(count // group,),
            in_specs=specs,
            out_specs=out_specs,
            scratch_shapes=[pltpu.VMEM((step, tile), F32)] * len(used),
        ),
        out_shape=out_shapes,
        input_output_aliases=aliases,
        compiler_params=pltpu.CompilerParams(vmem_limit_bytes=VMEM_LIMIT),
        cost_estimate=pl.CostEstimate(
            flops=weight * pairs * tile * tile * head_width,
            bytes_accessed=20 * tile * wide,
            transcendentals=0,
        ),
        name="pairs",
    )(far, *args)
    return {**sums, **{name: value for (name, _), value in zip(touched, results)}}


def finish_kernel(factor, own_q, from_partner, from_outer, own_kv, near, far, *rest):
    out_q, out_k, out_v = rest[-3:]
    query = own_q[...] + from_partner[...].astype(F32) + from_outer[...].astype(F32)
    out_q[...] = (query * factor).astype(BF16)
    for i, (out, scale) in enumerate(((out_k, factor), (out_v, 1.0))):
        others = near[i].astype(F32) + far[i].astype(F32)
        out[...] = (own_kv[i] * scale + others).astype(BF16)


def finish(first, count, head_width, full, parts, so_far):
    tile = parts[0].shape[0]
    wide = count * head_width
    one = pl.BlockSpec((tile, wide), lambda i: (0, 0))
    two = pl.BlockSpec((2, tile, wide), lambda i: (0, 0, 0))

    def part(array):
        offset = first * head_width if array.shape[2] > wide else 0
        return pl.BlockSpec(
            (pl.Element(2), pl.Element(tile), pl.Element(wide)), lambda i: (0, 0, offset)
        )

    cols = pl.BlockSpec(
        (pl.Element(tile), pl.Element(wide)), lambda i: (0, first * head_width)
    )
    kept = [] if so_far is None else list(so_far)
    return pl.pallas_call(
        functools.partial(finish_kernel, head_width**-0.5),
        grid=(1,),
        in_specs=[one, one, one, two, part(parts[4]), part(parts[5])] + [pl.BlockSpec(memory_space=pl.ANY)] * len(kept),
        out_specs=[cols] * 3,
        out_shape=[jax.ShapeDtypeStruct((tile, full), BF16)] * 3,
        input_output_aliases={6 + i: i for i in range(len(kept))},
        compiler_params=pltpu.CompilerParams(vmem_limit_bytes=VMEM_LIMIT),
        cost_estimate=pl.CostEstimate(
            flops=8 * tile * count * head_width,
            bytes_accessed=30 * tile * count * head_width,
            transcendentals=0,
        ),
        name="finish",
    )(*parts, *kept)


def after(value, *earlier):
    return lax.optimization_barrier((value, *earlier))[0]


def per_device(queries, keys, values, outputs, out_grads, log_sums, window_mask):
    tile, full = queries.shape[2:]
    heads = log_sums.shape[2]
    width = full // heads
    frames, rows = (lax.axis_size("tm"), lax.axis_size("space"))
    q, k, v, o, g = (a.reshape(tile, full) for a in (queries, keys, values, outputs, out_grads))
    partner = [(i, i ^ 1) for i in range(rows)]
    onward = [(i, (i + 2) % rows) for i in range(0, rows, 2)]
    onward += [(i, (i - 2) % rows) for i in range(1, rows, 2)]
    owners = [(0, 0), (rows - 1, rows - 1)]
    for i in range(1, rows - 1, 2):
        owners += [(i, i + 1), (i + 1, i)]
    near_pairs = [(i, i ^ 1) for i in range(frames)]
    far_pairs = [(0, 0), (frames - 1, frames - 1)]
    for i in range(1, frames - 1, 2):
        far_pairs += [(i, i + 1), (i + 1, i)]

    frame, row = (lax.axis_index("tm"), lax.axis_index("space"))
    far_frame = frame - 1 + 2 * lax.rem(frame, 2)
    has_far = ((far_frame >= 0) & (far_frame < frames)).astype(jnp.int32).reshape(1)
    place = (frame.reshape(1), row.reshape(1))

    firsts = [sum(CHUNKS[:c]) for c in range(len(CHUNKS))]
    lse = log_sums.reshape(heads, 1, tile)
    mask = window_mask.reshape(9)
    own_kv = pack(k, v)
    near_kv = lax.ppermute(own_kv, "tm", near_pairs)
    far_kv = lax.ppermute(own_kv, "tm", far_pairs)
    make = lambda first, counts, source: prep(
        first, counts, width, (frames, rows), place, mask, source, g, o, lse
    )
    mine = make(0, CHUNKS[:1], q)
    theirs = {0: lax.ppermute(mine[0], "space", partner)}
    mine += make(firsts[1], CHUNKS[1:], after(q, mine[0]))
    frames_kv = {HERE: own_kv, NEAR: near_kv, FAR: far_kv}
    last = len(CHUNKS) - 1
    outers = {}
    sums = [{} for _ in CHUNKS]
    backs = [{} for _ in CHUNKS]
    done = []
    out = None

    def stage(c, step, *awaited):
        messages = {OUTER: outers.get(c), OWN: mine[c], PARTNER: theirs.get(c)}
        stages = LATER_STAGES if c else STAGES
        work = stages[step]
        needed = {j: messages[j] for _, js in work for j in js}
        first_used = min(needed)
        arrived = [backs[i][name] for i, name in awaited]
        needed[first_used] = after(needed[first_used], *done[-1:], *arrived)
        later = {j for other in stages[step + 1 :] for _, js in other for j in js}
        slots = {slot for other in stages[step + 1 :] for slot, _ in other}
        closing = {"q%d" % j for j in (OUTER, OWN, PARTNER) if j not in later}
        final = closing - {"q%d" % OWN}
        final |= {"kv%d" % slot for slot in (NEAR, FAR) if slot not in slots}
        joined = {}
        if c < last and step + 1 == len(stages):
            for name in JOINED:
                joined[name] = (firsts[last] * width, sums[c - 1][name] if c else None)
        sums[c] = run_stage(
            work, WEIGHTS[c][step], closing, final, joined, firsts[c], CHUNKS[c], width, has_far, frames_kv, needed, sums[c]
        )
        done.append(sums[c]["kv0"])
        for name, axis, pairs in (
            ("q0", "space", owners),
            ("q2", "space", partner),
            ("kv1", "tm", near_pairs),
            ("kv2", "tm", far_pairs),
        ):
            if name not in final or name not in sums[c] or name in backs[c]:
                continue
            if name in joined and c + 1 < last:
                continue
            backs[c][name] = lax.ppermute(sums[c][name], axis, pairs)
            if name in joined:
                for earlier in range(c):
                    backs[earlier][name] = backs[c][name]

    def hand_on(c):
        outers[c] = lax.ppermute(after(theirs[c], *done[-1:]), "space", onward)

    def complete(c, so_far):
        back = backs[c]
        own = after(sums[c]["q1"], *done[-1:])
        so_far = finish(
            firsts[c], CHUNKS[c], width, full,
            (own, back["q2"], back["q0"], sums[c]["kv0"], back["kv1"], back["kv2"]), so_far,
        )
        done.append(so_far[0])
        return so_far

    for c in range(1, len(CHUNKS)):
        theirs[c] = lax.ppermute(mine[c], "space", partner)
    for kind, c, *rest in ORDER:
        if kind == "stage":
            stage(c, *rest)
        elif kind == "hand":
            hand_on(c)
        else:
            out = complete(c, out)
    return tuple(a.reshape(queries.shape) for a in out)


def solution(mesh):
    tile = P("tm", "space", None, None)
    return jax.shard_map(
        per_device,
        mesh=mesh,
        in_specs=(tile,) * 6 + (P("tm", "space", None),),
        out_specs=(tile,) * 3,
        check_vma=False,
    )
```

```python
import functools
import math

import jax
import jax.numpy as jnp
from jax import lax
from jax.experimental import pallas as pl
from jax.experimental.pallas import tpu as pltpu
from jax.sharding import PartitionSpec as P

F32 = jnp.float32
BF16 = jnp.bfloat16
FAR_AWAY = 1e30

OUTER, OWN, PARTNER = (0, 1, 2)
HERE, NEAR, FAR = (0, 1, 2)
CHUNKS = (4, 5, 3)
STAGES = (
    ((HERE, (OWN,)), (NEAR, (OWN,))),
    ((HERE, (PARTNER,)), (NEAR, (PARTNER,))),
    ((HERE, (OUTER,)), (NEAR, (OUTER,)), (FAR, (OWN, PARTNER, OUTER))),
)
LATER_STAGES = (
    STAGES[0],
    STAGES[1] + ((FAR, (PARTNER,)),),
    ((HERE, (OUTER,)), (NEAR, (OUTER,)), (FAR, (OWN, OUTER))),
)
ORDER = (('stage', 0, 0), ('stage', 1, 0), ('hand', 0), ('stage', 0, 1), ('stage', 2, 0), ('hand', 1), ('stage', 0, 2), ('hand', 2), ('stage', 1, 1), ('back', 0), ('stage', 1, 2), ('stage', 2, 1), ('back', 1), ('stage', 2, 2, (0, 'q2'), (0, 'kv1')), ('finish', 0), ('finish', 1), ('finish', 2))
JOINED = ('kv2',)
WEIGHTS = ((60, 60, 60), (60, 30, 60), (240, 120, 60))
EXTRA = 32
VMEM_LIMIT = 20 * 1024 * 1024
GROUP = 1


def dot(a, b, dims):
    return lax.dot_general(a, b, (dims, ((), ())), preferred_element_type=F32)


def three_terms(row):
    terms = []
    for _ in range(3):
        term = row.astype(BF16).astype(F32)
        terms.append(term)
        row = row - term
    return terms


def fold(row):
    lanes = 128
    return [row[:, i : i + lanes] for i in range(0, row.shape[1], lanes)]


def flag_row(frames, rows, frame, row, mask_ref, lanes):
    toward = 1 - 2 * lax.rem(row, 2)
    near = 1 - 2 * lax.rem(frame, 2)
    lane = lax.broadcasted_iota(jnp.int32, (1, lanes), 1)
    flags = jnp.zeros((1, lanes), F32)
    for role in (OUTER, OWN, PARTNER):
        for slot in (HERE, NEAR, FAR):
            row_off = (role - 1) * toward
            frame_off = (0, near, -near)[slot]
            inside = (
                (row + row_off >= 0)
                & (row + row_off < rows)
                & (frame + frame_off >= 0)
                & (frame + frame_off < frames)
            )
            index = 3 * (frame_off + 1) + row_off + 1
            on = inside & ((mask_ref[index] > 0) | (index == 4))
            flags = jnp.where(lane == 3 * role + slot, on.astype(F32), flags)
    return flags


def prep_kernel(
    counts, frames, rows, frame_ref, row_ref, mask_ref, q_ref, g_ref, o_ref, lse_ref, *outs
):
    tile = q_ref.shape[0]
    width = q_ref.shape[1] // sum(counts)
    flags = flag_row(frames, rows, frame_ref[0], row_ref[0], mask_ref, width)
    ones = jnp.ones((8, width), BF16)
    head = 0
    for out, count in zip(outs, counts):
        for h in range(count):
            source = slice(head * width, (head + 1) * width)
            cols = slice(h * width, (h + 1) * width)
            grad = g_ref[:, source]
            out[0:tile, cols] = q_ref[:, source]
            out[tile : 2 * tile, cols] = grad
            prod = grad.astype(F32) * o_ref[:, source].astype(F32)
            high = prod.astype(BF16)
            low = (prod - high.astype(F32)).astype(BF16)
            delta = dot(ones, high, ((1,), (1,))) + dot(ones, low, ((1,), (1,)))
            lines = []
            for line in (lse_ref[head], delta[0:1, :]):
                for term in three_terms(line):
                    lines += fold(term)
            lines.append(flags)
            lines.append(jnp.zeros((EXTRA - len(lines), width), F32))
            extra = jnp.concatenate(lines, axis=0).astype(BF16)
            out[2 * tile : 2 * tile + EXTRA, cols] = extra
            head += 1


def prep(first, counts, head_width, sizes, place, mask, q, g, o, lse):
    tile, full = q.shape
    count = sum(counts)
    offset = first * head_width
    cols = pl.BlockSpec(
        (pl.Element(tile), pl.Element(count * head_width)), lambda i, *_: (0, offset)
    )
    shapes = [(2 * tile + EXTRA, n * head_width) for n in counts]
    return pl.pallas_call(
        functools.partial(prep_kernel, counts, *sizes),
        grid_spec=pltpu.PrefetchScalarGridSpec(
            num_scalar_prefetch=3,
            grid=(1,),
            in_specs=[
                cols,
                cols,
                cols,
                pl.BlockSpec(
                    (pl.Element(count), pl.Element(1), pl.Element(tile)),
                    lambda i, *_: (first, 0, 0),
                ),
            ],
            out_specs=[pl.BlockSpec(shape, lambda i, *_: (0, 0)) for shape in shapes],
        ),
        out_shape=[jax.ShapeDtypeStruct(shape, BF16) for shape in shapes],
        compiler_params=pltpu.CompilerParams(vmem_limit_bytes=VMEM_LIMIT),
        cost_estimate=pl.CostEstimate(
            flops=2 * tile * count * head_width,
            bytes_accessed=10 * tile * count * head_width,
            transcendentals=0,
        ),
        name="prep",
    )(*place, mask, *(pltpu.with_memory_space_constraint(a, pltpu.HBM) for a in (q, g, o)), lse)


def pack_kernel(k_ref, v_ref, out):
    out[0] = k_ref[...]
    out[1] = v_ref[...]


def pack(k, v, steps=2):
    tile, full = k.shape
    cols = pl.BlockSpec((tile, full // steps), lambda i: (0, i))
    return pl.pallas_call(
        pack_kernel,
        grid=(steps,),
        in_specs=[cols, cols],
        out_specs=pl.BlockSpec((2, tile, full // steps), lambda i: (0, 0, i)),
        out_shape=jax.ShapeDtypeStruct((2, tile, full), k.dtype),
        compiler_params=pltpu.CompilerParams(vmem_limit_bytes=VMEM_LIMIT),
        cost_estimate=pl.CostEstimate(flops=0, bytes_accessed=8 * k.size, transcendentals=0),
        name="pack",
    )(*(pltpu.with_memory_space_constraint(a, pltpu.HBM) for a in (k, v)))


def row_stats(message, tile):
    extra = message[2 * tile : 2 * tile + EXTRA, :].astype(F32)
    parts = tile // 128
    rows = []
    for base in (0, 3 * parts):
        pieces = []
        for p in range(parts):
            a, b, c = (extra[base + i * parts + p : base + i * parts + p + 1] for i in range(3))
            pieces.append(a + b + c)
        rows.append(jnp.concatenate(pieces, axis=1))
    return (rows[0], rows[1], extra[6 * parts : 6 * parts + 1])


def stage_kernel(work, names, carried, last, factor, group, far_ref, *refs):
    env = dict(zip(names, refs))
    tile, wide = env["message%d" % work[0][1][0]].shape
    tile = (tile - EXTRA) // 2
    width = wide // group
    heads = [slice(i * width, (i + 1) * width) for i in range(group)]
    used = sorted({j for _, js in work for j in js})
    stats = {
        (j, i): row_stats(env["message%d" % j].at[:, cols], tile)
        for j in used
        for i, cols in enumerate(heads)
    }
    started = set()

    def add_q(j, i, term):
        name, cols = ("q%d" % j, heads[i])
        if (j, i) in started:
            env["sum_" + name][:, cols] += term
        elif "acc_" + name in env:
            env["sum_" + name][:, cols] = env["acc_" + name][:, cols] + term
        else:
            env["sum_" + name][:, cols] = term
        started.add((j, i))

    def pair_terms(slots, j, i):
        cols = heads[i]
        message = env["message%d" % j]
        queries, grads = (message[0:tile, cols], message[tile : 2 * tile, cols])
        stack = lambda parts: jnp.concatenate(parts, axis=0) if len(parts) > 1 else parts[0]
        key, value = (stack([env["keys%d" % slot][n, :, cols] for slot in slots]) for n in (0, 1))
        scores = dot(key, queries, ((1,), (1,)))
        grad_prob = dot(value, grads, ((1,), (1,)))
        shift, delta, flags = stats[j, i]
        grad_scores, probs = ([], [])
        for n, slot in enumerate(slots):
            lane = 3 * j + slot
            rows = slice(n * tile, (n + 1) * tile)
            far_off = jnp.where(flags[:, lane : lane + 1] > 0, shift, FAR_AWAY)
            weights = jnp.exp(scores[rows] * factor - far_off)
            probs.append(weights.astype(BF16))
            grad_scores.append((weights * (grad_prob[rows] - delta)).astype(BF16))
        grad_score = stack(grad_scores)
        add_q(j, i, dot(grad_score, key, ((0,), (0,))))
        return (
            dot(grad_score, queries, ((1,), (0,))),
            dot(stack(probs), grads, ((1,), (0,))),
        )

    def key_frames(slots, js):
        for i, cols in enumerate(heads):
            dk, dv = pair_terms(slots, js[0], i)
            for j in js[1:]:
                more_k, more_v = pair_terms(slots, j, i)
                dk, dv = (dk + more_k, dv + more_v)
            for n, slot in enumerate(slots):
                name = "kv%d" % slot
                out = env["out_" + name]
                rows = slice(n * tile, (n + 1) * tile)
                slot_k, slot_v = (dk[rows], dv[rows])
                if "acc_" + name in env:
                    acc = env["acc_" + name]
                    slot_k, slot_v = (slot_k + acc[0, :, cols], slot_v + acc[1, :, cols])
                out[0, :, cols] = (slot_k * factor if name in last else slot_k).astype(out.dtype)
                out[1, :, cols] = slot_v.astype(out.dtype)

    key_frames([slot for slot, _ in work if slot != FAR], work[0][1])
    for slot, js in work:
        if slot == FAR:
            fresh = [j for j in js if (j, 0) not in started]
            pl.when(far_ref[0] > 0)(functools.partial(key_frames, [slot], js))

            @pl.when(far_ref[0] == 0)
            def _():
                out = env["out_kv%d" % FAR]
                out[...] = jnp.zeros_like(out)
                for j in fresh:
                    name = "q%d" % j
                    env["sum_" + name][...] = env["acc_" + name][...]

    for j in used:
        out = env["out_q%d" % j]
        out[...] = (env["sum_q%d" % j][...]).astype(out.dtype)


def run_stage(work, weight, last, joined, first, count, head_width, far, keys, messages, sums):
    rows, wide = next(iter(messages.values())).shape
    tile = (rows - EXTRA) // 2
    group = math.gcd(count, GROUP) if first % math.gcd(count, GROUP) == 0 else 1
    step, begin = (group * head_width, first // group)
    one = pl.BlockSpec((tile, step), lambda h, *_: (0, h))
    two = pl.BlockSpec((2, tile, step), lambda h, *_: (0, 0, h))
    cols = pl.BlockSpec((2, tile, step), lambda h, *_: (0, 0, h + begin))
    whole = pl.BlockSpec((rows, step), lambda h, *_: (0, h))
    used = sorted({j for _, js in work for j in js})
    slots = [slot for slot, _ in work]
    names, args, specs = ([], [], [])

    def give(name, arg, spec):
        names.append(name)
        args.append(arg)
        specs.append(spec)

    for j in used:
        give("message%d" % j, messages[j], whole)
    for slot in slots:
        give("keys%d" % slot, keys[slot], cols)
    touched = [("q%d" % j, one) for j in used] + [("kv%d" % s, two) for s in slots]
    carried = [name for name, _ in touched if name in sums]
    for name, spec in touched:
        if name in sums:
            give("acc_" + name, sums[name], spec)
    out_specs, out_shapes, aliases = ([], [], {})
    for name, spec in touched:
        shape = (tile, wide) if name.startswith("q") else (2, tile, wide)
        if name in last and name in joined:
            total, begun = joined[name]
            spec = cols
            shape = (2, tile, total)
            if begun is not None:
                aliases[1 + len(args)] = len(out_specs)
                give("begun_" + name, begun, pl.BlockSpec(memory_space=pl.ANY))
        out_specs.append(spec)
        out_shapes.append(jax.ShapeDtypeStruct(shape, BF16 if name in last else F32))
    names += ["out_" + name for name, _ in touched]
    names += ["sum_q%d" % j for j in used]
    pairs = count * sum(len(js) for _, js in work)
    results = pl.pallas_call(
        functools.partial(stage_kernel, work, names, carried, last, head_width**-0.5, group),
        grid_spec=pltpu.PrefetchScalarGridSpec(
            num_scalar_prefetch=1,
            grid=(count // group,),
            in_specs=specs,
            out_specs=out_specs,
            scratch_shapes=[pltpu.VMEM((tile, step), F32)] * len(used),
        ),
        out_shape=out_shapes,
        input_output_aliases=aliases,
        compiler_params=pltpu.CompilerParams(vmem_limit_bytes=VMEM_LIMIT),
        cost_estimate=pl.CostEstimate(
            flops=weight * pairs * tile * tile * head_width,
            bytes_accessed=20 * tile * wide,
            transcendentals=0,
        ),
        name="pairs",
    )(far, *args)
    return {**sums, **{name: value for (name, _), value in zip(touched, results)}}


def finish_kernel(factor, backs, own_kv, near, far, own_q, *rest):
    out_q, out_k, out_v = rest[-3:]
    total = own_q[...]
    for back in rest[:backs]:
        total = total + back[...].astype(F32)
    out_q[...] = (total * factor).astype(BF16)
    for i, (out, scale) in enumerate(((out_k, factor), (out_v, 1.0))):
        others = near[i].astype(F32) + far[i].astype(F32)
        out[...] = (own_kv[i] * scale + others).astype(BF16)


def finish(first, count, head_width, full, parts, so_far):
    tile = parts[0].shape[1]
    wide = count * head_width
    one = pl.BlockSpec((tile, wide), lambda i: (0, 0))
    two = pl.BlockSpec((2, tile, wide), lambda i: (0, 0, 0))

    def part(array):
        offset = first * head_width if array.shape[2] > wide else 0
        return pl.BlockSpec(
            (pl.Element(2), pl.Element(tile), pl.Element(wide)), lambda i: (0, 0, offset)
        )

    cols = pl.BlockSpec(
        (pl.Element(tile), pl.Element(wide)), lambda i: (0, first * head_width)
    )
    kept = [] if so_far is None else list(so_far)
    return pl.pallas_call(
        functools.partial(finish_kernel, head_width**-0.5, len(parts) - 4),
        grid=(1,),
        in_specs=[two, part(parts[1]), part(parts[2])] + [one] * (len(parts) - 3) + [pl.BlockSpec(memory_space=pl.ANY)] * len(kept),
        out_specs=[cols] * 3,
        out_shape=[jax.ShapeDtypeStruct((tile, full), BF16)] * 3,
        input_output_aliases={len(parts) + i: i for i in range(len(kept))},
        compiler_params=pltpu.CompilerParams(vmem_limit_bytes=VMEM_LIMIT),
        cost_estimate=pl.CostEstimate(
            flops=8 * tile * count * head_width,
            bytes_accessed=30 * tile * count * head_width,
            transcendentals=0,
        ),
        name="finish",
    )(*parts, *kept)


def after(value, *earlier):
    return lax.optimization_barrier((value, *earlier))[0]


def per_device(queries, keys, values, outputs, out_grads, log_sums, window_mask):
    tile, full = queries.shape[2:]
    heads = log_sums.shape[2]
    width = full // heads
    frames, rows = (lax.axis_size("tm"), lax.axis_size("space"))
    q, k, v, o, g = (a.reshape(tile, full) for a in (queries, keys, values, outputs, out_grads))
    partner = [(i, i ^ 1) for i in range(rows)]
    onward = [(i, (i + 2) % rows) for i in range(0, rows, 2)]
    onward += [(i, (i - 2) % rows) for i in range(1, rows, 2)]
    homeward = [(i + 2, i) for i in range(0, rows - 2, 2)]
    homeward += [(i, i + 2) for i in range(1, rows - 2, 2)]
    homeward += [(0, 1), (rows - 1, rows - 2)]
    owners = [(0, 0), (rows - 1, rows - 1)]
    for i in range(1, rows - 1, 2):
        owners += [(i, i + 1), (i + 1, i)]
    near_pairs = [(i, i ^ 1) for i in range(frames)]
    far_pairs = [(0, 0), (frames - 1, frames - 1)]
    for i in range(1, frames - 1, 2):
        far_pairs += [(i, i + 1), (i + 1, i)]

    frame, row = (lax.axis_index("tm"), lax.axis_index("space"))
    far_frame = frame - 1 + 2 * lax.rem(frame, 2)
    has_far = ((far_frame >= 0) & (far_frame < frames)).astype(jnp.int32).reshape(1)
    place = (frame.reshape(1), row.reshape(1))

    firsts = [sum(CHUNKS[:c]) for c in range(len(CHUNKS))]
    lse = log_sums.reshape(heads, 1, tile)
    mask = window_mask.reshape(9)
    own_kv = pack(k, v)
    near_kv = lax.ppermute(own_kv, "tm", near_pairs)
    far_kv = lax.ppermute(own_kv, "tm", far_pairs)
    make = lambda first, counts, source: prep(
        first, counts, width, (frames, rows), place, mask, source, g, o, lse
    )
    mine = make(0, CHUNKS[:1], q)
    theirs = {0: lax.ppermute(mine[0], "space", partner)}
    mine += make(firsts[1], CHUNKS[1:], after(q, mine[0]))
    frames_kv = {HERE: own_kv, NEAR: near_kv, FAR: far_kv}
    last = len(CHUNKS) - 1
    outers = {}
    sums = [{} for _ in CHUNKS]
    backs = [{} for _ in CHUNKS]
    done = []
    out = None

    def stage(c, step, *awaited):
        messages = {OUTER: outers.get(c), OWN: mine[c], PARTNER: theirs.get(c)}
        stages = LATER_STAGES if c == last else STAGES
        work = stages[step]
        needed = {j: messages[j] for _, js in work for j in js}
        first_used = min(needed)
        arrived = [backs[i][name] for i, name in awaited]
        needed[first_used] = after(needed[first_used], *done[-1:], *arrived)
        later = {j for other in stages[step + 1 :] for _, js in other for j in js}
        slots = {slot for other in stages[step + 1 :] for slot, _ in other}
        straight = (OUTER, PARTNER) if c == last else (OUTER,)
        final = {"q%d" % j for j in straight if j not in later}
        final |= {"kv%d" % slot for slot in (NEAR, FAR) if slot not in slots}
        joined = {}
        if c < last and step + 1 == len(stages):
            for name in JOINED:
                joined[name] = (firsts[last] * width, sums[c - 1][name] if c else None)
        sums[c] = run_stage(
            work, WEIGHTS[c][step], final, joined, firsts[c], CHUNKS[c], width, has_far, frames_kv, needed, sums[c]
        )
        done.append(sums[c]["kv0"])
        for name, axis, pairs in (
            ("q0", "space", owners if c == last else homeward),
            ("q2", "space", partner),
            ("kv1", "tm", near_pairs),
            ("kv2", "tm", far_pairs),
        ):
            if name not in final or name not in sums[c] or name in backs[c]:
                continue
            if name in joined and c + 1 < last:
                continue
            backs[c][name] = lax.ppermute(sums[c][name], axis, pairs)
            if name in joined:
                for earlier in range(c):
                    backs[earlier][name] = backs[c][name]

    def hand_on(c):
        outers[c] = lax.ppermute(after(theirs[c], *done[-1:]), "space", onward)

    def send_back(c):
        total = sums[c]["q2"] + after(backs[c]["q0"], *done[-1:]).astype(F32)
        backs[c]["q2"] = lax.ppermute(total.astype(BF16), "space", partner)

    def complete(c, so_far):
        back = backs[c]
        own = after(sums[c]["q1"], *done[-1:])
        from_others = [back["q2"]] + ([back["q0"]] if c == last else [])
        so_far = finish(
            firsts[c], CHUNKS[c], width, full,
            (sums[c]["kv0"], back["kv1"], back["kv2"], own, *from_others), so_far,
        )
        done.append(so_far[0])
        return so_far

    for c in range(1, len(CHUNKS)):
        theirs[c] = lax.ppermute(mine[c], "space", partner)
    for kind, c, *rest in ORDER:
        if kind == "stage":
            stage(c, *rest)
        elif kind == "hand":
            hand_on(c)
        elif kind == "back":
            send_back(c)
        else:
            out = complete(c, out)
    return tuple(a.reshape(queries.shape) for a in out)


def solution(mesh):
    tile = P("tm", "space", None, None)
    return jax.shard_map(
        per_device,
        mesh=mesh,
        in_specs=(tile,) * 6 + (P("tm", "space", None),),
        out_specs=(tile,) * 3,
        check_vma=False,
    )
```

```python
import functools
import math

import jax
import jax.numpy as jnp
from jax import lax
from jax.experimental import pallas as pl
from jax.experimental.pallas import tpu as pltpu
from jax.sharding import PartitionSpec as P

F32 = jnp.float32
BF16 = jnp.bfloat16
FAR_AWAY = 1e30

OUTER, OWN, PARTNER = (0, 1, 2)
HERE, NEAR, FAR = (0, 1, 2)
CHUNKS = (4, 5, 3)
STAGES = (
    ((HERE, (OWN,)), (NEAR, (OWN,))),
    ((HERE, (PARTNER,)), (NEAR, (PARTNER,))),
    ((HERE, (OUTER,)), (NEAR, (OUTER,)), (FAR, (OWN, PARTNER, OUTER))),
)
LATER_STAGES = (
    STAGES[0],
    STAGES[1] + ((FAR, (PARTNER,)),),
    ((HERE, (OUTER,)), (NEAR, (OUTER,)), (FAR, (OWN, OUTER))),
)
ORDER = (('stage', 0, 0), ('stage', 1, 0), ('hand', 0), ('stage', 0, 1), ('stage', 2, 0), ('hand', 1), ('stage', 0, 2), ('hand', 2), ('stage', 1, 1), ('back', 0), ('stage', 1, 2), ('stage', 2, 1), ('back', 1), ('stage', 2, 2, (0, 'q2'), (0, 'kv1')), ('finish', 0), ('finish', 1), ('finish', 2))
JOINED = ('kv2',)
WEIGHTS = ((60, 60, 60), (60, 30, 60), (240, 120, 60))
EXTRA = 32
VMEM_LIMIT = 20 * 1024 * 1024
GROUP = 1
BLOCK = 256


def dot(a, b, dims):
    return lax.dot_general(a, b, (dims, ((), ())), preferred_element_type=F32)


def three_terms(row):
    terms = []
    for _ in range(3):
        term = row.astype(BF16).astype(F32)
        terms.append(term)
        row = row - term
    return terms


def fold(row):
    lanes = 128
    return [row[:, i : i + lanes] for i in range(0, row.shape[1], lanes)]


def flag_row(frames, rows, frame, row, mask_ref, lanes):
    toward = 1 - 2 * lax.rem(row, 2)
    near = 1 - 2 * lax.rem(frame, 2)
    lane = lax.broadcasted_iota(jnp.int32, (1, lanes), 1)
    flags = jnp.zeros((1, lanes), F32)
    for role in (OUTER, OWN, PARTNER):
        for slot in (HERE, NEAR, FAR):
            row_off = (role - 1) * toward
            frame_off = (0, near, -near)[slot]
            inside = (
                (row + row_off >= 0)
                & (row + row_off < rows)
                & (frame + frame_off >= 0)
                & (frame + frame_off < frames)
            )
            index = 3 * (frame_off + 1) + row_off + 1
            on = inside & ((mask_ref[index] > 0) | (index == 4))
            flags = jnp.where(lane == 3 * role + slot, on.astype(F32), flags)
    return flags


def prep_kernel(
    counts, frames, rows, frame_ref, row_ref, mask_ref, q_ref, g_ref, o_ref, lse_ref, *outs
):
    tile = q_ref.shape[0]
    width = q_ref.shape[1] // sum(counts)
    flags = flag_row(frames, rows, frame_ref[0], row_ref[0], mask_ref, width)
    ones = jnp.ones((8, width), BF16)
    head = 0
    for out, count in zip(outs, counts):
        for h in range(count):
            source = slice(head * width, (head + 1) * width)
            cols = slice(h * width, (h + 1) * width)
            grad = g_ref[:, source]
            out[0:tile, cols] = q_ref[:, source]
            out[tile : 2 * tile, cols] = grad
            prod = grad.astype(F32) * o_ref[:, source].astype(F32)
            high = prod.astype(BF16)
            low = (prod - high.astype(F32)).astype(BF16)
            delta = dot(ones, high, ((1,), (1,))) + dot(ones, low, ((1,), (1,)))
            lines = []
            for line in (lse_ref[head], delta[0:1, :]):
                for term in three_terms(line):
                    lines += fold(term)
            lines.append(flags)
            lines.append(jnp.zeros((EXTRA - len(lines), width), F32))
            extra = jnp.concatenate(lines, axis=0).astype(BF16)
            out[2 * tile : 2 * tile + EXTRA, cols] = extra
            head += 1


def prep(first, counts, head_width, sizes, place, mask, q, g, o, lse):
    tile, full = q.shape
    count = sum(counts)
    offset = first * head_width
    cols = pl.BlockSpec(
        (pl.Element(tile), pl.Element(count * head_width)), lambda i, *_: (0, offset)
    )
    shapes = [(2 * tile + EXTRA, n * head_width) for n in counts]
    return pl.pallas_call(
        functools.partial(prep_kernel, counts, *sizes),
        grid_spec=pltpu.PrefetchScalarGridSpec(
            num_scalar_prefetch=3,
            grid=(1,),
            in_specs=[
                cols,
                cols,
                cols,
                pl.BlockSpec(
                    (pl.Element(count), pl.Element(1), pl.Element(tile)),
                    lambda i, *_: (first, 0, 0),
                ),
            ],
            out_specs=[pl.BlockSpec(shape, lambda i, *_: (0, 0)) for shape in shapes],
        ),
        out_shape=[jax.ShapeDtypeStruct(shape, BF16) for shape in shapes],
        compiler_params=pltpu.CompilerParams(vmem_limit_bytes=VMEM_LIMIT),
        cost_estimate=pl.CostEstimate(
            flops=2 * tile * count * head_width,
            bytes_accessed=10 * tile * count * head_width,
            transcendentals=0,
        ),
        name="prep",
    )(*place, mask, *(pltpu.with_memory_space_constraint(a, pltpu.HBM) for a in (q, g, o)), lse)


def pack_kernel(k_ref, v_ref, out):
    out[0] = k_ref[...]
    out[1] = v_ref[...]


def pack(k, v, steps=2):
    tile, full = k.shape
    cols = pl.BlockSpec((tile, full // steps), lambda i: (0, i))
    return pl.pallas_call(
        pack_kernel,
        grid=(steps,),
        in_specs=[cols, cols],
        out_specs=pl.BlockSpec((2, tile, full // steps), lambda i: (0, 0, i)),
        out_shape=jax.ShapeDtypeStruct((2, tile, full), k.dtype),
        compiler_params=pltpu.CompilerParams(vmem_limit_bytes=VMEM_LIMIT),
        cost_estimate=pl.CostEstimate(flops=0, bytes_accessed=8 * k.size, transcendentals=0),
        name="pack",
    )(*(pltpu.with_memory_space_constraint(a, pltpu.HBM) for a in (k, v)))


def row_stats(message, tile):
    extra = message[2 * tile : 2 * tile + EXTRA, :].astype(F32)
    parts = tile // 128
    rows = []
    for base in (0, 3 * parts):
        pieces = []
        for p in range(parts):
            a, b, c = (extra[base + i * parts + p : base + i * parts + p + 1] for i in range(3))
            pieces.append(a + b + c)
        rows.append(jnp.concatenate(pieces, axis=1))
    return (rows[0], rows[1], extra[6 * parts : 6 * parts + 1])


def stage_kernel(work, names, carried, last, factor, group, far_ref, *refs):
    env = dict(zip(names, refs))
    tile, wide = env["message%d" % work[0][1][0]].shape
    tile = (tile - EXTRA) // 2
    width = wide // group
    heads = [slice(i * width, (i + 1) * width) for i in range(group)]
    used = sorted({j for _, js in work for j in js})
    stats = {
        (j, i): row_stats(env["message%d" % j].at[:, cols], tile)
        for j in used
        for i, cols in enumerate(heads)
    }
    started = set()

    def add_q(j, i, rows, term):
        name, cols = ("q%d" % j, heads[i])
        if (j, i, rows.start) in started:
            env["sum_" + name][rows, cols] += term
        elif "acc_" + name in env:
            env["sum_" + name][rows, cols] = env["acc_" + name][rows, cols] + term
        else:
            env["sum_" + name][rows, cols] = term
        started.add((j, i, rows.start))

    def pair_terms(slot, j, i):
        cols = heads[i]
        message, keys = (env["message%d" % j], env["keys%d" % slot])
        key, value = (keys[0, :, cols], keys[1, :, cols])
        shift, delta, flags = stats[j, i]
        lane = 3 * j + slot
        shift = jnp.where(flags[:, lane : lane + 1] > 0, shift, FAR_AWAY)
        term_k, term_v = (None, None)
        for low in range(0, tile, BLOCK):
            rows = slice(low, min(low + BLOCK, tile))
            queries = message[rows, cols]
            grads = message[tile + rows.start : tile + rows.stop, cols]
            scores = dot(key, queries, ((1,), (1,)))
            weights = jnp.exp(scores * factor - shift[:, rows])
            grad_prob = dot(value, grads, ((1,), (1,)))
            grad_score = (weights * (grad_prob - delta[:, rows])).astype(BF16)
            more_v = dot(weights.astype(BF16), grads, ((1,), (0,)))
            more_k = dot(grad_score, queries, ((1,), (0,)))
            add_q(j, i, rows, dot(grad_score, key, ((0,), (0,))))
            term_k = more_k if term_k is None else term_k + more_k
            term_v = more_v if term_v is None else term_v + more_v
        return (term_k, term_v)

    def key_frames(slots_js):
        for slot, js in slots_js:
            name = "kv%d" % slot
            out = env["out_" + name]
            for i, cols in enumerate(heads):
                dk, dv = pair_terms(slot, js[0], i)
                for j in js[1:]:
                    more_k, more_v = pair_terms(slot, j, i)
                    dk, dv = (dk + more_k, dv + more_v)
                if "acc_" + name in env:
                    acc = env["acc_" + name]
                    dk, dv = (dk + acc[0, :, cols], dv + acc[1, :, cols])
                out[0, :, cols] = (dk * factor if name in last else dk).astype(out.dtype)
                out[1, :, cols] = dv.astype(out.dtype)

    key_frames([(slot, js) for slot, js in work if slot != FAR])
    for slot, js in work:
        if slot == FAR:
            fresh = [j for j in js if (j, 0, 0) not in started]
            pl.when(far_ref[0] > 0)(functools.partial(key_frames, [(slot, js)]))

            @pl.when(far_ref[0] == 0)
            def _():
                out = env["out_kv%d" % FAR]
                out[...] = jnp.zeros_like(out)
                for j in fresh:
                    name = "q%d" % j
                    env["sum_" + name][...] = env["acc_" + name][...]

    for j in used:
        out = env["out_q%d" % j]
        out[...] = (env["sum_q%d" % j][...]).astype(out.dtype)


def run_stage(work, weight, last, joined, first, count, head_width, far, keys, messages, sums):
    rows, wide = next(iter(messages.values())).shape
    tile = (rows - EXTRA) // 2
    group = math.gcd(count, GROUP) if first % math.gcd(count, GROUP) == 0 else 1
    step, begin = (group * head_width, first // group)
    one = pl.BlockSpec((tile, step), lambda h, *_: (0, h))
    two = pl.BlockSpec((2, tile, step), lambda h, *_: (0, 0, h))
    cols = pl.BlockSpec((2, tile, step), lambda h, *_: (0, 0, h + begin))
    whole = pl.BlockSpec((rows, step), lambda h, *_: (0, h))
    used = sorted({j for _, js in work for j in js})
    slots = [slot for slot, _ in work]
    names, args, specs = ([], [], [])

    def give(name, arg, spec):
        names.append(name)
        args.append(arg)
        specs.append(spec)

    for j in used:
        give("message%d" % j, messages[j], whole)
    for slot in slots:
        give("keys%d" % slot, keys[slot], cols)
    touched = [("q%d" % j, one) for j in used] + [("kv%d" % s, two) for s in slots]
    carried = [name for name, _ in touched if name in sums]
    for name, spec in touched:
        if name in sums:
            give("acc_" + name, sums[name], spec)
    out_specs, out_shapes, aliases = ([], [], {})
    for name, spec in touched:
        shape = (tile, wide) if name.startswith("q") else (2, tile, wide)
        if name in last and name in joined:
            total, begun = joined[name]
            spec = cols
            shape = (2, tile, total)
            if begun is not None:
                aliases[1 + len(args)] = len(out_specs)
                give("begun_" + name, begun, pl.BlockSpec(memory_space=pl.ANY))
        out_specs.append(spec)
        out_shapes.append(jax.ShapeDtypeStruct(shape, BF16 if name in last else F32))
    names += ["out_" + name for name, _ in touched]
    names += ["sum_q%d" % j for j in used]
    pairs = count * sum(len(js) for _, js in work)
    results = pl.pallas_call(
        functools.partial(stage_kernel, work, names, carried, last, head_width**-0.5, group),
        grid_spec=pltpu.PrefetchScalarGridSpec(
            num_scalar_prefetch=1,
            grid=(count // group,),
            in_specs=specs,
            out_specs=out_specs,
            scratch_shapes=[pltpu.VMEM((tile, step), F32)] * len(used),
        ),
        out_shape=out_shapes,
        input_output_aliases=aliases,
        compiler_params=pltpu.CompilerParams(vmem_limit_bytes=VMEM_LIMIT),
        cost_estimate=pl.CostEstimate(
            flops=weight * pairs * tile * tile * head_width,
            bytes_accessed=20 * tile * wide,
            transcendentals=0,
        ),
        name="pairs",
    )(far, *args)
    return {**sums, **{name: value for (name, _), value in zip(touched, results)}}


def finish_kernel(factor, backs, own_kv, near, far, own_q, *rest):
    out_q, out_k, out_v = rest[-3:]
    total = own_q[...]
    for back in rest[:backs]:
        total = total + back[...].astype(F32)
    out_q[...] = (total * factor).astype(BF16)
    for i, (out, scale) in enumerate(((out_k, factor), (out_v, 1.0))):
        others = near[i].astype(F32) + far[i].astype(F32)
        out[...] = (own_kv[i] * scale + others).astype(BF16)


def finish(first, count, head_width, full, parts, so_far):
    tile = parts[0].shape[1]
    wide = count * head_width
    one = pl.BlockSpec((tile, wide), lambda i: (0, 0))
    two = pl.BlockSpec((2, tile, wide), lambda i: (0, 0, 0))

    def part(array):
        offset = first * head_width if array.shape[2] > wide else 0
        return pl.BlockSpec(
            (pl.Element(2), pl.Element(tile), pl.Element(wide)), lambda i: (0, 0, offset)
        )

    cols = pl.BlockSpec(
        (pl.Element(tile), pl.Element(wide)), lambda i: (0, first * head_width)
    )
    kept = [] if so_far is None else list(so_far)
    return pl.pallas_call(
        functools.partial(finish_kernel, head_width**-0.5, len(parts) - 4),
        grid=(1,),
        in_specs=[two, part(parts[1]), part(parts[2])] + [one] * (len(parts) - 3) + [pl.BlockSpec(memory_space=pl.ANY)] * len(kept),
        out_specs=[cols] * 3,
        out_shape=[jax.ShapeDtypeStruct((tile, full), BF16)] * 3,
        input_output_aliases={len(parts) + i: i for i in range(len(kept))},
        compiler_params=pltpu.CompilerParams(vmem_limit_bytes=VMEM_LIMIT),
        cost_estimate=pl.CostEstimate(
            flops=8 * tile * count * head_width,
            bytes_accessed=30 * tile * count * head_width,
            transcendentals=0,
        ),
        name="finish",
    )(*parts, *kept)


def after(value, *earlier):
    return lax.optimization_barrier((value, *earlier))[0]


def per_device(queries, keys, values, outputs, out_grads, log_sums, window_mask):
    tile, full = queries.shape[2:]
    heads = log_sums.shape[2]
    width = full // heads
    frames, rows = (lax.axis_size("tm"), lax.axis_size("space"))
    q, k, v, o, g = (a.reshape(tile, full) for a in (queries, keys, values, outputs, out_grads))
    partner = [(i, i ^ 1) for i in range(rows)]
    onward = [(i, (i + 2) % rows) for i in range(0, rows, 2)]
    onward += [(i, (i - 2) % rows) for i in range(1, rows, 2)]
    homeward = [(i + 2, i) for i in range(0, rows - 2, 2)]
    homeward += [(i, i + 2) for i in range(1, rows - 2, 2)]
    homeward += [(0, 1), (rows - 1, rows - 2)]
    owners = [(0, 0), (rows - 1, rows - 1)]
    for i in range(1, rows - 1, 2):
        owners += [(i, i + 1), (i + 1, i)]
    near_pairs = [(i, i ^ 1) for i in range(frames)]
    far_pairs = [(0, 0), (frames - 1, frames - 1)]
    for i in range(1, frames - 1, 2):
        far_pairs += [(i, i + 1), (i + 1, i)]

    frame, row = (lax.axis_index("tm"), lax.axis_index("space"))
    far_frame = frame - 1 + 2 * lax.rem(frame, 2)
    has_far = ((far_frame >= 0) & (far_frame < frames)).astype(jnp.int32).reshape(1)
    place = (frame.reshape(1), row.reshape(1))

    firsts = [sum(CHUNKS[:c]) for c in range(len(CHUNKS))]
    lse = log_sums.reshape(heads, 1, tile)
    mask = window_mask.reshape(9)
    own_kv = pack(k, v)
    near_kv = lax.ppermute(own_kv, "tm", near_pairs)
    far_kv = lax.ppermute(own_kv, "tm", far_pairs)
    make = lambda first, counts, source: prep(
        first, counts, width, (frames, rows), place, mask, source, g, o, lse
    )
    mine = make(0, CHUNKS[:1], q)
    theirs = {0: lax.ppermute(mine[0], "space", partner)}
    mine += make(firsts[1], CHUNKS[1:], after(q, mine[0]))
    frames_kv = {HERE: own_kv, NEAR: near_kv, FAR: far_kv}
    last = len(CHUNKS) - 1
    outers = {}
    sums = [{} for _ in CHUNKS]
    backs = [{} for _ in CHUNKS]
    done = []
    out = None

    def stage(c, step, *awaited):
        messages = {OUTER: outers.get(c), OWN: mine[c], PARTNER: theirs.get(c)}
        stages = LATER_STAGES if c == last else STAGES
        work = stages[step]
        needed = {j: messages[j] for _, js in work for j in js}
        first_used = min(needed)
        arrived = [backs[i][name] for i, name in awaited]
        needed[first_used] = after(needed[first_used], *done[-1:], *arrived)
        later = {j for other in stages[step + 1 :] for _, js in other for j in js}
        slots = {slot for other in stages[step + 1 :] for slot, _ in other}
        straight = (OUTER, PARTNER) if c == last else (OUTER,)
        final = {"q%d" % j for j in straight if j not in later}
        final |= {"kv%d" % slot for slot in (NEAR, FAR) if slot not in slots}
        joined = {}
        if c < last and step + 1 == len(stages):
            for name in JOINED:
                joined[name] = (firsts[last] * width, sums[c - 1][name] if c else None)
        sums[c] = run_stage(
            work, WEIGHTS[c][step], final, joined, firsts[c], CHUNKS[c], width, has_far, frames_kv, needed, sums[c]
        )
        done.append(sums[c]["kv0"])
        for name, axis, pairs in (
            ("q0", "space", owners if c == last else homeward),
            ("q2", "space", partner),
            ("kv1", "tm", near_pairs),
            ("kv2", "tm", far_pairs),
        ):
            if name not in final or name not in sums[c] or name in backs[c]:
                continue
            if name in joined and c + 1 < last:
                continue
            backs[c][name] = lax.ppermute(sums[c][name], axis, pairs)
            if name in joined:
                for earlier in range(c):
                    backs[earlier][name] = backs[c][name]

    def hand_on(c):
        outers[c] = lax.ppermute(after(theirs[c], *done[-1:]), "space", onward)

    def send_back(c):
        total = sums[c]["q2"] + after(backs[c]["q0"], *done[-1:]).astype(F32)
        backs[c]["q2"] = lax.ppermute(total.astype(BF16), "space", partner)

    def complete(c, so_far):
        back = backs[c]
        own = after(sums[c]["q1"], *done[-1:])
        from_others = [back["q2"]] + ([back["q0"]] if c == last else [])
        so_far = finish(
            firsts[c], CHUNKS[c], width, full,
            (sums[c]["kv0"], back["kv1"], back["kv2"], own, *from_others), so_far,
        )
        done.append(so_far[0])
        return so_far

    for c in range(1, len(CHUNKS)):
        theirs[c] = lax.ppermute(mine[c], "space", partner)
    for kind, c, *rest in ORDER:
        if kind == "stage":
            stage(c, *rest)
        elif kind == "hand":
            hand_on(c)
        elif kind == "back":
            send_back(c)
        else:
            out = complete(c, out)
    return tuple(a.reshape(queries.shape) for a in out)


def solution(mesh):
    tile = P("tm", "space", None, None)
    return jax.shard_map(
        per_device,
        mesh=mesh,
        in_specs=(tile,) * 6 + (P("tm", "space", None),),
        out_specs=(tile,) * 3,
        check_vma=False,
    )
```

```python
import functools
import math

import jax
import jax.numpy as jnp
from jax import lax
from jax.experimental import pallas as pl
from jax.experimental.pallas import tpu as pltpu
from jax.sharding import PartitionSpec as P

F32 = jnp.float32
BF16 = jnp.bfloat16
LOG2E = math.log2(math.e)
FAR_AWAY = 1e30

OUTER, OWN, PARTNER = (0, 1, 2)
HERE, NEAR, FAR = (0, 1, 2)
CHUNKS = (4, 5, 3)
STAGES = (
    ((HERE, (OWN,)), (NEAR, (OWN,))),
    ((HERE, (PARTNER,)), (NEAR, (PARTNER,))),
    ((HERE, (OUTER,)), (NEAR, (OUTER,)), (FAR, (OWN, PARTNER, OUTER))),
)
LATER_STAGES = (
    STAGES[0],
    STAGES[1] + ((FAR, (PARTNER,)),),
    ((HERE, (OUTER,)), (NEAR, (OUTER,)), (FAR, (OWN, OUTER))),
)
ORDER = (('stage', 0, 0), ('stage', 1, 0), ('hand', 0), ('stage', 0, 1), ('stage', 2, 0), ('hand', 1), ('stage', 0, 2), ('hand', 2), ('stage', 1, 1), ('back', 0), ('stage', 1, 2), ('stage', 2, 1), ('back', 1), ('stage', 2, 2, (0, 'q2'), (0, 'kv1')), ('finish', 0), ('finish', 1), ('finish', 2))
JOINED = ('kv2',)
WEIGHTS = ((60, 60, 60), (60, 30, 60), (240, 120, 60))
EXTRA = 32
VMEM_LIMIT = 20 * 1024 * 1024
GROUP = 1


def dot(a, b, dims):
    return lax.dot_general(a, b, (dims, ((), ())), preferred_element_type=F32)


def three_terms(row):
    terms = []
    for _ in range(3):
        term = row.astype(BF16).astype(F32)
        terms.append(term)
        row = row - term
    return terms


def fold(row):
    lanes = 128
    return [row[:, i : i + lanes] for i in range(0, row.shape[1], lanes)]


def flag_row(frames, rows, frame, row, mask_ref, lanes):
    toward = 1 - 2 * lax.rem(row, 2)
    near = 1 - 2 * lax.rem(frame, 2)
    lane = lax.broadcasted_iota(jnp.int32, (1, lanes), 1)
    flags = jnp.zeros((1, lanes), F32)
    for role in (OUTER, OWN, PARTNER):
        for slot in (HERE, NEAR, FAR):
            row_off = (role - 1) * toward
            frame_off = (0, near, -near)[slot]
            inside = (
                (row + row_off >= 0)
                & (row + row_off < rows)
                & (frame + frame_off >= 0)
                & (frame + frame_off < frames)
            )
            index = 3 * (frame_off + 1) + row_off + 1
            on = inside & ((mask_ref[index] > 0) | (index == 4))
            flags = jnp.where(lane == 3 * role + slot, on.astype(F32), flags)
    return flags


def prep_kernel(
    counts, frames, rows, frame_ref, row_ref, mask_ref, q_ref, g_ref, o_ref, lse_ref, *outs
):
    tile = q_ref.shape[0]
    width = q_ref.shape[1] // sum(counts)
    flags = flag_row(frames, rows, frame_ref[0], row_ref[0], mask_ref, width)
    ones = jnp.ones((8, width), BF16)
    head = 0
    for out, count in zip(outs, counts):
        for h in range(count):
            source = slice(head * width, (head + 1) * width)
            cols = slice(h * width, (h + 1) * width)
            grad = g_ref[:, source]
            out[0:tile, cols] = q_ref[:, source]
            out[tile : 2 * tile, cols] = grad
            prod = grad.astype(F32) * o_ref[:, source].astype(F32)
            high = prod.astype(BF16)
            low = (prod - high.astype(F32)).astype(BF16)
            delta = dot(ones, high, ((1,), (1,))) + dot(ones, low, ((1,), (1,)))
            lines = []
            for line in (lse_ref[head] * LOG2E, delta[0:1, :]):
                for term in three_terms(line):
                    lines += fold(term)
            lines.append(flags)
            lines.append(jnp.zeros((EXTRA - len(lines), width), F32))
            extra = jnp.concatenate(lines, axis=0).astype(BF16)
            out[2 * tile : 2 * tile + EXTRA, cols] = extra
            head += 1


def prep(first, counts, head_width, sizes, place, mask, q, g, o, lse):
    tile, full = q.shape
    count = sum(counts)
    offset = first * head_width
    cols = pl.BlockSpec(
        (pl.Element(tile), pl.Element(count * head_width)), lambda i, *_: (0, offset)
    )
    shapes = [(2 * tile + EXTRA, n * head_width) for n in counts]
    return pl.pallas_call(
        functools.partial(prep_kernel, counts, *sizes),
        grid_spec=pltpu.PrefetchScalarGridSpec(
            num_scalar_prefetch=3,
            grid=(1,),
            in_specs=[
                cols,
                cols,
                cols,
                pl.BlockSpec(
                    (pl.Element(count), pl.Element(1), pl.Element(tile)),
                    lambda i, *_: (first, 0, 0),
                ),
            ],
            out_specs=[pl.BlockSpec(shape, lambda i, *_: (0, 0)) for shape in shapes],
        ),
        out_shape=[jax.ShapeDtypeStruct(shape, BF16) for shape in shapes],
        compiler_params=pltpu.CompilerParams(vmem_limit_bytes=VMEM_LIMIT),
        cost_estimate=pl.CostEstimate(
            flops=2 * tile * count * head_width,
            bytes_accessed=10 * tile * count * head_width,
            transcendentals=0,
        ),
        name="prep",
    )(*place, mask, *(pltpu.with_memory_space_constraint(a, pltpu.HBM) for a in (q, g, o)), lse)


def pack_kernel(k_ref, v_ref, out):
    out[0] = k_ref[...]
    out[1] = v_ref[...]


def pack(k, v, steps=2):
    tile, full = k.shape
    cols = pl.BlockSpec((tile, full // steps), lambda i: (0, i))
    return pl.pallas_call(
        pack_kernel,
        grid=(steps,),
        in_specs=[cols, cols],
        out_specs=pl.BlockSpec((2, tile, full // steps), lambda i: (0, 0, i)),
        out_shape=jax.ShapeDtypeStruct((2, tile, full), k.dtype),
        compiler_params=pltpu.CompilerParams(vmem_limit_bytes=VMEM_LIMIT),
        cost_estimate=pl.CostEstimate(flops=0, bytes_accessed=8 * k.size, transcendentals=0),
        name="pack",
    )(*(pltpu.with_memory_space_constraint(a, pltpu.HBM) for a in (k, v)))


def row_stats(message, tile):
    extra = message[2 * tile : 2 * tile + EXTRA, :].astype(F32)
    parts = tile // 128
    rows = []
    for base in (0, 3 * parts):
        pieces = []
        for p in range(parts):
            a, b, c = (extra[base + i * parts + p : base + i * parts + p + 1] for i in range(3))
            pieces.append(a + b + c)
        rows.append(jnp.concatenate(pieces, axis=1))
    return (rows[0], rows[1], extra[6 * parts : 6 * parts + 1])


def stage_kernel(work, names, carried, last, factor, group, far_ref, *refs):
    env = dict(zip(names, refs))
    tile, wide = env["message%d" % work[0][1][0]].shape
    tile = (tile - EXTRA) // 2
    width = wide // group
    heads = [slice(i * width, (i + 1) * width) for i in range(group)]
    used = sorted({j for _, js in work for j in js})
    stats = {
        (j, i): row_stats(env["message%d" % j].at[:, cols], tile)
        for j in used
        for i, cols in enumerate(heads)
    }
    started = set()

    def add_q(j, i, term):
        name, cols = ("q%d" % j, heads[i])
        if (j, i) in started:
            env["sum_" + name][:, cols] += term
        elif "acc_" + name in env:
            env["sum_" + name][:, cols] = env["acc_" + name][:, cols] + term
        else:
            env["sum_" + name][:, cols] = term
        started.add((j, i))

    def pair_terms(slot, j, i):
        cols = heads[i]
        message, keys = (env["message%d" % j], env["keys%d" % slot])
        queries, grads = (message[0:tile, cols], message[tile : 2 * tile, cols])
        key, value = (keys[0, :, cols], keys[1, :, cols])
        shift, delta, flags = stats[j, i]
        lane = 3 * j + slot
        shift = jnp.where(flags[:, lane : lane + 1] > 0, shift, FAR_AWAY)
        scores = dot(key, queries, ((1,), (1,)))
        weights = jnp.exp2(scores * (factor * LOG2E) - shift)
        grad_prob = dot(value, grads, ((1,), (1,)))
        grad_score = (weights * (grad_prob - delta)).astype(BF16)
        term_v = dot(weights.astype(BF16), grads, ((1,), (0,)))
        term_k = dot(grad_score, queries, ((1,), (0,)))
        add_q(j, i, dot(grad_score, key, ((0,), (0,))))
        return (term_k, term_v)

    def key_frames(slots_js):
        for slot, js in slots_js:
            name = "kv%d" % slot
            out = env["out_" + name]
            for i, cols in enumerate(heads):
                dk, dv = pair_terms(slot, js[0], i)
                for j in js[1:]:
                    more_k, more_v = pair_terms(slot, j, i)
                    dk, dv = (dk + more_k, dv + more_v)
                if "acc_" + name in env:
                    acc = env["acc_" + name]
                    dk, dv = (dk + acc[0, :, cols], dv + acc[1, :, cols])
                out[0, :, cols] = (dk * factor if name in last else dk).astype(out.dtype)
                out[1, :, cols] = dv.astype(out.dtype)

    key_frames([(slot, js) for slot, js in work if slot != FAR])
    for slot, js in work:
        if slot == FAR:
            fresh = [j for j in js if (j, 0) not in started]
            pl.when(far_ref[0] > 0)(functools.partial(key_frames, [(slot, js)]))

            @pl.when(far_ref[0] == 0)
            def _():
                out = env["out_kv%d" % FAR]
                out[...] = jnp.zeros_like(out)
                for j in fresh:
                    name = "q%d" % j
                    env["sum_" + name][...] = env["acc_" + name][...]

    for j in used:
        out = env["out_q%d" % j]
        out[...] = (env["sum_q%d" % j][...]).astype(out.dtype)


def run_stage(work, weight, last, joined, first, count, head_width, far, keys, messages, sums):
    rows, wide = next(iter(messages.values())).shape
    tile = (rows - EXTRA) // 2
    group = math.gcd(count, GROUP) if first % math.gcd(count, GROUP) == 0 else 1
    step, begin = (group * head_width, first // group)
    one = pl.BlockSpec((tile, step), lambda h, *_: (0, h))
    two = pl.BlockSpec((2, tile, step), lambda h, *_: (0, 0, h))
    cols = pl.BlockSpec((2, tile, step), lambda h, *_: (0, 0, h + begin))
    whole = pl.BlockSpec((rows, step), lambda h, *_: (0, h))
    used = sorted({j for _, js in work for j in js})
    slots = [slot for slot, _ in work]
    names, args, specs = ([], [], [])

    def give(name, arg, spec):
        names.append(name)
        args.append(arg)
        specs.append(spec)

    for j in used:
        give("message%d" % j, messages[j], whole)
    for slot in slots:
        give("keys%d" % slot, keys[slot], cols)
    touched = [("q%d" % j, one) for j in used] + [("kv%d" % s, two) for s in slots]
    carried = [name for name, _ in touched if name in sums]
    for name, spec in touched:
        if name in sums:
            give("acc_" + name, sums[name], spec)
    out_specs, out_shapes, aliases = ([], [], {})
    for name, spec in touched:
        shape = (tile, wide) if name.startswith("q") else (2, tile, wide)
        if name in last and name in joined:
            total, begun = joined[name]
            spec = cols
            shape = (2, tile, total)
            if begun is not None:
                aliases[1 + len(args)] = len(out_specs)
                give("begun_" + name, begun, pl.BlockSpec(memory_space=pl.ANY))
        out_specs.append(spec)
        out_shapes.append(jax.ShapeDtypeStruct(shape, BF16 if name in last else F32))
    names += ["out_" + name for name, _ in touched]
    names += ["sum_q%d" % j for j in used]
    pairs = count * sum(len(js) for _, js in work)
    results = pl.pallas_call(
        functools.partial(stage_kernel, work, names, carried, last, head_width**-0.5, group),
        grid_spec=pltpu.PrefetchScalarGridSpec(
            num_scalar_prefetch=1,
            grid=(count // group,),
            in_specs=specs,
            out_specs=out_specs,
            scratch_shapes=[pltpu.VMEM((tile, step), F32)] * len(used),
        ),
        out_shape=out_shapes,
        input_output_aliases=aliases,
        compiler_params=pltpu.CompilerParams(vmem_limit_bytes=VMEM_LIMIT),
        cost_estimate=pl.CostEstimate(
            flops=weight * pairs * tile * tile * head_width,
            bytes_accessed=20 * tile * wide,
            transcendentals=0,
        ),
        name="pairs",
    )(far, *args)
    return {**sums, **{name: value for (name, _), value in zip(touched, results)}}


def finish_kernel(factor, backs, own_kv, near, far, own_q, *rest):
    out_q, out_k, out_v = rest[-3:]
    total = own_q[...]
    for back in rest[:backs]:
        total = total + back[...].astype(F32)
    out_q[...] = (total * factor).astype(BF16)
    for i, (out, scale) in enumerate(((out_k, factor), (out_v, 1.0))):
        others = near[i].astype(F32) + far[i].astype(F32)
        out[...] = (own_kv[i] * scale + others).astype(BF16)


def finish(first, count, head_width, full, parts, so_far):
    tile = parts[0].shape[1]
    wide = count * head_width
    one = pl.BlockSpec((tile, wide), lambda i: (0, 0))
    two = pl.BlockSpec((2, tile, wide), lambda i: (0, 0, 0))

    def part(array):
        offset = first * head_width if array.shape[2] > wide else 0
        return pl.BlockSpec(
            (pl.Element(2), pl.Element(tile), pl.Element(wide)), lambda i: (0, 0, offset)
        )

    cols = pl.BlockSpec(
        (pl.Element(tile), pl.Element(wide)), lambda i: (0, first * head_width)
    )
    kept = [] if so_far is None else list(so_far)
    return pl.pallas_call(
        functools.partial(finish_kernel, head_width**-0.5, len(parts) - 4),
        grid=(1,),
        in_specs=[two, part(parts[1]), part(parts[2])] + [one] * (len(parts) - 3) + [pl.BlockSpec(memory_space=pl.ANY)] * len(kept),
        out_specs=[cols] * 3,
        out_shape=[jax.ShapeDtypeStruct((tile, full), BF16)] * 3,
        input_output_aliases={len(parts) + i: i for i in range(len(kept))},
        compiler_params=pltpu.CompilerParams(vmem_limit_bytes=VMEM_LIMIT),
        cost_estimate=pl.CostEstimate(
            flops=8 * tile * count * head_width,
            bytes_accessed=30 * tile * count * head_width,
            transcendentals=0,
        ),
        name="finish",
    )(*parts, *kept)


def after(value, *earlier):
    return lax.optimization_barrier((value, *earlier))[0]


def per_device(queries, keys, values, outputs, out_grads, log_sums, window_mask):
    tile, full = queries.shape[2:]
    heads = log_sums.shape[2]
    width = full // heads
    frames, rows = (lax.axis_size("tm"), lax.axis_size("space"))
    q, k, v, o, g = (a.reshape(tile, full) for a in (queries, keys, values, outputs, out_grads))
    partner = [(i, i ^ 1) for i in range(rows)]
    onward = [(i, (i + 2) % rows) for i in range(0, rows, 2)]
    onward += [(i, (i - 2) % rows) for i in range(1, rows, 2)]
    homeward = [(i + 2, i) for i in range(0, rows - 2, 2)]
    homeward += [(i, i + 2) for i in range(1, rows - 2, 2)]
    homeward += [(0, 1), (rows - 1, rows - 2)]
    owners = [(0, 0), (rows - 1, rows - 1)]
    for i in range(1, rows - 1, 2):
        owners += [(i, i + 1), (i + 1, i)]
    near_pairs = [(i, i ^ 1) for i in range(frames)]
    far_pairs = [(0, 0), (frames - 1, frames - 1)]
    for i in range(1, frames - 1, 2):
        far_pairs += [(i, i + 1), (i + 1, i)]

    frame, row = (lax.axis_index("tm"), lax.axis_index("space"))
    far_frame = frame - 1 + 2 * lax.rem(frame, 2)
    has_far = ((far_frame >= 0) & (far_frame < frames)).astype(jnp.int32).reshape(1)
    place = (frame.reshape(1), row.reshape(1))

    firsts = [sum(CHUNKS[:c]) for c in range(len(CHUNKS))]
    lse = log_sums.reshape(heads, 1, tile)
    mask = window_mask.reshape(9)
    own_kv = pack(k, v)
    near_kv = lax.ppermute(own_kv, "tm", near_pairs)
    far_kv = lax.ppermute(own_kv, "tm", far_pairs)
    make = lambda first, counts, source: prep(
        first, counts, width, (frames, rows), place, mask, source, g, o, lse
    )
    mine = make(0, CHUNKS[:1], q)
    theirs = {0: lax.ppermute(mine[0], "space", partner)}
    mine += make(firsts[1], CHUNKS[1:], after(q, mine[0]))
    frames_kv = {HERE: own_kv, NEAR: near_kv, FAR: far_kv}
    last = len(CHUNKS) - 1
    outers = {}
    sums = [{} for _ in CHUNKS]
    backs = [{} for _ in CHUNKS]
    done = []
    out = None

    def stage(c, step, *awaited):
        messages = {OUTER: outers.get(c), OWN: mine[c], PARTNER: theirs.get(c)}
        stages = LATER_STAGES if c == last else STAGES
        work = stages[step]
        needed = {j: messages[j] for _, js in work for j in js}
        first_used = min(needed)
        arrived = [backs[i][name] for i, name in awaited]
        needed[first_used] = after(needed[first_used], *done[-1:], *arrived)
        later = {j for other in stages[step + 1 :] for _, js in other for j in js}
        slots = {slot for other in stages[step + 1 :] for slot, _ in other}
        straight = (OUTER, PARTNER) if c == last else (OUTER,)
        final = {"q%d" % j for j in straight if j not in later}
        final |= {"kv%d" % slot for slot in (NEAR, FAR) if slot not in slots}
        joined = {}
        if c < last and step + 1 == len(stages):
            for name in JOINED:
                joined[name] = (firsts[last] * width, sums[c - 1][name] if c else None)
        sums[c] = run_stage(
            work, WEIGHTS[c][step], final, joined, firsts[c], CHUNKS[c], width, has_far, frames_kv, needed, sums[c]
        )
        done.append(sums[c]["kv0"])
        for name, axis, pairs in (
            ("q0", "space", owners if c == last else homeward),
            ("q2", "space", partner),
            ("kv1", "tm", near_pairs),
            ("kv2", "tm", far_pairs),
        ):
            if name not in final or name not in sums[c] or name in backs[c]:
                continue
            if name in joined and c + 1 < last:
                continue
            backs[c][name] = lax.ppermute(sums[c][name], axis, pairs)
            if name in joined:
                for earlier in range(c):
                    backs[earlier][name] = backs[c][name]

    def hand_on(c):
        outers[c] = lax.ppermute(after(theirs[c], *done[-1:]), "space", onward)

    def send_back(c):
        total = sums[c]["q2"] + after(backs[c]["q0"], *done[-1:]).astype(F32)
        backs[c]["q2"] = lax.ppermute(total.astype(BF16), "space", partner)

    def complete(c, so_far):
        back = backs[c]
        own = after(sums[c]["q1"], *done[-1:])
        from_others = [back["q2"]] + ([back["q0"]] if c == last else [])
        so_far = finish(
            firsts[c], CHUNKS[c], width, full,
            (sums[c]["kv0"], back["kv1"], back["kv2"], own, *from_others), so_far,
        )
        done.append(so_far[0])
        return so_far

    for c in range(1, len(CHUNKS)):
        theirs[c] = lax.ppermute(mine[c], "space", partner)
    for kind, c, *rest in ORDER:
        if kind == "stage":
            stage(c, *rest)
        elif kind == "hand":
            hand_on(c)
        elif kind == "back":
            send_back(c)
        else:
            out = complete(c, out)
    return tuple(a.reshape(queries.shape) for a in out)


def solution(mesh):
    tile = P("tm", "space", None, None)
    return jax.shard_map(
        per_device,
        mesh=mesh,
        in_specs=(tile,) * 6 + (P("tm", "space", None),),
        out_specs=(tile,) * 3,
        check_vma=False,
    )
```

```python
import functools
import math

import jax
import jax.numpy as jnp
from jax import lax
from jax.experimental import pallas as pl
from jax.experimental.pallas import tpu as pltpu
from jax.sharding import PartitionSpec as P

F32 = jnp.float32
BF16 = jnp.bfloat16
LOG2E = math.log2(math.e)
FAR_AWAY = 1e30

OUTER, OWN, PARTNER = (0, 1, 2)
HERE, NEAR, FAR = (0, 1, 2)
CHUNKS = (4, 5, 3)
STAGES = (
    ((HERE, (OWN,)), (NEAR, (OWN,))),
    ((HERE, (PARTNER,)), (NEAR, (PARTNER,))),
    ((HERE, (OUTER,)), (NEAR, (OUTER,)), (FAR, (OWN, PARTNER, OUTER))),
)
LATER_STAGES = (
    STAGES[0],
    STAGES[1] + ((FAR, (PARTNER,)),),
    ((HERE, (OUTER,)), (NEAR, (OUTER,)), (FAR, (OWN, OUTER))),
)
ORDER = (('stage', 0, 0), ('stage', 1, 0), ('hand', 0), ('stage', 0, 1), ('stage', 2, 0), ('hand', 1), ('stage', 0, 2), ('hand', 2), ('stage', 1, 1), ('back', 0), ('stage', 1, 2), ('stage', 2, 1), ('back', 1), ('stage', 2, 2, (0, 'q2'), (0, 'kv1')), ('finish', 0), ('finish', 1), ('finish', 2))
JOINED = ('kv2',)
WEIGHTS = ((60, 60, 60), (60, 30, 60), (240, 120, 60))
EXTRA = 32
VMEM_LIMIT = 20 * 1024 * 1024
GROUP = 1


def dot(a, b, dims):
    return lax.dot_general(a, b, (dims, ((), ())), preferred_element_type=F32)


def three_terms(row):
    terms = []
    for _ in range(3):
        term = row.astype(BF16).astype(F32)
        terms.append(term)
        row = row - term
    return terms


def fold(row):
    lanes = 128
    return [row[:, i : i + lanes] for i in range(0, row.shape[1], lanes)]


def flag_row(frames, rows, frame, row, mask_ref, lanes):
    toward = 1 - 2 * lax.rem(row, 2)
    near = 1 - 2 * lax.rem(frame, 2)
    lane = lax.broadcasted_iota(jnp.int32, (1, lanes), 1)
    flags = jnp.zeros((1, lanes), F32)
    for role in (OUTER, OWN, PARTNER):
        for slot in (HERE, NEAR, FAR):
            row_off = (role - 1) * toward
            frame_off = (0, near, -near)[slot]
            inside = (
                (row + row_off >= 0)
                & (row + row_off < rows)
                & (frame + frame_off >= 0)
                & (frame + frame_off < frames)
            )
            index = 3 * (frame_off + 1) + row_off + 1
            on = inside & ((mask_ref[index] > 0) | (index == 4))
            flags = jnp.where(lane == 3 * role + slot, on.astype(F32), flags)
    return flags


def prep_kernel(
    counts, frames, rows, frame_ref, row_ref, mask_ref, q_ref, g_ref, o_ref, lse_ref, *outs
):
    tile = q_ref.shape[0]
    width = q_ref.shape[1] // sum(counts)
    flags = flag_row(frames, rows, frame_ref[0], row_ref[0], mask_ref, width)
    ones = jnp.ones((8, width), BF16)
    head = 0
    for out, count in zip(outs, counts):
        for h in range(count):
            source = slice(head * width, (head + 1) * width)
            cols = slice(h * width, (h + 1) * width)
            grad = g_ref[:, source]
            out[0:tile, cols] = q_ref[:, source]
            out[tile : 2 * tile, cols] = grad
            prod = grad.astype(F32) * o_ref[:, source].astype(F32)
            high = prod.astype(BF16)
            low = (prod - high.astype(F32)).astype(BF16)
            delta = dot(ones, high, ((1,), (1,))) + dot(ones, low, ((1,), (1,)))
            lines = []
            for line in (lse_ref[head] * LOG2E, delta[0:1, :]):
                for term in three_terms(line):
                    lines += fold(term)
            lines.append(flags)
            lines.append(jnp.zeros((EXTRA - len(lines), width), F32))
            extra = jnp.concatenate(lines, axis=0).astype(BF16)
            out[2 * tile : 2 * tile + EXTRA, cols] = extra
            head += 1


def prep(first, counts, head_width, sizes, place, mask, q, g, o, lse):
    tile, full = q.shape
    count = sum(counts)
    offset = first * head_width
    cols = pl.BlockSpec(
        (pl.Element(tile), pl.Element(count * head_width)), lambda i, *_: (0, offset)
    )
    shapes = [(2 * tile + EXTRA, n * head_width) for n in counts]
    return pl.pallas_call(
        functools.partial(prep_kernel, counts, *sizes),
        grid_spec=pltpu.PrefetchScalarGridSpec(
            num_scalar_prefetch=3,
            grid=(1,),
            in_specs=[
                cols,
                cols,
                cols,
                pl.BlockSpec(
                    (pl.Element(count), pl.Element(1), pl.Element(tile)),
                    lambda i, *_: (first, 0, 0),
                ),
            ],
            out_specs=[pl.BlockSpec(shape, lambda i, *_: (0, 0)) for shape in shapes],
        ),
        out_shape=[jax.ShapeDtypeStruct(shape, BF16) for shape in shapes],
        compiler_params=pltpu.CompilerParams(vmem_limit_bytes=VMEM_LIMIT),
        cost_estimate=pl.CostEstimate(
            flops=2 * tile * count * head_width,
            bytes_accessed=10 * tile * count * head_width,
            transcendentals=0,
        ),
        name="prep",
    )(*place, mask, *(pltpu.with_memory_space_constraint(a, pltpu.HBM) for a in (q, g, o)), lse)


def pack_kernel(k_ref, v_ref, out):
    out[0] = k_ref[...]
    out[1] = v_ref[...]


def pack(k, v, steps=2):
    tile, full = k.shape
    cols = pl.BlockSpec((tile, full // steps), lambda i: (0, i))
    return pl.pallas_call(
        pack_kernel,
        grid=(steps,),
        in_specs=[cols, cols],
        out_specs=pl.BlockSpec((2, tile, full // steps), lambda i: (0, 0, i)),
        out_shape=jax.ShapeDtypeStruct((2, tile, full), k.dtype),
        compiler_params=pltpu.CompilerParams(vmem_limit_bytes=VMEM_LIMIT),
        cost_estimate=pl.CostEstimate(flops=0, bytes_accessed=8 * k.size, transcendentals=0),
        name="pack",
    )(*(pltpu.with_memory_space_constraint(a, pltpu.HBM) for a in (k, v)))


def row_stats(message, tile):
    extra = message[2 * tile : 2 * tile + EXTRA, :].astype(F32)
    parts = tile // 128
    rows = []
    for base in (0, 3 * parts):
        pieces = []
        for p in range(parts):
            a, b, c = (extra[base + i * parts + p : base + i * parts + p + 1] for i in range(3))
            pieces.append(a + b + c)
        rows.append(jnp.concatenate(pieces, axis=1))
    return (rows[0], rows[1], extra[6 * parts : 6 * parts + 1])


def stage_kernel(work, names, factor, group, far_ref, *refs):
    env = dict(zip(names, refs))
    tile, wide = env["message%d" % work[0][1][0]].shape
    tile = (tile - EXTRA) // 2
    width = wide // group
    heads = [slice(i * width, (i + 1) * width) for i in range(group)]
    used = sorted({j for _, js in work for j in js})
    stats = {
        (j, i): row_stats(env["message%d" % j].at[:, cols], tile)
        for j in used
        for i, cols in enumerate(heads)
    }
    started = set()

    def add_q(j, i, term):
        name, cols = ("q%d" % j, heads[i])
        if (j, i) in started:
            env["sum_" + name][:, cols] += term
        elif "acc_" + name in env:
            env["sum_" + name][:, cols] = env["acc_" + name][:, cols] + term
        else:
            env["sum_" + name][:, cols] = term
        started.add((j, i))

    def pair_terms(slot, j, i):
        cols = heads[i]
        message, keys = (env["message%d" % j], env["keys%d" % slot])
        queries, grads = (message[0:tile, cols], message[tile : 2 * tile, cols])
        key, value = (keys[0, :, cols], keys[1, :, cols])
        shift, delta, flags = stats[j, i]
        lane = 3 * j + slot
        shift = jnp.where(flags[:, lane : lane + 1] > 0, shift, FAR_AWAY)
        scores = dot(key, queries, ((1,), (1,)))
        weights = jnp.exp2(scores * (factor * LOG2E) - shift)
        grad_prob = dot(value, grads, ((1,), (1,)))
        grad_score = (weights * (grad_prob - delta)).astype(BF16)
        term_v = dot(weights.astype(BF16), grads, ((1,), (0,)))
        term_k = dot(grad_score, queries, ((1,), (0,))) * factor
        add_q(j, i, dot(grad_score, key, ((0,), (0,))))
        return (term_k, term_v)

    def key_frames(slots_js):
        for slot, js in slots_js:
            name = "kv%d" % slot
            out = env["out_" + name]
            for i, cols in enumerate(heads):
                dk, dv = (None, None)
                if "acc_" + name in env:
                    acc = env["acc_" + name]
                    dk, dv = (acc[0, :, cols], acc[1, :, cols])
                for j in js:
                    term_k, term_v = pair_terms(slot, j, i)
                    dk = term_k if dk is None else dk + term_k
                    dv = term_v if dv is None else dv + term_v
                out[0, :, cols] = dk.astype(out.dtype)
                out[1, :, cols] = dv.astype(out.dtype)

    key_frames([(slot, js) for slot, js in work if slot != FAR])
    for slot, js in work:
        if slot == FAR:
            fresh = [j for j in js if (j, 0) not in started]
            pl.when(far_ref[0] > 0)(functools.partial(key_frames, [(slot, js)]))

            @pl.when(far_ref[0] == 0)
            def _():
                out = env["out_kv%d" % FAR]
                out[...] = jnp.zeros_like(out)
                for j in fresh:
                    name = "q%d" % j
                    env["sum_" + name][...] = env["acc_" + name][...]

    for j in used:
        out = env["out_q%d" % j]
        out[...] = (env["sum_q%d" % j][...]).astype(out.dtype)


def run_stage(work, weight, last, joined, first, count, head_width, far, keys, messages, sums):
    rows, wide = next(iter(messages.values())).shape
    tile = (rows - EXTRA) // 2
    group = math.gcd(count, GROUP) if first % math.gcd(count, GROUP) == 0 else 1
    step, begin = (group * head_width, first // group)
    one = pl.BlockSpec((tile, step), lambda h, *_: (0, h))
    two = pl.BlockSpec((2, tile, step), lambda h, *_: (0, 0, h))
    cols = pl.BlockSpec((2, tile, step), lambda h, *_: (0, 0, h + begin))
    whole = pl.BlockSpec((rows, step), lambda h, *_: (0, h))
    used = sorted({j for _, js in work for j in js})
    slots = [slot for slot, _ in work]
    names, args, specs = ([], [], [])

    def give(name, arg, spec):
        names.append(name)
        args.append(arg)
        specs.append(spec)

    for j in used:
        give("message%d" % j, messages[j], whole)
    for slot in slots:
        give("keys%d" % slot, keys[slot], cols)
    touched = [("q%d" % j, one) for j in used] + [("kv%d" % s, two) for s in slots]
    for name, spec in touched:
        if name in sums:
            give("acc_" + name, sums[name], spec)
    out_specs, out_shapes, aliases = ([], [], {})
    for name, spec in touched:
        shape = (tile, wide) if name.startswith("q") else (2, tile, wide)
        if name in last and name in joined:
            total, begun = joined[name]
            spec = cols
            shape = (2, tile, total)
            if begun is not None:
                aliases[1 + len(args)] = len(out_specs)
                give("begun_" + name, begun, pl.BlockSpec(memory_space=pl.ANY))
        out_specs.append(spec)
        out_shapes.append(jax.ShapeDtypeStruct(shape, BF16 if name in last else F32))
    names += ["out_" + name for name, _ in touched]
    names += ["sum_q%d" % j for j in used]
    pairs = count * sum(len(js) for _, js in work)
    results = pl.pallas_call(
        functools.partial(stage_kernel, work, names, head_width**-0.5, group),
        grid_spec=pltpu.PrefetchScalarGridSpec(
            num_scalar_prefetch=1,
            grid=(count // group,),
            in_specs=specs,
            out_specs=out_specs,
            scratch_shapes=[pltpu.VMEM((tile, step), F32)] * len(used),
        ),
        out_shape=out_shapes,
        input_output_aliases=aliases,
        compiler_params=pltpu.CompilerParams(vmem_limit_bytes=VMEM_LIMIT),
        cost_estimate=pl.CostEstimate(
            flops=weight * pairs * tile * tile * head_width,
            bytes_accessed=20 * tile * wide,
            transcendentals=0,
        ),
        name="pairs",
    )(far, *args)
    return {**sums, **{name: value for (name, _), value in zip(touched, results)}}


def finish_kernel(factor, backs, own_kv, near, far, own_q, *rest):
    out_q, out_k, out_v = rest[-3:]
    total = own_q[...]
    for back in rest[:backs]:
        total = total + back[...].astype(F32)
    out_q[...] = (total * factor).astype(BF16)
    sums = own_kv[...] + near[...].astype(F32) + far[...].astype(F32)
    out_k[...] = sums[0].astype(BF16)
    out_v[...] = sums[1].astype(BF16)


def finish(first, count, head_width, full, parts, so_far):
    tile = parts[0].shape[1]
    wide = count * head_width
    one = pl.BlockSpec((tile, wide), lambda i: (0, 0))
    two = pl.BlockSpec((2, tile, wide), lambda i: (0, 0, 0))

    def part(array):
        offset = first * head_width if array.shape[2] > wide else 0
        return pl.BlockSpec(
            (pl.Element(2), pl.Element(tile), pl.Element(wide)), lambda i: (0, 0, offset)
        )

    cols = pl.BlockSpec(
        (pl.Element(tile), pl.Element(wide)), lambda i: (0, first * head_width)
    )
    kept = [] if so_far is None else list(so_far)
    return pl.pallas_call(
        functools.partial(finish_kernel, head_width**-0.5, len(parts) - 4),
        grid=(1,),
        in_specs=[two, part(parts[1]), part(parts[2])] + [one] * (len(parts) - 3) + [pl.BlockSpec(memory_space=pl.ANY)] * len(kept),
        out_specs=[cols] * 3,
        out_shape=[jax.ShapeDtypeStruct((tile, full), BF16)] * 3,
        input_output_aliases={len(parts) + i: i for i in range(len(kept))},
        compiler_params=pltpu.CompilerParams(vmem_limit_bytes=VMEM_LIMIT),
        cost_estimate=pl.CostEstimate(
            flops=8 * tile * count * head_width,
            bytes_accessed=30 * tile * count * head_width,
            transcendentals=0,
        ),
        name="finish",
    )(*parts, *kept)


def after(value, *earlier):
    return lax.optimization_barrier((value, *earlier))[0]


def per_device(queries, keys, values, outputs, out_grads, log_sums, window_mask):
    tile, full = queries.shape[2:]
    heads = log_sums.shape[2]
    width = full // heads
    frames, rows = (lax.axis_size("tm"), lax.axis_size("space"))
    q, k, v, o, g = (a.reshape(tile, full) for a in (queries, keys, values, outputs, out_grads))
    partner = [(i, i ^ 1) for i in range(rows)]
    onward = [(i, (i + 2) % rows) for i in range(0, rows, 2)]
    onward += [(i, (i - 2) % rows) for i in range(1, rows, 2)]
    homeward = [(i + 2, i) for i in range(0, rows - 2, 2)]
    homeward += [(i, i + 2) for i in range(1, rows - 2, 2)]
    homeward += [(0, 1), (rows - 1, rows - 2)]
    owners = [(0, 0), (rows - 1, rows - 1)]
    for i in range(1, rows - 1, 2):
        owners += [(i, i + 1), (i + 1, i)]
    near_pairs = [(i, i ^ 1) for i in range(frames)]
    far_pairs = [(0, 0), (frames - 1, frames - 1)]
    for i in range(1, frames - 1, 2):
        far_pairs += [(i, i + 1), (i + 1, i)]

    frame, row = (lax.axis_index("tm"), lax.axis_index("space"))
    far_frame = frame - 1 + 2 * lax.rem(frame, 2)
    has_far = ((far_frame >= 0) & (far_frame < frames)).astype(jnp.int32).reshape(1)
    place = (frame.reshape(1), row.reshape(1))

    firsts = [sum(CHUNKS[:c]) for c in range(len(CHUNKS))]
    lse = log_sums.reshape(heads, 1, tile)
    mask = window_mask.reshape(9)
    own_kv = pack(k, v)
    near_kv = lax.ppermute(own_kv, "tm", near_pairs)
    make = lambda first, counts, source: prep(
        first, counts, width, (frames, rows), place, mask, source, g, o, lse
    )
    mine = make(0, CHUNKS[:1], q)
    theirs = {0: lax.ppermute(mine[0], "space", partner)}
    far_kv = lax.ppermute(after(own_kv, mine[0]), "tm", far_pairs)
    mine += make(firsts[1], CHUNKS[1:], after(q, mine[0]))
    frames_kv = {HERE: own_kv, NEAR: near_kv, FAR: far_kv}
    last = len(CHUNKS) - 1
    outers = {}
    sums = [{} for _ in CHUNKS]
    backs = [{} for _ in CHUNKS]
    done = []
    out = None

    def stage(c, step, *awaited):
        messages = {OUTER: outers.get(c), OWN: mine[c], PARTNER: theirs.get(c)}
        stages = LATER_STAGES if c == last else STAGES
        work = stages[step]
        needed = {j: messages[j] for _, js in work for j in js}
        first_used = min(needed)
        arrived = [backs[i][name] for i, name in awaited]
        needed[first_used] = after(needed[first_used], *done[-1:], *arrived)
        later = {j for other in stages[step + 1 :] for _, js in other for j in js}
        slots = {slot for other in stages[step + 1 :] for slot, _ in other}
        straight = (OUTER, PARTNER) if c == last else (OUTER,)
        final = {"q%d" % j for j in straight if j not in later}
        final |= {"kv%d" % slot for slot in (NEAR, FAR) if slot not in slots}
        joined = {}
        if c < last and step + 1 == len(stages):
            for name in JOINED:
                joined[name] = (firsts[last] * width, sums[c - 1][name] if c else None)
        sums[c] = run_stage(
            work, WEIGHTS[c][step], final, joined, firsts[c], CHUNKS[c], width, has_far, frames_kv, needed, sums[c]
        )
        done.append(sums[c]["kv0"])
        for name, axis, pairs in (
            ("q0", "space", owners if c == last else homeward),
            ("q2", "space", partner),
            ("kv1", "tm", near_pairs),
            ("kv2", "tm", far_pairs),
        ):
            if name not in final or name not in sums[c] or name in backs[c]:
                continue
            if name in joined and c + 1 < last:
                continue
            backs[c][name] = lax.ppermute(sums[c][name], axis, pairs)
            if name in joined:
                for earlier in range(c):
                    backs[earlier][name] = backs[c][name]

    def hand_on(c):
        outers[c] = lax.ppermute(after(theirs[c], *done[-1:]), "space", onward)

    def send_back(c):
        total = sums[c]["q2"] + after(backs[c]["q0"], *done[-1:]).astype(F32)
        backs[c]["q2"] = lax.ppermute(total.astype(BF16), "space", partner)

    def complete(c, so_far):
        back = backs[c]
        own = after(sums[c]["q1"], *done[-1:])
        from_others = [back["q2"]] + ([back["q0"]] if c == last else [])
        so_far = finish(
            firsts[c], CHUNKS[c], width, full,
            (sums[c]["kv0"], back["kv1"], back["kv2"], own, *from_others), so_far,
        )
        done.append(so_far[0])
        return so_far

    for c in range(1, len(CHUNKS)):
        theirs[c] = lax.ppermute(mine[c], "space", partner)
    for kind, c, *rest in ORDER:
        if kind == "stage":
            stage(c, *rest)
        elif kind == "hand":
            hand_on(c)
        elif kind == "back":
            send_back(c)
        else:
            out = complete(c, out)
    return tuple(a.reshape(queries.shape) for a in out)


def solution(mesh):
    tile = P("tm", "space", None, None)
    return jax.shard_map(
        per_device,
        mesh=mesh,
        in_specs=(tile,) * 6 + (P("tm", "space", None),),
        out_specs=(tile,) * 3,
        check_vma=False,
    )
```

```python
import functools
import math

import jax
import jax.numpy as jnp
from jax import lax
from jax.experimental import pallas as pl
from jax.experimental.pallas import tpu as pltpu
from jax.sharding import PartitionSpec as P

F32 = jnp.float32
BF16 = jnp.bfloat16
LOG2E = math.log2(math.e)
FAR_AWAY = 1e30

OUTER, OWN, PARTNER = (0, 1, 2)
HERE, NEAR, FAR = (0, 1, 2)
CHUNKS = (4, 5, 3)
STAGES = (
    ((HERE, (OWN,)), (NEAR, (OWN,))),
    ((HERE, (PARTNER,)), (NEAR, (PARTNER,))),
    ((HERE, (OUTER,)), (NEAR, (OUTER,)), (FAR, (OWN, PARTNER, OUTER))),
)
LATER_STAGES = (
    STAGES[0],
    STAGES[1] + ((FAR, (PARTNER,)),),
    ((HERE, (OUTER,)), (NEAR, (OUTER,)), (FAR, (OWN, OUTER))),
)
DIRECT = 2
ORDER = (('stage', 0, 0), ('stage', 1, 0), ('hand', 0), ('stage', 0, 1), ('stage', 2, 0), ('hand', 1), ('stage', 0, 2), ('hand', 2), ('stage', 1, 1), ('back', 0), ('stage', 1, 2), ('stage', 2, 1), ('send', 1, 'kv2'), ('back', 1), ('stage', 2, 2, (0, 'q2'), (0, 'kv1')), ('finish', 0), ('finish', 1), ('finish', 2))
JOINED = ('kv2',)
WEIGHTS = ((60, 60, 60), (60, 30, 60), (240, 120, 60))
EXTRA = 16
TERMS = 2
VMEM_LIMIT = 20 * 1024 * 1024
GROUP = 1


def dot(a, b, dims):
    return lax.dot_general(a, b, (dims, ((), ())), preferred_element_type=F32)


def split_terms(row):
    terms = []
    for _ in range(TERMS):
        term = row.astype(BF16).astype(F32)
        terms.append(term)
        row = row - term
    return terms


def fold(row):
    lanes = 128
    return [row[:, i : i + lanes] for i in range(0, row.shape[1], lanes)]


def flag_row(frames, rows, frame, row, mask_ref, lanes):
    toward = 1 - 2 * lax.rem(row, 2)
    near = 1 - 2 * lax.rem(frame, 2)
    lane = lax.broadcasted_iota(jnp.int32, (1, lanes), 1)
    flags = jnp.zeros((1, lanes), F32)
    for role in (OUTER, OWN, PARTNER):
        for slot in (HERE, NEAR, FAR):
            row_off = (role - 1) * toward
            frame_off = (0, near, -near)[slot]
            inside = (
                (row + row_off >= 0)
                & (row + row_off < rows)
                & (frame + frame_off >= 0)
                & (frame + frame_off < frames)
            )
            index = 3 * (frame_off + 1) + row_off + 1
            on = inside & ((mask_ref[index] > 0) | (index == 4))
            flags = jnp.where(lane == 3 * role + slot, on.astype(F32), flags)
    return flags


def prep_kernel(
    counts, frames, rows, frame_ref, row_ref, mask_ref, q_ref, g_ref, o_ref, lse_ref, *outs
):
    tile = q_ref.shape[0]
    width = q_ref.shape[1] // sum(counts)
    flags = flag_row(frames, rows, frame_ref[0], row_ref[0], mask_ref, width)
    ones = jnp.ones((8, width), BF16)
    head = 0
    for out, count in zip(outs, counts):
        for h in range(count):
            source = slice(head * width, (head + 1) * width)
            cols = slice(h * width, (h + 1) * width)
            grad = g_ref[:, source]
            out[0:tile, cols] = q_ref[:, source]
            out[tile : 2 * tile, cols] = grad
            prod = grad.astype(F32) * o_ref[:, source].astype(F32)
            high = prod.astype(BF16)
            low = (prod - high.astype(F32)).astype(BF16)
            delta = dot(ones, high, ((1,), (1,))) + dot(ones, low, ((1,), (1,)))
            lines = []
            for line in (lse_ref[head] * LOG2E, delta[0:1, :]):
                for term in split_terms(line):
                    lines += fold(term)
            lines.append(flags)
            lines.append(jnp.zeros((EXTRA - len(lines), width), F32))
            extra = jnp.concatenate(lines, axis=0).astype(BF16)
            out[2 * tile : 2 * tile + EXTRA, cols] = extra
            head += 1


def prep(first, counts, head_width, sizes, place, mask, q, g, o, lse):
    tile, full = q.shape
    count = sum(counts)
    offset = first * head_width
    cols = pl.BlockSpec(
        (pl.Element(tile), pl.Element(count * head_width)), lambda i, *_: (0, offset)
    )
    shapes = [(2 * tile + EXTRA, n * head_width) for n in counts]
    return pl.pallas_call(
        functools.partial(prep_kernel, counts, *sizes),
        grid_spec=pltpu.PrefetchScalarGridSpec(
            num_scalar_prefetch=3,
            grid=(1,),
            in_specs=[
                cols,
                cols,
                cols,
                pl.BlockSpec(
                    (pl.Element(count), pl.Element(1), pl.Element(tile)),
                    lambda i, *_: (first, 0, 0),
                ),
            ],
            out_specs=[pl.BlockSpec(shape, lambda i, *_: (0, 0)) for shape in shapes],
        ),
        out_shape=[jax.ShapeDtypeStruct(shape, BF16) for shape in shapes],
        compiler_params=pltpu.CompilerParams(vmem_limit_bytes=VMEM_LIMIT),
        cost_estimate=pl.CostEstimate(
            flops=2 * tile * count * head_width,
            bytes_accessed=10 * tile * count * head_width,
            transcendentals=0,
        ),
        name="prep",
    )(*place, mask, *(pltpu.with_memory_space_constraint(a, pltpu.HBM) for a in (q, g, o)), lse)


def pack_kernel(k_ref, v_ref, out):
    out[0] = k_ref[...]
    out[1] = v_ref[...]


def pack(k, v, steps=2):
    tile, full = k.shape
    cols = pl.BlockSpec((tile, full // steps), lambda i: (0, i))
    return pl.pallas_call(
        pack_kernel,
        grid=(steps,),
        in_specs=[cols, cols],
        out_specs=pl.BlockSpec((2, tile, full // steps), lambda i: (0, 0, i)),
        out_shape=jax.ShapeDtypeStruct((2, tile, full), k.dtype),
        compiler_params=pltpu.CompilerParams(vmem_limit_bytes=VMEM_LIMIT),
        cost_estimate=pl.CostEstimate(flops=0, bytes_accessed=8 * k.size, transcendentals=0),
        name="pack",
    )(*(pltpu.with_memory_space_constraint(a, pltpu.HBM) for a in (k, v)))


def row_stats(message, tile):
    extra = message[2 * tile : 2 * tile + EXTRA, :].astype(F32)
    parts = tile // 128
    rows = []
    for base in (0, TERMS * parts):
        pieces = []
        for p in range(parts):
            first = base + p
            terms = [extra[first + i * parts : first + i * parts + 1] for i in range(TERMS)]
            pieces.append(sum(terms[1:], terms[0]))
        rows.append(jnp.concatenate(pieces, axis=1))
    return (rows[0], rows[1], extra[2 * TERMS * parts : 2 * TERMS * parts + 1])


def stage_kernel(work, names, factor, group, far_ref, *refs):
    env = dict(zip(names, refs))
    tile, wide = env["message%d" % work[0][1][0]].shape
    tile = (tile - EXTRA) // 2
    width = wide // group
    heads = [slice(i * width, (i + 1) * width) for i in range(group)]
    used = sorted({j for _, js in work for j in js})
    stats = {
        (j, i): row_stats(env["message%d" % j].at[:, cols], tile)
        for j in used
        for i, cols in enumerate(heads)
    }
    started = set()

    def add_q(j, i, term):
        name, cols = ("q%d" % j, heads[i])
        if (j, i) in started:
            env["sum_" + name][:, cols] += term
        elif "acc_" + name in env:
            env["sum_" + name][:, cols] = env["acc_" + name][:, cols] + term
        else:
            env["sum_" + name][:, cols] = term
        started.add((j, i))

    def pair_terms(slot, j, i):
        cols = heads[i]
        message, keys = (env["message%d" % j], env["keys%d" % slot])
        queries, grads = (message[0:tile, cols], message[tile : 2 * tile, cols])
        key, value = (keys[0, :, cols], keys[1, :, cols])
        shift, delta, flags = stats[j, i]
        lane = 3 * j + slot
        shift = jnp.where(flags[:, lane : lane + 1] > 0, shift, FAR_AWAY)
        scores = dot(key, queries, ((1,), (1,)))
        weights = jnp.exp2(scores * (factor * LOG2E) - shift)
        grad_prob = dot(value, grads, ((1,), (1,)))
        grad_score = (weights * (grad_prob - delta)).astype(BF16)
        term_v = dot(weights.astype(BF16), grads, ((1,), (0,)))
        term_k = dot(grad_score, queries, ((1,), (0,))) * factor
        add_q(j, i, dot(grad_score, key, ((0,), (0,))))
        return (term_k, term_v)

    def key_frames(slots_js):
        for slot, js in slots_js:
            name = "kv%d" % slot
            out = env["out_" + name]
            for i, cols in enumerate(heads):
                dk, dv = (None, None)
                if "acc_" + name in env:
                    acc = env["acc_" + name]
                    dk, dv = (acc[0, :, cols], acc[1, :, cols])
                for j in js:
                    term_k, term_v = pair_terms(slot, j, i)
                    dk = term_k if dk is None else dk + term_k
                    dv = term_v if dv is None else dv + term_v
                out[0, :, cols] = dk.astype(out.dtype)
                out[1, :, cols] = dv.astype(out.dtype)

    key_frames([(slot, js) for slot, js in work if slot != FAR])
    for slot, js in work:
        if slot == FAR:
            fresh = [j for j in js if (j, 0) not in started]
            pl.when(far_ref[0] > 0)(functools.partial(key_frames, [(slot, js)]))

            @pl.when(far_ref[0] == 0)
            def _():
                out = env["out_kv%d" % FAR]
                out[...] = jnp.zeros_like(out)
                for j in fresh:
                    name = "q%d" % j
                    env["sum_" + name][...] = env["acc_" + name][...]

    for j in used:
        out = env["out_q%d" % j]
        out[...] = (env["sum_q%d" % j][...]).astype(out.dtype)


def run_stage(work, weight, last, joined, first, count, head_width, far, keys, messages, sums):
    rows, wide = next(iter(messages.values())).shape
    tile = (rows - EXTRA) // 2
    group = math.gcd(count, GROUP) if first % math.gcd(count, GROUP) == 0 else 1
    step, begin = (group * head_width, first // group)
    one = pl.BlockSpec((tile, step), lambda h, *_: (0, h))
    two = pl.BlockSpec((2, tile, step), lambda h, *_: (0, 0, h))
    cols = pl.BlockSpec((2, tile, step), lambda h, *_: (0, 0, h + begin))
    whole = pl.BlockSpec((rows, step), lambda h, *_: (0, h))
    used = sorted({j for _, js in work for j in js})
    slots = [slot for slot, _ in work]
    names, args, specs = ([], [], [])

    def give(name, arg, spec):
        names.append(name)
        args.append(arg)
        specs.append(spec)

    for j in used:
        give("message%d" % j, messages[j], whole)
    for slot in slots:
        give("keys%d" % slot, keys[slot], cols)
    touched = [("q%d" % j, one) for j in used] + [("kv%d" % s, two) for s in slots]
    for name, spec in touched:
        if name in sums:
            give("acc_" + name, sums[name], spec)
    out_specs, out_shapes, aliases = ([], [], {})
    for name, spec in touched:
        shape = (tile, wide) if name.startswith("q") else (2, tile, wide)
        if name in last and name in joined:
            total, begun = joined[name]
            spec = cols
            shape = (2, tile, total)
            if begun is not None:
                aliases[1 + len(args)] = len(out_specs)
                give("begun_" + name, begun, pl.BlockSpec(memory_space=pl.ANY))
        out_specs.append(spec)
        out_shapes.append(jax.ShapeDtypeStruct(shape, BF16 if name in last else F32))
    names += ["out_" + name for name, _ in touched]
    names += ["sum_q%d" % j for j in used]
    pairs = count * sum(len(js) for _, js in work)
    results = pl.pallas_call(
        functools.partial(stage_kernel, work, names, head_width**-0.5, group),
        grid_spec=pltpu.PrefetchScalarGridSpec(
            num_scalar_prefetch=1,
            grid=(count // group,),
            in_specs=specs,
            out_specs=out_specs,
            scratch_shapes=[pltpu.VMEM((tile, step), F32)] * len(used),
        ),
        out_shape=out_shapes,
        input_output_aliases=aliases,
        compiler_params=pltpu.CompilerParams(vmem_limit_bytes=VMEM_LIMIT),
        cost_estimate=pl.CostEstimate(
            flops=weight * pairs * tile * tile * head_width,
            bytes_accessed=20 * tile * wide,
            transcendentals=0,
        ),
        name="pairs",
    )(far, *args)
    return {**sums, **{name: value for (name, _), value in zip(touched, results)}}


def finish_kernel(factor, backs, own_kv, near, far, own_q, *rest):
    out_q, out_k, out_v = rest[-3:]
    total = own_q[...]
    for back in rest[:backs]:
        total = total + back[...].astype(F32)
    out_q[...] = (total * factor).astype(BF16)
    sums = own_kv[...] + near[...].astype(F32) + far[...].astype(F32)
    out_k[...] = sums[0].astype(BF16)
    out_v[...] = sums[1].astype(BF16)


def finish(first, count, head_width, full, parts, so_far):
    tile = parts[0].shape[1]
    wide = count * head_width
    one = pl.BlockSpec((tile, wide), lambda i: (0, 0))
    two = pl.BlockSpec((2, tile, wide), lambda i: (0, 0, 0))

    def part(array):
        offset = first * head_width if array.shape[2] > wide else 0
        return pl.BlockSpec(
            (pl.Element(2), pl.Element(tile), pl.Element(wide)), lambda i: (0, 0, offset)
        )

    cols = pl.BlockSpec(
        (pl.Element(tile), pl.Element(wide)), lambda i: (0, first * head_width)
    )
    kept = [] if so_far is None else list(so_far)
    return pl.pallas_call(
        functools.partial(finish_kernel, head_width**-0.5, len(parts) - 4),
        grid=(1,),
        in_specs=[two, part(parts[1]), part(parts[2])] + [one] * (len(parts) - 3) + [pl.BlockSpec(memory_space=pl.ANY)] * len(kept),
        out_specs=[cols] * 3,
        out_shape=[jax.ShapeDtypeStruct((tile, full), BF16)] * 3,
        input_output_aliases={len(parts) + i: i for i in range(len(kept))},
        compiler_params=pltpu.CompilerParams(vmem_limit_bytes=VMEM_LIMIT),
        cost_estimate=pl.CostEstimate(
            flops=8 * tile * count * head_width,
            bytes_accessed=30 * tile * count * head_width,
            transcendentals=0,
        ),
        name="finish",
    )(*parts, *kept)


def after(value, *earlier):
    return lax.optimization_barrier((value, *earlier))[0]


def per_device(queries, keys, values, outputs, out_grads, log_sums, window_mask):
    tile, full = queries.shape[2:]
    heads = log_sums.shape[2]
    width = full // heads
    frames, rows = (lax.axis_size("tm"), lax.axis_size("space"))
    q, k, v, o, g = (a.reshape(tile, full) for a in (queries, keys, values, outputs, out_grads))
    partner = [(i, i ^ 1) for i in range(rows)]
    onward = [(i, (i + 2) % rows) for i in range(0, rows, 2)]
    onward += [(i, (i - 2) % rows) for i in range(1, rows, 2)]
    homeward = [(i + 2, i) for i in range(0, rows - 2, 2)]
    homeward += [(i, i + 2) for i in range(1, rows - 2, 2)]
    homeward += [(0, 1), (rows - 1, rows - 2)]
    owners = [(0, 0), (rows - 1, rows - 1)]
    for i in range(1, rows - 1, 2):
        owners += [(i, i + 1), (i + 1, i)]
    near_pairs = [(i, i ^ 1) for i in range(frames)]
    far_pairs = [(0, 0), (frames - 1, frames - 1)]
    for i in range(1, frames - 1, 2):
        far_pairs += [(i, i + 1), (i + 1, i)]

    frame, row = (lax.axis_index("tm"), lax.axis_index("space"))
    far_frame = frame - 1 + 2 * lax.rem(frame, 2)
    has_far = ((far_frame >= 0) & (far_frame < frames)).astype(jnp.int32).reshape(1)
    place = (frame.reshape(1), row.reshape(1))

    firsts = [sum(CHUNKS[:c]) for c in range(len(CHUNKS))]
    lse = log_sums.reshape(heads, 1, tile)
    mask = window_mask.reshape(9)
    own_kv = pack(k, v)
    near_kv = lax.ppermute(own_kv, "tm", near_pairs)
    make = lambda first, counts, source: prep(
        first, counts, width, (frames, rows), place, mask, source, g, o, lse
    )
    mine = make(0, CHUNKS[:1], q)
    theirs = {0: lax.ppermute(mine[0], "space", partner)}
    far_kv = lax.ppermute(after(own_kv, mine[0]), "tm", far_pairs)
    mine += make(firsts[1], CHUNKS[1:], after(q, mine[0]))
    frames_kv = {HERE: own_kv, NEAR: near_kv, FAR: far_kv}
    last = len(CHUNKS) - 1
    outers = {}
    sums = [{} for _ in CHUNKS]
    backs = [{} for _ in CHUNKS]
    done = []
    out = None

    def stage(c, step, *awaited):
        messages = {OUTER: outers.get(c), OWN: mine[c], PARTNER: theirs.get(c)}
        stages = LATER_STAGES if c >= DIRECT else STAGES
        work = stages[step]
        needed = {j: messages[j] for _, js in work for j in js}
        first_used = min(needed)
        arrived = [backs[i][name] for i, name in awaited]
        needed[first_used] = after(needed[first_used], *done[-1:], *arrived)
        later = {j for other in stages[step + 1 :] for _, js in other for j in js}
        slots = {slot for other in stages[step + 1 :] for slot, _ in other}
        straight = (OUTER, PARTNER) if c >= DIRECT else (OUTER,)
        final = {"q%d" % j for j in straight if j not in later}
        final |= {"kv%d" % slot for slot in (NEAR, FAR) if slot not in slots}
        joined = {}
        if c < last and step + 1 == len(stages):
            for name in JOINED:
                joined[name] = (firsts[last] * width, sums[c - 1][name] if c else None)
        sums[c] = run_stage(
            work, WEIGHTS[c][step], final, joined, firsts[c], CHUNKS[c], width, has_far, frames_kv, needed, sums[c]
        )
        done.append(sums[c]["kv0"])
        for name, axis, pairs in (
            ("q0", "space", owners if c >= DIRECT else homeward),
            ("q2", "space", partner),
            ("kv1", "tm", near_pairs),
            ("kv2", "tm", far_pairs),
        ):
            if name not in final or name not in sums[c] or name in backs[c]:
                continue
            if name in joined and (c + 1 < last or ("send", c, name) in ORDER):
                continue
            backs[c][name] = lax.ppermute(sums[c][name], axis, pairs)
            if name in joined:
                for earlier in range(c):
                    backs[earlier][name] = backs[c][name]

    def send_joined(c, name):
        axis_pairs = near_pairs if name == "kv1" else far_pairs
        joined = lax.ppermute(after(sums[c][name], *done[-1:]), "tm", axis_pairs)
        for earlier in range(c + 1):
            backs[earlier][name] = joined

    def hand_on(c):
        outers[c] = lax.ppermute(after(theirs[c], *done[-1:]), "space", onward)

    def send_back(c):
        total = sums[c]["q2"] + after(backs[c]["q0"], *done[-1:]).astype(F32)
        backs[c]["q2"] = lax.ppermute(total.astype(BF16), "space", partner)

    def complete(c, so_far):
        back = backs[c]
        own = after(sums[c]["q1"], *done[-1:])
        from_others = [back["q2"]] + ([back["q0"]] if c >= DIRECT else [])
        so_far = finish(
            firsts[c], CHUNKS[c], width, full,
            (sums[c]["kv0"], back["kv1"], back["kv2"], own, *from_others), so_far,
        )
        done.append(so_far[0])
        return so_far

    for c in range(1, len(CHUNKS)):
        theirs[c] = lax.ppermute(mine[c], "space", partner)
    for kind, c, *rest in ORDER:
        if kind == "stage":
            stage(c, *rest)
        elif kind == "hand":
            hand_on(c)
        elif kind == "back":
            send_back(c)
        elif kind == "send":
            send_joined(c, *rest)
        else:
            out = complete(c, out)
    return tuple(a.reshape(queries.shape) for a in out)


def solution(mesh):
    tile = P("tm", "space", None, None)
    return jax.shard_map(
        per_device,
        mesh=mesh,
        in_specs=(tile,) * 6 + (P("tm", "space", None),),
        out_specs=(tile,) * 3,
        check_vma=False,
    )
```

```python
import functools
import math

import jax
import jax.numpy as jnp
from jax import lax
from jax.experimental import pallas as pl
from jax.experimental.pallas import tpu as pltpu
from jax.sharding import PartitionSpec as P

F32 = jnp.float32
BF16 = jnp.bfloat16
LOG2E = math.log2(math.e)
FAR_AWAY = 1e30

OUTER, OWN, PARTNER = (0, 1, 2)
HERE, NEAR, FAR = (0, 1, 2)
CHUNKS = (4, 5, 3)
STAGES = (
    ((HERE, (OWN,)), (NEAR, (OWN,))),
    ((HERE, (PARTNER,)), (NEAR, (PARTNER,))),
    ((HERE, (OUTER,)), (NEAR, (OUTER,)), (FAR, (OWN, PARTNER, OUTER))),
)
LATER_STAGES = (
    STAGES[0],
    STAGES[1] + ((FAR, (PARTNER,)),),
    ((HERE, (OUTER,)), (NEAR, (OUTER,)), (FAR, (OWN, OUTER))),
)
SECOND_STAGES = (
    STAGES[0],
    ((FAR, (OWN,)),),
    STAGES[1],
    ((HERE, (OUTER,)), (NEAR, (OUTER,)), (FAR, (PARTNER, OUTER))),
)
DIRECT = 2
ORDER = (('stage', 0, 0), ('stage', 1, 0), ('hand', 0), ('stage', 0, 1), ('stage', 2, 0), ('stage', 1, 1), ('hand', 1), ('stage', 0, 2), ('hand', 2), ('stage', 1, 2), ('back', 0), ('stage', 1, 3), ('stage', 2, 1), ('send', 1, 'kv2'), ('back', 1), ('stage', 2, 2, (0, 'q2'), (0, 'kv1')), ('finish', 0), ('finish', 1), ('finish', 2))
JOINED = ('kv2',)
WEIGHTS = ((60, 60, 60), (60, 60, 30, 60), (240, 120, 60))
EXTRA = 16
TERMS = 2
VMEM_LIMIT = 20 * 1024 * 1024
GROUP = 1


def dot(a, b, dims):
    return lax.dot_general(a, b, (dims, ((), ())), preferred_element_type=F32)


def split_terms(row):
    terms = []
    for _ in range(TERMS):
        term = row.astype(BF16).astype(F32)
        terms.append(term)
        row = row - term
    return terms


def fold(row):
    lanes = 128
    return [row[:, i : i + lanes] for i in range(0, row.shape[1], lanes)]


def flag_row(frames, rows, frame, row, mask_ref, lanes):
    toward = 1 - 2 * lax.rem(row, 2)
    near = 1 - 2 * lax.rem(frame, 2)
    lane = lax.broadcasted_iota(jnp.int32, (1, lanes), 1)
    flags = jnp.zeros((1, lanes), F32)
    for role in (OUTER, OWN, PARTNER):
        for slot in (HERE, NEAR, FAR):
            row_off = (role - 1) * toward
            frame_off = (0, near, -near)[slot]
            inside = (
                (row + row_off >= 0)
                & (row + row_off < rows)
                & (frame + frame_off >= 0)
                & (frame + frame_off < frames)
            )
            index = 3 * (frame_off + 1) + row_off + 1
            on = inside & ((mask_ref[index] > 0) | (index == 4))
            flags = jnp.where(lane == 3 * role + slot, on.astype(F32), flags)
    return flags


def prep_kernel(
    counts, frames, rows, frame_ref, row_ref, mask_ref, q_ref, g_ref, o_ref, lse_ref, *outs
):
    tile = q_ref.shape[0]
    width = q_ref.shape[1] // sum(counts)
    flags = flag_row(frames, rows, frame_ref[0], row_ref[0], mask_ref, width)
    ones = jnp.ones((8, width), BF16)
    head = 0
    for out, count in zip(outs, counts):
        for h in range(count):
            source = slice(head * width, (head + 1) * width)
            cols = slice(h * width, (h + 1) * width)
            grad = g_ref[:, source]
            out[0:tile, cols] = q_ref[:, source]
            out[tile : 2 * tile, cols] = grad
            prod = grad.astype(F32) * o_ref[:, source].astype(F32)
            high = prod.astype(BF16)
            low = (prod - high.astype(F32)).astype(BF16)
            delta = dot(ones, high, ((1,), (1,))) + dot(ones, low, ((1,), (1,)))
            lines = []
            for line in (lse_ref[head] * LOG2E, delta[0:1, :]):
                for term in split_terms(line):
                    lines += fold(term)
            lines.append(flags)
            lines.append(jnp.zeros((EXTRA - len(lines), width), F32))
            extra = jnp.concatenate(lines, axis=0).astype(BF16)
            out[2 * tile : 2 * tile + EXTRA, cols] = extra
            head += 1


def prep(first, counts, head_width, sizes, place, mask, q, g, o, lse):
    tile, full = q.shape
    count = sum(counts)
    offset = first * head_width
    cols = pl.BlockSpec(
        (pl.Element(tile), pl.Element(count * head_width)), lambda i, *_: (0, offset)
    )
    shapes = [(2 * tile + EXTRA, n * head_width) for n in counts]
    return pl.pallas_call(
        functools.partial(prep_kernel, counts, *sizes),
        grid_spec=pltpu.PrefetchScalarGridSpec(
            num_scalar_prefetch=3,
            grid=(1,),
            in_specs=[
                cols,
                cols,
                cols,
                pl.BlockSpec(
                    (pl.Element(count), pl.Element(1), pl.Element(tile)),
                    lambda i, *_: (first, 0, 0),
                ),
            ],
            out_specs=[pl.BlockSpec(shape, lambda i, *_: (0, 0)) for shape in shapes],
        ),
        out_shape=[jax.ShapeDtypeStruct(shape, BF16) for shape in shapes],
        compiler_params=pltpu.CompilerParams(vmem_limit_bytes=VMEM_LIMIT),
        cost_estimate=pl.CostEstimate(
            flops=2 * tile * count * head_width,
            bytes_accessed=10 * tile * count * head_width,
            transcendentals=0,
        ),
        name="prep",
    )(*place, mask, *(pltpu.with_memory_space_constraint(a, pltpu.HBM) for a in (q, g, o)), lse)


def pack_kernel(k_ref, v_ref, out):
    out[0] = k_ref[...]
    out[1] = v_ref[...]


def pack(k, v, steps=2):
    tile, full = k.shape
    cols = pl.BlockSpec((tile, full // steps), lambda i: (0, i))
    return pl.pallas_call(
        pack_kernel,
        grid=(steps,),
        in_specs=[cols, cols],
        out_specs=pl.BlockSpec((2, tile, full // steps), lambda i: (0, 0, i)),
        out_shape=jax.ShapeDtypeStruct((2, tile, full), k.dtype),
        compiler_params=pltpu.CompilerParams(vmem_limit_bytes=VMEM_LIMIT),
        cost_estimate=pl.CostEstimate(flops=0, bytes_accessed=8 * k.size, transcendentals=0),
        name="pack",
    )(*(pltpu.with_memory_space_constraint(a, pltpu.HBM) for a in (k, v)))


def row_stats(message, tile):
    extra = message[2 * tile : 2 * tile + EXTRA, :].astype(F32)
    parts = tile // 128
    rows = []
    for base in (0, TERMS * parts):
        pieces = []
        for p in range(parts):
            first = base + p
            terms = [extra[first + i * parts : first + i * parts + 1] for i in range(TERMS)]
            pieces.append(sum(terms[1:], terms[0]))
        rows.append(jnp.concatenate(pieces, axis=1))
    return (rows[0], rows[1], extra[2 * TERMS * parts : 2 * TERMS * parts + 1])


def stage_kernel(work, names, factor, group, far_ref, *refs):
    env = dict(zip(names, refs))
    tile, wide = env["message%d" % work[0][1][0]].shape
    tile = (tile - EXTRA) // 2
    width = wide // group
    heads = [slice(i * width, (i + 1) * width) for i in range(group)]
    used = sorted({j for _, js in work for j in js})
    stats = {
        (j, i): row_stats(env["message%d" % j].at[:, cols], tile)
        for j in used
        for i, cols in enumerate(heads)
    }
    started = set()

    def add_q(j, i, term):
        name, cols = ("q%d" % j, heads[i])
        if (j, i) in started:
            env["sum_" + name][:, cols] += term
        elif "acc_" + name in env:
            env["sum_" + name][:, cols] = env["acc_" + name][:, cols] + term
        else:
            env["sum_" + name][:, cols] = term
        started.add((j, i))

    def pair_terms(slot, j, i):
        cols = heads[i]
        message, keys = (env["message%d" % j], env["keys%d" % slot])
        queries, grads = (message[0:tile, cols], message[tile : 2 * tile, cols])
        key, value = (keys[0, :, cols], keys[1, :, cols])
        shift, delta, flags = stats[j, i]
        lane = 3 * j + slot
        shift = jnp.where(flags[:, lane : lane + 1] > 0, shift, FAR_AWAY)
        scores = dot(key, queries, ((1,), (1,)))
        weights = jnp.exp2(scores * (factor * LOG2E) - shift)
        grad_prob = dot(value, grads, ((1,), (1,)))
        grad_score = (weights * (grad_prob - delta)).astype(BF16)
        term_v = dot(weights.astype(BF16), grads, ((1,), (0,)))
        term_k = dot(grad_score, queries, ((1,), (0,))) * factor
        add_q(j, i, dot(grad_score, key, ((0,), (0,))))
        return (term_k, term_v)

    def key_frames(slots_js):
        for slot, js in slots_js:
            name = "kv%d" % slot
            out = env["out_" + name]
            for i, cols in enumerate(heads):
                dk, dv = (None, None)
                if "acc_" + name in env:
                    acc = env["acc_" + name]
                    dk, dv = (acc[0, :, cols], acc[1, :, cols])
                for j in js:
                    term_k, term_v = pair_terms(slot, j, i)
                    dk = term_k if dk is None else dk + term_k
                    dv = term_v if dv is None else dv + term_v
                out[0, :, cols] = dk.astype(out.dtype)
                out[1, :, cols] = dv.astype(out.dtype)

    key_frames([(slot, js) for slot, js in work if slot != FAR])
    for slot, js in work:
        if slot == FAR:
            fresh = [j for j in js if (j, 0) not in started]
            pl.when(far_ref[0] > 0)(functools.partial(key_frames, [(slot, js)]))

            @pl.when(far_ref[0] == 0)
            def _():
                out = env["out_kv%d" % FAR]
                out[...] = jnp.zeros_like(out)
                for j in fresh:
                    name = "q%d" % j
                    env["sum_" + name][...] = env["acc_" + name][...]

    for j in used:
        out = env["out_q%d" % j]
        out[...] = (env["sum_q%d" % j][...]).astype(out.dtype)


def run_stage(work, weight, last, joined, first, count, head_width, far, keys, messages, sums):
    rows, wide = next(iter(messages.values())).shape
    tile = (rows - EXTRA) // 2
    group = math.gcd(count, GROUP) if first % math.gcd(count, GROUP) == 0 else 1
    step, begin = (group * head_width, first // group)
    one = pl.BlockSpec((tile, step), lambda h, *_: (0, h))
    two = pl.BlockSpec((2, tile, step), lambda h, *_: (0, 0, h))
    cols = pl.BlockSpec((2, tile, step), lambda h, *_: (0, 0, h + begin))
    whole = pl.BlockSpec((rows, step), lambda h, *_: (0, h))
    used = sorted({j for _, js in work for j in js})
    slots = [slot for slot, _ in work]
    names, args, specs = ([], [], [])

    def give(name, arg, spec):
        names.append(name)
        args.append(arg)
        specs.append(spec)

    for j in used:
        give("message%d" % j, messages[j], whole)
    for slot in slots:
        give("keys%d" % slot, keys[slot], cols)
    touched = [("q%d" % j, one) for j in used] + [("kv%d" % s, two) for s in slots]
    for name, spec in touched:
        if name in sums:
            give("acc_" + name, sums[name], spec)
    out_specs, out_shapes, aliases = ([], [], {})
    for name, spec in touched:
        shape = (tile, wide) if name.startswith("q") else (2, tile, wide)
        if name in last and name in joined:
            total, begun = joined[name]
            spec = cols
            shape = (2, tile, total)
            if begun is not None:
                aliases[1 + len(args)] = len(out_specs)
                give("begun_" + name, begun, pl.BlockSpec(memory_space=pl.ANY))
        out_specs.append(spec)
        out_shapes.append(jax.ShapeDtypeStruct(shape, BF16 if name in last else F32))
    names += ["out_" + name for name, _ in touched]
    names += ["sum_q%d" % j for j in used]
    pairs = count * sum(len(js) for _, js in work)
    results = pl.pallas_call(
        functools.partial(stage_kernel, work, names, head_width**-0.5, group),
        grid_spec=pltpu.PrefetchScalarGridSpec(
            num_scalar_prefetch=1,
            grid=(count // group,),
            in_specs=specs,
            out_specs=out_specs,
            scratch_shapes=[pltpu.VMEM((tile, step), F32)] * len(used),
        ),
        out_shape=out_shapes,
        input_output_aliases=aliases,
        compiler_params=pltpu.CompilerParams(vmem_limit_bytes=VMEM_LIMIT),
        cost_estimate=pl.CostEstimate(
            flops=weight * pairs * tile * tile * head_width,
            bytes_accessed=20 * tile * wide,
            transcendentals=0,
        ),
        name="pairs",
    )(far, *args)
    return {**sums, **{name: value for (name, _), value in zip(touched, results)}}


def finish_kernel(factor, backs, own_kv, near, far, own_q, *rest):
    out_q, out_k, out_v = rest[-3:]
    total = own_q[...]
    for back in rest[:backs]:
        total = total + back[...].astype(F32)
    out_q[...] = (total * factor).astype(BF16)
    sums = own_kv[...] + near[...].astype(F32) + far[...].astype(F32)
    out_k[...] = sums[0].astype(BF16)
    out_v[...] = sums[1].astype(BF16)


def finish(first, count, head_width, full, parts, so_far):
    tile = parts[0].shape[1]
    wide = count * head_width
    one = pl.BlockSpec((tile, wide), lambda i: (0, 0))
    two = pl.BlockSpec((2, tile, wide), lambda i: (0, 0, 0))

    def part(array):
        offset = first * head_width if array.shape[2] > wide else 0
        return pl.BlockSpec(
            (pl.Element(2), pl.Element(tile), pl.Element(wide)), lambda i: (0, 0, offset)
        )

    cols = pl.BlockSpec(
        (pl.Element(tile), pl.Element(wide)), lambda i: (0, first * head_width)
    )
    kept = [] if so_far is None else list(so_far)
    return pl.pallas_call(
        functools.partial(finish_kernel, head_width**-0.5, len(parts) - 4),
        grid=(1,),
        in_specs=[two, part(parts[1]), part(parts[2])] + [one] * (len(parts) - 3) + [pl.BlockSpec(memory_space=pl.ANY)] * len(kept),
        out_specs=[cols] * 3,
        out_shape=[jax.ShapeDtypeStruct((tile, full), BF16)] * 3,
        input_output_aliases={len(parts) + i: i for i in range(len(kept))},
        compiler_params=pltpu.CompilerParams(vmem_limit_bytes=VMEM_LIMIT),
        cost_estimate=pl.CostEstimate(
            flops=8 * tile * count * head_width,
            bytes_accessed=30 * tile * count * head_width,
            transcendentals=0,
        ),
        name="finish",
    )(*parts, *kept)


def after(value, *earlier):
    return lax.optimization_barrier((value, *earlier))[0]


def per_device(queries, keys, values, outputs, out_grads, log_sums, window_mask):
    tile, full = queries.shape[2:]
    heads = log_sums.shape[2]
    width = full // heads
    frames, rows = (lax.axis_size("tm"), lax.axis_size("space"))
    q, k, v, o, g = (a.reshape(tile, full) for a in (queries, keys, values, outputs, out_grads))
    partner = [(i, i ^ 1) for i in range(rows)]
    onward = [(i, (i + 2) % rows) for i in range(0, rows, 2)]
    onward += [(i, (i - 2) % rows) for i in range(1, rows, 2)]
    homeward = [(i + 2, i) for i in range(0, rows - 2, 2)]
    homeward += [(i, i + 2) for i in range(1, rows - 2, 2)]
    homeward += [(0, 1), (rows - 1, rows - 2)]
    owners = [(0, 0), (rows - 1, rows - 1)]
    for i in range(1, rows - 1, 2):
        owners += [(i, i + 1), (i + 1, i)]
    near_pairs = [(i, i ^ 1) for i in range(frames)]
    far_pairs = [(0, 0), (frames - 1, frames - 1)]
    for i in range(1, frames - 1, 2):
        far_pairs += [(i, i + 1), (i + 1, i)]

    frame, row = (lax.axis_index("tm"), lax.axis_index("space"))
    far_frame = frame - 1 + 2 * lax.rem(frame, 2)
    has_far = ((far_frame >= 0) & (far_frame < frames)).astype(jnp.int32).reshape(1)
    place = (frame.reshape(1), row.reshape(1))

    firsts = [sum(CHUNKS[:c]) for c in range(len(CHUNKS))]
    lse = log_sums.reshape(heads, 1, tile)
    mask = window_mask.reshape(9)
    own_kv = pack(k, v)
    near_kv = lax.ppermute(own_kv, "tm", near_pairs)
    make = lambda first, counts, source: prep(
        first, counts, width, (frames, rows), place, mask, source, g, o, lse
    )
    mine = make(0, CHUNKS[:1], q)
    theirs = {0: lax.ppermute(mine[0], "space", partner)}
    far_kv = lax.ppermute(after(own_kv, mine[0]), "tm", far_pairs)
    mine += make(firsts[1], CHUNKS[1:], after(q, mine[0]))
    frames_kv = {HERE: own_kv, NEAR: near_kv, FAR: far_kv}
    last = len(CHUNKS) - 1
    outers = {}
    sums = [{} for _ in CHUNKS]
    backs = [{} for _ in CHUNKS]
    done = []
    out = None

    def stage(c, step, *awaited):
        messages = {OUTER: outers.get(c), OWN: mine[c], PARTNER: theirs.get(c)}
        stages = LATER_STAGES if c >= DIRECT else SECOND_STAGES if c == 1 else STAGES
        work = stages[step]
        needed = {j: messages[j] for _, js in work for j in js}
        first_used = min(needed)
        arrived = [backs[i][name] for i, name in awaited]
        needed[first_used] = after(needed[first_used], *done[-1:], *arrived)
        later = {j for other in stages[step + 1 :] for _, js in other for j in js}
        slots = {slot for other in stages[step + 1 :] for slot, _ in other}
        straight = (OUTER, PARTNER) if c >= DIRECT else (OUTER,)
        final = {"q%d" % j for j in straight if j not in later}
        final |= {"kv%d" % slot for slot in (NEAR, FAR) if slot not in slots}
        joined = {}
        if c < last and step + 1 == len(stages):
            for name in JOINED:
                joined[name] = (firsts[last] * width, sums[c - 1][name] if c else None)
        sums[c] = run_stage(
            work, WEIGHTS[c][step], final, joined, firsts[c], CHUNKS[c], width, has_far, frames_kv, needed, sums[c]
        )
        done.append(sums[c]["kv%d" % work[0][0]])
        for name, axis, pairs in (
            ("q0", "space", owners if c >= DIRECT else homeward),
            ("q2", "space", partner),
            ("kv1", "tm", near_pairs),
            ("kv2", "tm", far_pairs),
        ):
            if name not in final or name not in sums[c] or name in backs[c]:
                continue
            if name in joined and (c + 1 < last or ("send", c, name) in ORDER):
                continue
            backs[c][name] = lax.ppermute(sums[c][name], axis, pairs)
            if name in joined:
                for earlier in range(c):
                    backs[earlier][name] = backs[c][name]

    def send_joined(c, name):
        axis_pairs = near_pairs if name == "kv1" else far_pairs
        joined = lax.ppermute(after(sums[c][name], *done[-1:]), "tm", axis_pairs)
        for earlier in range(c + 1):
            backs[earlier][name] = joined

    def hand_on(c):
        outers[c] = lax.ppermute(after(theirs[c], *done[-1:]), "space", onward)

    def send_back(c):
        total = sums[c]["q2"] + after(backs[c]["q0"], *done[-1:]).astype(F32)
        backs[c]["q2"] = lax.ppermute(total.astype(BF16), "space", partner)

    def complete(c, so_far):
        back = backs[c]
        own = after(sums[c]["q1"], *done[-1:])
        from_others = [back["q2"]] + ([back["q0"]] if c >= DIRECT else [])
        so_far = finish(
            firsts[c], CHUNKS[c], width, full,
            (sums[c]["kv0"], back["kv1"], back["kv2"], own, *from_others), so_far,
        )
        done.append(so_far[0])
        return so_far

    for c in range(1, len(CHUNKS)):
        theirs[c] = lax.ppermute(mine[c], "space", partner)
    for kind, c, *rest in ORDER:
        if kind == "stage":
            stage(c, *rest)
        elif kind == "hand":
            hand_on(c)
        elif kind == "back":
            send_back(c)
        elif kind == "send":
            send_joined(c, *rest)
        else:
            out = complete(c, out)
    return tuple(a.reshape(queries.shape) for a in out)


def solution(mesh):
    tile = P("tm", "space", None, None)
    return jax.shard_map(
        per_device,
        mesh=mesh,
        in_specs=(tile,) * 6 + (P("tm", "space", None),),
        out_specs=(tile,) * 3,
        check_vma=False,
    )
```

```python
import functools
import math

import jax
import jax.numpy as jnp
from jax import lax
from jax.experimental import pallas as pl
from jax.experimental.pallas import tpu as pltpu
from jax.sharding import PartitionSpec as P

F32 = jnp.float32
BF16 = jnp.bfloat16
LOG2E = math.log2(math.e)
FAR_AWAY = 1e30

OUTER, OWN, PARTNER = (0, 1, 2)
HERE, NEAR, FAR = (0, 1, 2)
CHUNKS = (4, 5, 3)
STAGES = (
    ((HERE, (OWN,)), (NEAR, (OWN,))),
    ((HERE, (PARTNER,)), (NEAR, (PARTNER,))),
    ((HERE, (OUTER,)), (NEAR, (OUTER,)), (FAR, (OWN, PARTNER, OUTER))),
)
LATER_STAGES = (
    STAGES[0],
    STAGES[1] + ((FAR, (PARTNER,)),),
    ((HERE, (OUTER,)), (NEAR, (OUTER,)), (FAR, (OWN, OUTER))),
)
SECOND_STAGES = (
    STAGES[0],
    ((FAR, (OWN,)),),
    STAGES[1],
    ((HERE, (OUTER,)), (NEAR, (OUTER,)), (FAR, (PARTNER, OUTER))),
)
DIRECT = 2
ORDER = (('stage', 0, 0), ('stage', 1, 0), ('hand', 0), ('stage', 0, 1), ('stage', 2, 0), ('stage', 1, 1), ('hand', 1), ('stage', 0, 2), ('hand', 2), ('stage', 1, 2), ('back', 0), ('stage', 1, 3), ('stage', 2, 1), ('send', 1, 'kv2'), ('back', 1), ('stage', 2, 2, (0, 'q2'), (0, 'kv1')), ('finish', 0), ('finish', 1), ('finish', 2))
JOINED = ('kv2',)
WEIGHTS = ((60, 60, 60), (60, 60, 30, 60), (240, 120, 60))
EXTRA = 16
TERMS = 2
VMEM_LIMIT = 20 * 1024 * 1024
GROUP = 1


def dot(a, b, dims):
    return lax.dot_general(a, b, (dims, ((), ())), preferred_element_type=F32)


def split_terms(row):
    terms = []
    for _ in range(TERMS):
        term = row.astype(BF16).astype(F32)
        terms.append(term)
        row = row - term
    return terms


def fold(row):
    lanes = 128
    return [row[:, i : i + lanes] for i in range(0, row.shape[1], lanes)]


def flag_row(frames, rows, frame, row, mask_ref, lanes):
    toward = 1 - 2 * lax.rem(row, 2)
    near = 1 - 2 * lax.rem(frame, 2)
    lane = lax.broadcasted_iota(jnp.int32, (1, lanes), 1)
    flags = jnp.zeros((1, lanes), F32)
    for role in (OUTER, OWN, PARTNER):
        for slot in (HERE, NEAR, FAR):
            row_off = (role - 1) * toward
            frame_off = (0, near, -near)[slot]
            inside = (
                (row + row_off >= 0)
                & (row + row_off < rows)
                & (frame + frame_off >= 0)
                & (frame + frame_off < frames)
            )
            index = 3 * (frame_off + 1) + row_off + 1
            on = inside & ((mask_ref[index] > 0) | (index == 4))
            flags = jnp.where(lane == 3 * role + slot, on.astype(F32), flags)
    return flags


def prep_kernel(
    counts, frames, rows, frame_ref, row_ref, mask_ref, q_ref, g_ref, o_ref, lse_ref, *outs
):
    tile = q_ref.shape[0]
    width = q_ref.shape[1] // sum(counts)
    flags = flag_row(frames, rows, frame_ref[0], row_ref[0], mask_ref, width)
    ones = jnp.ones((8, width), BF16)
    head = 0
    for out, count in zip(outs, counts):
        for h in range(count):
            source = slice(head * width, (head + 1) * width)
            cols = slice(h * width, (h + 1) * width)
            grad = g_ref[:, source]
            out[0:tile, cols] = q_ref[:, source]
            out[tile : 2 * tile, cols] = grad
            prod = grad.astype(F32) * o_ref[:, source].astype(F32)
            high = prod.astype(BF16)
            low = (prod - high.astype(F32)).astype(BF16)
            delta = dot(ones, high, ((1,), (1,))) + dot(ones, low, ((1,), (1,)))
            lines = []
            for line in (lse_ref[head] * LOG2E, delta[0:1, :]):
                for term in split_terms(line):
                    lines += fold(term)
            lines.append(flags)
            lines.append(jnp.zeros((EXTRA - len(lines), width), F32))
            extra = jnp.concatenate(lines, axis=0).astype(BF16)
            out[2 * tile : 2 * tile + EXTRA, cols] = extra
            head += 1


def prep(first, counts, head_width, sizes, place, mask, q, g, o, lse):
    tile, full = q.shape
    count = sum(counts)
    offset = first * head_width
    cols = pl.BlockSpec(
        (pl.Element(tile), pl.Element(count * head_width)), lambda i, *_: (0, offset)
    )
    shapes = [(2 * tile + EXTRA, n * head_width) for n in counts]
    return pl.pallas_call(
        functools.partial(prep_kernel, counts, *sizes),
        grid_spec=pltpu.PrefetchScalarGridSpec(
            num_scalar_prefetch=3,
            grid=(1,),
            in_specs=[
                cols,
                cols,
                cols,
                pl.BlockSpec(
                    (pl.Element(count), pl.Element(1), pl.Element(tile)),
                    lambda i, *_: (first, 0, 0),
                ),
            ],
            out_specs=[pl.BlockSpec(shape, lambda i, *_: (0, 0)) for shape in shapes],
        ),
        out_shape=[jax.ShapeDtypeStruct(shape, BF16) for shape in shapes],
        compiler_params=pltpu.CompilerParams(vmem_limit_bytes=VMEM_LIMIT),
        cost_estimate=pl.CostEstimate(
            flops=2 * tile * count * head_width,
            bytes_accessed=10 * tile * count * head_width,
            transcendentals=0,
        ),
        name="prep",
    )(*place, mask, *(pltpu.with_memory_space_constraint(a, pltpu.HBM) for a in (q, g, o)), lse)


def pack_kernel(k_ref, v_ref, out):
    out[0] = k_ref[...]
    out[1] = v_ref[...]


def pack(k, v, steps=2):
    tile, full = k.shape
    cols = pl.BlockSpec((tile, full // steps), lambda i: (0, i))
    return pl.pallas_call(
        pack_kernel,
        grid=(steps,),
        in_specs=[cols, cols],
        out_specs=pl.BlockSpec((2, tile, full // steps), lambda i: (0, 0, i)),
        out_shape=jax.ShapeDtypeStruct((2, tile, full), k.dtype),
        compiler_params=pltpu.CompilerParams(vmem_limit_bytes=VMEM_LIMIT),
        cost_estimate=pl.CostEstimate(flops=0, bytes_accessed=8 * k.size, transcendentals=0),
        name="pack",
    )(*(pltpu.with_memory_space_constraint(a, pltpu.HBM) for a in (k, v)))


def row_stats(message, tile):
    extra = message[2 * tile : 2 * tile + EXTRA, :].astype(F32)
    parts = tile // 128
    rows = []
    for base in (0, TERMS * parts):
        pieces = []
        for p in range(parts):
            first = base + p
            terms = [extra[first + i * parts : first + i * parts + 1] for i in range(TERMS)]
            pieces.append(sum(terms[1:], terms[0]))
        rows.append(jnp.concatenate(pieces, axis=1))
    return (rows[0], rows[1], extra[2 * TERMS * parts : 2 * TERMS * parts + 1])


def stage_kernel(work, names, factor, group, far_ref, *refs):
    env = dict(zip(names, refs))
    tile, wide = env["message%d" % work[0][1][0]].shape
    tile = (tile - EXTRA) // 2
    width = wide // group
    heads = [slice(i * width, (i + 1) * width) for i in range(group)]
    used = sorted({j for _, js in work for j in js})
    stats = {
        (j, i): row_stats(env["message%d" % j].at[:, cols], tile)
        for j in used
        for i, cols in enumerate(heads)
    }
    started = set()

    def add_q(j, i, term):
        name, cols = ("q%d" % j, heads[i])
        if (j, i) in started:
            env["sum_" + name][:, cols] += term
        elif "acc_" + name in env:
            env["sum_" + name][:, cols] = env["acc_" + name][:, cols] + term
        else:
            env["sum_" + name][:, cols] = term
        started.add((j, i))

    def pair_terms(slot, j, i):
        cols = heads[i]
        message, keys = (env["message%d" % j], env["keys%d" % slot])
        queries, grads = (message[0:tile, cols], message[tile : 2 * tile, cols])
        key, value = (keys[0, :, cols], keys[1, :, cols])
        shift, delta, flags = stats[j, i]
        lane = 3 * j + slot
        shift = jnp.where(flags[:, lane : lane + 1] > 0, shift, FAR_AWAY)
        scores = dot(key, queries, ((1,), (1,)))
        weights = jnp.exp2(scores * (factor * LOG2E) - shift)
        grad_prob = dot(value, grads, ((1,), (1,)))
        grad_score = (weights * (grad_prob - delta)).astype(BF16)
        term_v = dot(weights.astype(BF16), grads, ((1,), (0,)))
        term_k = dot(grad_score, queries, ((1,), (0,))) * factor
        add_q(j, i, dot(grad_score, key, ((0,), (0,))))
        return (term_k, term_v)

    def key_frames(slots_js):
        for slot, js in slots_js:
            name = "kv%d" % slot
            out = env["out_" + name]
            for i, cols in enumerate(heads):
                dk, dv = (None, None)
                if "acc_" + name in env:
                    acc = env["acc_" + name]
                    dk, dv = (acc[0, :, cols], acc[1, :, cols])
                for j in js:
                    term_k, term_v = pair_terms(slot, j, i)
                    dk = term_k if dk is None else dk + term_k
                    dv = term_v if dv is None else dv + term_v
                out[0, :, cols] = dk.astype(out.dtype)
                out[1, :, cols] = dv.astype(out.dtype)

    key_frames([(slot, js) for slot, js in work if slot != FAR])
    for slot, js in work:
        if slot == FAR:
            fresh = [j for j in js if (j, 0) not in started]
            pl.when(far_ref[0] > 0)(functools.partial(key_frames, [(slot, js)]))

            @pl.when(far_ref[0] == 0)
            def _():
                out = env["out_kv%d" % FAR]
                out[...] = jnp.zeros_like(out)
                for j in fresh:
                    name = "q%d" % j
                    env["sum_" + name][...] = env["acc_" + name][...]

    for j in used:
        out = env["out_q%d" % j]
        out[...] = (env["sum_q%d" % j][...]).astype(out.dtype)


def run_stage(work, weight, last, joined, first, count, head_width, far, keys, messages, sums):
    rows, wide = next(iter(messages.values())).shape
    tile = (rows - EXTRA) // 2
    group = math.gcd(count, GROUP) if first % math.gcd(count, GROUP) == 0 else 1
    step, begin = (group * head_width, first // group)
    one = pl.BlockSpec((tile, step), lambda h, *_: (0, h))
    two = pl.BlockSpec((2, tile, step), lambda h, *_: (0, 0, h))
    cols = pl.BlockSpec((2, tile, step), lambda h, *_: (0, 0, h + begin))
    whole = pl.BlockSpec((rows, step), lambda h, *_: (0, h))
    used = sorted({j for _, js in work for j in js})
    slots = [slot for slot, _ in work]
    names, args, specs = ([], [], [])

    def give(name, arg, spec):
        names.append(name)
        args.append(arg)
        specs.append(spec)

    for j in used:
        give("message%d" % j, messages[j], whole)
    for slot in slots:
        give("keys%d" % slot, keys[slot], cols)
    touched = [("q%d" % j, one) for j in used] + [("kv%d" % s, two) for s in slots]
    for name, spec in touched:
        if name in sums:
            give("acc_" + name, sums[name], spec)
    out_specs, out_shapes, aliases = ([], [], {})
    for name, spec in touched:
        shape = (tile, wide) if name.startswith("q") else (2, tile, wide)
        if name in last and name in joined:
            total, begun = joined[name]
            spec = cols
            shape = (2, tile, total)
            if begun is not None:
                aliases[1 + len(args)] = len(out_specs)
                give("begun_" + name, begun, pl.BlockSpec(memory_space=pl.ANY))
        out_specs.append(spec)
        out_shapes.append(jax.ShapeDtypeStruct(shape, BF16 if name in last else F32))
    names += ["out_" + name for name, _ in touched]
    names += ["sum_q%d" % j for j in used]
    pairs = count * sum(len(js) for _, js in work)
    results = pl.pallas_call(
        functools.partial(stage_kernel, work, names, head_width**-0.5, group),
        grid_spec=pltpu.PrefetchScalarGridSpec(
            num_scalar_prefetch=1,
            grid=(count // group,),
            in_specs=specs,
            out_specs=out_specs,
            scratch_shapes=[pltpu.VMEM((tile, step), F32)] * len(used),
        ),
        out_shape=out_shapes,
        input_output_aliases=aliases,
        compiler_params=pltpu.CompilerParams(vmem_limit_bytes=VMEM_LIMIT),
        cost_estimate=pl.CostEstimate(
            flops=weight * pairs * tile * tile * head_width,
            bytes_accessed=20 * tile * wide,
            transcendentals=0,
        ),
        name="pairs",
    )(far, *args)
    return {**sums, **{name: value for (name, _), value in zip(touched, results)}}


def finish_kernel(factor, backs, own_kv, near, far, own_q, *rest):
    out_q, out_k, out_v = rest[-3:]
    total = own_q[...]
    for back in rest[:backs]:
        total = total + back[...].astype(F32)
    out_q[...] = (total * factor).astype(BF16)
    sums = own_kv[...] + near[...].astype(F32) + far[...].astype(F32)
    out_k[...] = sums[0].astype(BF16)
    out_v[...] = sums[1].astype(BF16)


def finish(first, count, head_width, full, parts, so_far):
    tile = parts[0].shape[1]
    wide = count * head_width
    one = pl.BlockSpec((tile, wide), lambda i: (0, 0))
    two = pl.BlockSpec((2, tile, wide), lambda i: (0, 0, 0))

    def part(array):
        offset = first * head_width if array.shape[2] > wide else 0
        return pl.BlockSpec(
            (pl.Element(2), pl.Element(tile), pl.Element(wide)), lambda i: (0, 0, offset)
        )

    cols = pl.BlockSpec(
        (pl.Element(tile), pl.Element(wide)), lambda i: (0, first * head_width)
    )
    kept = [] if so_far is None else list(so_far)
    return pl.pallas_call(
        functools.partial(finish_kernel, head_width**-0.5, len(parts) - 4),
        grid=(1,),
        in_specs=[two, part(parts[1]), part(parts[2])] + [one] * (len(parts) - 3) + [pl.BlockSpec(memory_space=pl.ANY)] * len(kept),
        out_specs=[cols] * 3,
        out_shape=[jax.ShapeDtypeStruct((tile, full), BF16)] * 3,
        input_output_aliases={len(parts) + i: i for i in range(len(kept))},
        compiler_params=pltpu.CompilerParams(vmem_limit_bytes=VMEM_LIMIT),
        cost_estimate=pl.CostEstimate(
            flops=8 * tile * count * head_width,
            bytes_accessed=30 * tile * count * head_width,
            transcendentals=0,
        ),
        name="finish",
    )(*parts, *kept)


def after(value, *earlier):
    return lax.optimization_barrier((value, *earlier))[0]


def per_device(queries, keys, values, outputs, out_grads, log_sums, window_mask):
    tile, full = queries.shape[2:]
    heads = log_sums.shape[2]
    width = full // heads
    frames, rows = (lax.axis_size("tm"), lax.axis_size("space"))
    q, k, v, o, g = (a.reshape(tile, full) for a in (queries, keys, values, outputs, out_grads))
    partner = [(i, i ^ 1) for i in range(rows)]
    onward = [(i, (i + 2) % rows) for i in range(0, rows, 2)]
    onward += [(i, (i - 2) % rows) for i in range(1, rows, 2)]
    onward_open = [(i, i + 2) for i in range(0, rows - 2, 2)]
    onward_open += [(i, i - 2) for i in range(3, rows, 2)]
    homeward = [(i + 2, i) for i in range(0, rows - 2, 2)]
    homeward += [(i, i + 2) for i in range(1, rows - 2, 2)]
    homeward += [(0, 1), (rows - 1, rows - 2)]
    owners = [(0, 0), (rows - 1, rows - 1)]
    for i in range(1, rows - 1, 2):
        owners += [(i, i + 1), (i + 1, i)]
    near_pairs = [(i, i ^ 1) for i in range(frames)]
    far_pairs = [(0, 0), (frames - 1, frames - 1)]
    for i in range(1, frames - 1, 2):
        far_pairs += [(i, i + 1), (i + 1, i)]

    frame, row = (lax.axis_index("tm"), lax.axis_index("space"))
    far_frame = frame - 1 + 2 * lax.rem(frame, 2)
    has_far = ((far_frame >= 0) & (far_frame < frames)).astype(jnp.int32).reshape(1)
    place = (frame.reshape(1), row.reshape(1))

    firsts = [sum(CHUNKS[:c]) for c in range(len(CHUNKS))]
    lse = log_sums.reshape(heads, 1, tile)
    mask = window_mask.reshape(9)
    own_kv = pack(k, v)
    near_kv = lax.ppermute(own_kv, "tm", near_pairs)
    make = lambda first, counts, source: prep(
        first, counts, width, (frames, rows), place, mask, source, g, o, lse
    )
    mine = make(0, CHUNKS[:1], q)
    theirs = {0: lax.ppermute(mine[0], "space", partner)}
    far_kv = lax.ppermute(after(own_kv, mine[0]), "tm", far_pairs)
    mine += make(firsts[1], CHUNKS[1:], after(q, mine[0]))
    frames_kv = {HERE: own_kv, NEAR: near_kv, FAR: far_kv}
    last = len(CHUNKS) - 1
    outers = {}
    sums = [{} for _ in CHUNKS]
    backs = [{} for _ in CHUNKS]
    done = []
    out = None

    def stage(c, step, *awaited):
        messages = {OUTER: outers.get(c), OWN: mine[c], PARTNER: theirs.get(c)}
        stages = LATER_STAGES if c >= DIRECT else SECOND_STAGES if c == 1 else STAGES
        work = stages[step]
        needed = {j: messages[j] for _, js in work for j in js}
        first_used = min(needed)
        arrived = [backs[i][name] for i, name in awaited]
        needed[first_used] = after(needed[first_used], *done[-1:], *arrived)
        later = {j for other in stages[step + 1 :] for _, js in other for j in js}
        slots = {slot for other in stages[step + 1 :] for slot, _ in other}
        straight = (OUTER, PARTNER) if c >= DIRECT else (OUTER,)
        final = {"q%d" % j for j in straight if j not in later}
        final |= {"kv%d" % slot for slot in (NEAR, FAR) if slot not in slots}
        joined = {}
        if c < last and step + 1 == len(stages):
            for name in JOINED:
                joined[name] = (firsts[last] * width, sums[c - 1][name] if c else None)
        sums[c] = run_stage(
            work, WEIGHTS[c][step], final, joined, firsts[c], CHUNKS[c], width, has_far, frames_kv, needed, sums[c]
        )
        done.append(sums[c]["kv%d" % work[0][0]])
        for name, axis, pairs in (
            ("q0", "space", owners if c >= DIRECT else homeward),
            ("q2", "space", partner),
            ("kv1", "tm", near_pairs),
            ("kv2", "tm", far_pairs),
        ):
            if name not in final or name not in sums[c] or name in backs[c]:
                continue
            if name in joined and (c + 1 < last or ("send", c, name) in ORDER):
                continue
            backs[c][name] = lax.ppermute(sums[c][name], axis, pairs)
            if name in joined:
                for earlier in range(c):
                    backs[earlier][name] = backs[c][name]

    def send_joined(c, name):
        axis_pairs = near_pairs if name == "kv1" else far_pairs
        joined = lax.ppermute(after(sums[c][name], *done[-1:]), "tm", axis_pairs)
        for earlier in range(c + 1):
            backs[earlier][name] = joined

    def hand_on(c):
        chain = onward_open if c == last else onward
        outers[c] = lax.ppermute(after(theirs[c], *done[-1:]), "space", chain)

    def send_back(c):
        total = sums[c]["q2"] + after(backs[c]["q0"], *done[-1:]).astype(F32)
        backs[c]["q2"] = lax.ppermute(total.astype(BF16), "space", partner)

    def complete(c, so_far):
        back = backs[c]
        own = after(sums[c]["q1"], *done[-1:])
        from_others = [back["q2"]] + ([back["q0"]] if c >= DIRECT else [])
        so_far = finish(
            firsts[c], CHUNKS[c], width, full,
            (sums[c]["kv0"], back["kv1"], back["kv2"], own, *from_others), so_far,
        )
        done.append(so_far[0])
        return so_far

    for c in range(1, len(CHUNKS)):
        theirs[c] = lax.ppermute(mine[c], "space", partner)
    for kind, c, *rest in ORDER:
        if kind == "stage":
            stage(c, *rest)
        elif kind == "hand":
            hand_on(c)
        elif kind == "back":
            send_back(c)
        elif kind == "send":
            send_joined(c, *rest)
        else:
            out = complete(c, out)
    return tuple(a.reshape(queries.shape) for a in out)


def solution(mesh):
    tile = P("tm", "space", None, None)
    return jax.shard_map(
        per_device,
        mesh=mesh,
        in_specs=(tile,) * 6 + (P("tm", "space", None),),
        out_specs=(tile,) * 3,
        check_vma=False,
    )
```

```python
import functools
import math

import jax
import jax.numpy as jnp
from jax import lax
from jax.experimental import pallas as pl
from jax.experimental.pallas import tpu as pltpu
from jax.sharding import PartitionSpec as P

F32 = jnp.float32
BF16 = jnp.bfloat16
LOG2E = math.log2(math.e)
FAR_AWAY = 1e30

OUTER, OWN, PARTNER = (0, 1, 2)
HERE, NEAR, FAR = (0, 1, 2)
CHUNKS = (4, 5, 3)
STAGES = (
    ((HERE, (OWN,)), (NEAR, (OWN,))),
    ((HERE, (PARTNER,)), (NEAR, (PARTNER,))),
    ((HERE, (OUTER,)), (NEAR, (OUTER,)), (FAR, (OWN, PARTNER, OUTER))),
)
LATER_STAGES = (
    STAGES[0],
    STAGES[1] + ((FAR, (PARTNER,)),),
    ((HERE, (OUTER,)), (NEAR, (OUTER,)), (FAR, (OWN, OUTER))),
)
SECOND_STAGES = (
    STAGES[0],
    ((FAR, (OWN,)),),
    STAGES[1],
    ((HERE, (OUTER,)), (NEAR, (OUTER,)), (FAR, (PARTNER, OUTER))),
)
DIRECT = 2
ORDER = (('stage', 0, 0), ('stage', 1, 0), ('hand', 0), ('stage', 0, 1), ('stage', 2, 0), ('stage', 1, 1), ('hand', 1), ('stage', 0, 2), ('hand', 2), ('stage', 1, 2), ('back', 0), ('stage', 1, 3), ('stage', 2, 1), ('back', 1), ('stage', 2, 2, (0, 'q2'), (0, 'kv1')), ('finish', 0), ('finish', 1), ('finish', 2))
JOINED = ('kv2',)
WEIGHTS = ((60, 60, 60), (60, 60, 30, 60), (240, 120, 60))
EXTRA = 16
TERMS = 2
VMEM_LIMIT = 20 * 1024 * 1024
GROUP = 1


def dot(a, b, dims):
    return lax.dot_general(a, b, (dims, ((), ())), preferred_element_type=F32)


def split_terms(row):
    terms = []
    for _ in range(TERMS):
        term = row.astype(BF16).astype(F32)
        terms.append(term)
        row = row - term
    return terms


def fold(row):
    lanes = 128
    return [row[:, i : i + lanes] for i in range(0, row.shape[1], lanes)]


def flag_row(frames, rows, frame, row, mask_ref, lanes):
    toward = 1 - 2 * lax.rem(row, 2)
    near = 1 - 2 * lax.rem(frame, 2)
    lane = lax.broadcasted_iota(jnp.int32, (1, lanes), 1)
    flags = jnp.zeros((1, lanes), F32)
    for role in (OUTER, OWN, PARTNER):
        for slot in (HERE, NEAR, FAR):
            row_off = (role - 1) * toward
            frame_off = (0, near, -near)[slot]
            inside = (
                (row + row_off >= 0)
                & (row + row_off < rows)
                & (frame + frame_off >= 0)
                & (frame + frame_off < frames)
            )
            index = 3 * (frame_off + 1) + row_off + 1
            on = inside & ((mask_ref[index] > 0) | (index == 4))
            flags = jnp.where(lane == 3 * role + slot, on.astype(F32), flags)
    return flags


def prep_kernel(
    counts, frames, rows, frame_ref, row_ref, mask_ref, q_ref, g_ref, o_ref, lse_ref, *outs
):
    tile = q_ref.shape[0]
    width = q_ref.shape[1] // sum(counts)
    flags = flag_row(frames, rows, frame_ref[0], row_ref[0], mask_ref, width)
    ones = jnp.ones((8, width), BF16)
    head = 0
    for out, count in zip(outs, counts):
        for h in range(count):
            source = slice(head * width, (head + 1) * width)
            cols = slice(h * width, (h + 1) * width)
            grad = g_ref[:, source]
            out[0:tile, cols] = q_ref[:, source]
            out[tile : 2 * tile, cols] = grad
            prod = grad.astype(F32) * o_ref[:, source].astype(F32)
            high = prod.astype(BF16)
            low = (prod - high.astype(F32)).astype(BF16)
            delta = dot(ones, high, ((1,), (1,))) + dot(ones, low, ((1,), (1,)))
            lines = []
            for line in (lse_ref[head] * LOG2E, delta[0:1, :]):
                for term in split_terms(line):
                    lines += fold(term)
            lines.append(flags)
            lines.append(jnp.zeros((EXTRA - len(lines), width), F32))
            extra = jnp.concatenate(lines, axis=0).astype(BF16)
            out[2 * tile : 2 * tile + EXTRA, cols] = extra
            head += 1


def prep(first, counts, head_width, sizes, place, mask, q, g, o, lse):
    tile, full = q.shape
    count = sum(counts)
    offset = first * head_width
    cols = pl.BlockSpec(
        (pl.Element(tile), pl.Element(count * head_width)), lambda i, *_: (0, offset)
    )
    shapes = [(2 * tile + EXTRA, n * head_width) for n in counts]
    return pl.pallas_call(
        functools.partial(prep_kernel, counts, *sizes),
        grid_spec=pltpu.PrefetchScalarGridSpec(
            num_scalar_prefetch=3,
            grid=(1,),
            in_specs=[
                cols,
                cols,
                cols,
                pl.BlockSpec(
                    (pl.Element(count), pl.Element(1), pl.Element(tile)),
                    lambda i, *_: (first, 0, 0),
                ),
            ],
            out_specs=[pl.BlockSpec(shape, lambda i, *_: (0, 0)) for shape in shapes],
        ),
        out_shape=[jax.ShapeDtypeStruct(shape, BF16) for shape in shapes],
        compiler_params=pltpu.CompilerParams(vmem_limit_bytes=VMEM_LIMIT),
        cost_estimate=pl.CostEstimate(
            flops=2 * tile * count * head_width,
            bytes_accessed=10 * tile * count * head_width,
            transcendentals=0,
        ),
        name="prep",
    )(*place, mask, *(pltpu.with_memory_space_constraint(a, pltpu.HBM) for a in (q, g, o)), lse)


def pack_kernel(k_ref, v_ref, out):
    out[0] = k_ref[...]
    out[1] = v_ref[...]


def pack(k, v, steps=2):
    tile, full = k.shape
    cols = pl.BlockSpec((tile, full // steps), lambda i: (0, i))
    return pl.pallas_call(
        pack_kernel,
        grid=(steps,),
        in_specs=[cols, cols],
        out_specs=pl.BlockSpec((2, tile, full // steps), lambda i: (0, 0, i)),
        out_shape=jax.ShapeDtypeStruct((2, tile, full), k.dtype),
        compiler_params=pltpu.CompilerParams(vmem_limit_bytes=VMEM_LIMIT),
        cost_estimate=pl.CostEstimate(flops=0, bytes_accessed=8 * k.size, transcendentals=0),
        name="pack",
    )(*(pltpu.with_memory_space_constraint(a, pltpu.HBM) for a in (k, v)))


def row_stats(message, tile):
    extra = message[2 * tile : 2 * tile + EXTRA, :].astype(F32)
    parts = tile // 128
    rows = []
    for base in (0, TERMS * parts):
        pieces = []
        for p in range(parts):
            first = base + p
            terms = [extra[first + i * parts : first + i * parts + 1] for i in range(TERMS)]
            pieces.append(sum(terms[1:], terms[0]))
        rows.append(jnp.concatenate(pieces, axis=1))
    return (rows[0], rows[1], extra[2 * TERMS * parts : 2 * TERMS * parts + 1])


def stage_kernel(work, names, factor, group, far_ref, *refs):
    env = dict(zip(names, refs))
    tile, wide = env["message%d" % work[0][1][0]].shape
    tile = (tile - EXTRA) // 2
    width = wide // group
    heads = [slice(i * width, (i + 1) * width) for i in range(group)]
    used = sorted({j for _, js in work for j in js})
    stats = {
        (j, i): row_stats(env["message%d" % j].at[:, cols], tile)
        for j in used
        for i, cols in enumerate(heads)
    }
    started = set()

    def add_q(j, i, term):
        name, cols = ("q%d" % j, heads[i])
        if (j, i) in started:
            env["sum_" + name][:, cols] += term
        elif "acc_" + name in env:
            env["sum_" + name][:, cols] = env["acc_" + name][:, cols] + term
        else:
            env["sum_" + name][:, cols] = term
        started.add((j, i))

    def pair_terms(slot, j, i):
        cols = heads[i]
        message, keys = (env["message%d" % j], env["keys%d" % slot])
        queries, grads = (message[0:tile, cols], message[tile : 2 * tile, cols])
        key, value = (keys[0, :, cols], keys[1, :, cols])
        shift, delta, flags = stats[j, i]
        lane = 3 * j + slot
        shift = jnp.where(flags[:, lane : lane + 1] > 0, shift, FAR_AWAY)
        scores = dot(key, queries, ((1,), (1,)))
        weights = jnp.exp2(scores * (factor * LOG2E) - shift)
        grad_prob = dot(value, grads, ((1,), (1,)))
        grad_score = (weights * (grad_prob - delta)).astype(BF16)
        term_v = dot(weights.astype(BF16), grads, ((1,), (0,)))
        term_k = dot(grad_score, queries, ((1,), (0,))) * factor
        add_q(j, i, dot(grad_score, key, ((0,), (0,))))
        return (term_k, term_v)

    def key_frames(slots_js):
        for slot, js in slots_js:
            name = "kv%d" % slot
            out = env["out_" + name]
            for i, cols in enumerate(heads):
                dk, dv = (None, None)
                if "acc_" + name in env:
                    acc = env["acc_" + name]
                    dk, dv = (acc[0, :, cols], acc[1, :, cols])
                for j in js:
                    term_k, term_v = pair_terms(slot, j, i)
                    dk = term_k if dk is None else dk + term_k
                    dv = term_v if dv is None else dv + term_v
                out[0, :, cols] = dk.astype(out.dtype)
                out[1, :, cols] = dv.astype(out.dtype)

    key_frames([(slot, js) for slot, js in work if slot != FAR])
    for slot, js in work:
        if slot == FAR:
            fresh = [j for j in js if (j, 0) not in started]
            pl.when(far_ref[0] > 0)(functools.partial(key_frames, [(slot, js)]))

            @pl.when(far_ref[0] == 0)
            def _():
                out = env["out_kv%d" % FAR]
                out[...] = jnp.zeros_like(out)
                for j in fresh:
                    name = "q%d" % j
                    env["sum_" + name][...] = env["acc_" + name][...]

    for j in used:
        out = env["out_q%d" % j]
        out[...] = (env["sum_q%d" % j][...]).astype(out.dtype)


def run_stage(work, weight, last, joined, first, count, head_width, far, keys, messages, sums):
    rows, wide = next(iter(messages.values())).shape
    tile = (rows - EXTRA) // 2
    group = math.gcd(count, GROUP) if first % math.gcd(count, GROUP) == 0 else 1
    step, begin = (group * head_width, first // group)
    one = pl.BlockSpec((tile, step), lambda h, *_: (0, h))
    two = pl.BlockSpec((2, tile, step), lambda h, *_: (0, 0, h))
    cols = pl.BlockSpec((2, tile, step), lambda h, *_: (0, 0, h + begin))
    whole = pl.BlockSpec((rows, step), lambda h, *_: (0, h))
    used = sorted({j for _, js in work for j in js})
    slots = [slot for slot, _ in work]
    names, args, specs = ([], [], [])

    def give(name, arg, spec):
        names.append(name)
        args.append(arg)
        specs.append(spec)

    for j in used:
        give("message%d" % j, messages[j], whole)
    for slot in slots:
        give("keys%d" % slot, keys[slot], cols)
    touched = [("q%d" % j, one) for j in used] + [("kv%d" % s, two) for s in slots]
    for name, spec in touched:
        if name in sums:
            give("acc_" + name, sums[name], spec)
    out_specs, out_shapes, aliases = ([], [], {})
    for name, spec in touched:
        shape = (tile, wide) if name.startswith("q") else (2, tile, wide)
        if name in last and name in joined:
            total, begun = joined[name]
            spec = cols
            shape = (2, tile, total)
            if begun is not None:
                aliases[1 + len(args)] = len(out_specs)
                give("begun_" + name, begun, pl.BlockSpec(memory_space=pl.ANY))
        out_specs.append(spec)
        out_shapes.append(jax.ShapeDtypeStruct(shape, BF16 if name in last else F32))
    names += ["out_" + name for name, _ in touched]
    names += ["sum_q%d" % j for j in used]
    pairs = count * sum(len(js) for _, js in work)
    results = pl.pallas_call(
        functools.partial(stage_kernel, work, names, head_width**-0.5, group),
        grid_spec=pltpu.PrefetchScalarGridSpec(
            num_scalar_prefetch=1,
            grid=(count // group,),
            in_specs=specs,
            out_specs=out_specs,
            scratch_shapes=[pltpu.VMEM((tile, step), F32)] * len(used),
        ),
        out_shape=out_shapes,
        input_output_aliases=aliases,
        compiler_params=pltpu.CompilerParams(vmem_limit_bytes=VMEM_LIMIT),
        cost_estimate=pl.CostEstimate(
            flops=weight * pairs * tile * tile * head_width,
            bytes_accessed=20 * tile * wide,
            transcendentals=0,
        ),
        name="pairs",
    )(far, *args)
    return {**sums, **{name: value for (name, _), value in zip(touched, results)}}


def finish_kernel(factor, backs, own_kv, near, far, own_q, *rest):
    out_q, out_k, out_v = rest[-3:]
    total = own_q[...]
    for back in rest[:backs]:
        total = total + back[...].astype(F32)
    out_q[...] = (total * factor).astype(BF16)
    sums = own_kv[...] + near[...].astype(F32) + far[...].astype(F32)
    out_k[...] = sums[0].astype(BF16)
    out_v[...] = sums[1].astype(BF16)


def finish(first, count, head_width, full, parts, so_far):
    tile = parts[0].shape[1]
    wide = count * head_width
    one = pl.BlockSpec((tile, wide), lambda i: (0, 0))
    two = pl.BlockSpec((2, tile, wide), lambda i: (0, 0, 0))

    def part(array):
        offset = first * head_width if array.shape[2] > wide else 0
        return pl.BlockSpec(
            (pl.Element(2), pl.Element(tile), pl.Element(wide)), lambda i: (0, 0, offset)
        )

    cols = pl.BlockSpec(
        (pl.Element(tile), pl.Element(wide)), lambda i: (0, first * head_width)
    )
    kept = [] if so_far is None else list(so_far)
    return pl.pallas_call(
        functools.partial(finish_kernel, head_width**-0.5, len(parts) - 4),
        grid=(1,),
        in_specs=[two, part(parts[1]), part(parts[2])] + [one] * (len(parts) - 3) + [pl.BlockSpec(memory_space=pl.ANY)] * len(kept),
        out_specs=[cols] * 3,
        out_shape=[jax.ShapeDtypeStruct((tile, full), BF16)] * 3,
        input_output_aliases={len(parts) + i: i for i in range(len(kept))},
        compiler_params=pltpu.CompilerParams(vmem_limit_bytes=VMEM_LIMIT),
        cost_estimate=pl.CostEstimate(
            flops=8 * tile * count * head_width,
            bytes_accessed=30 * tile * count * head_width,
            transcendentals=0,
        ),
        name="finish",
    )(*parts, *kept)


def after(value, *earlier):
    return lax.optimization_barrier((value, *earlier))[0]


def per_device(queries, keys, values, outputs, out_grads, log_sums, window_mask):
    tile, full = queries.shape[2:]
    heads = log_sums.shape[2]
    width = full // heads
    frames, rows = (lax.axis_size("tm"), lax.axis_size("space"))
    q, k, v, o, g = (a.reshape(tile, full) for a in (queries, keys, values, outputs, out_grads))
    partner = [(i, i ^ 1) for i in range(rows)]
    onward = [(i, (i + 2) % rows) for i in range(0, rows, 2)]
    onward += [(i, (i - 2) % rows) for i in range(1, rows, 2)]
    onward_open = [(i, i + 2) for i in range(0, rows - 2, 2)]
    onward_open += [(i, i - 2) for i in range(3, rows, 2)]
    homeward = [(i + 2, i) for i in range(0, rows - 2, 2)]
    homeward += [(i, i + 2) for i in range(1, rows - 2, 2)]
    owners = [(0, 0), (rows - 1, rows - 1)]
    for i in range(1, rows - 1, 2):
        owners += [(i, i + 1), (i + 1, i)]
    near_pairs = [(i, i ^ 1) for i in range(frames)]
    far_pairs = [(0, 0), (frames - 1, frames - 1)]
    for i in range(1, frames - 1, 2):
        far_pairs += [(i, i + 1), (i + 1, i)]

    frame, row = (lax.axis_index("tm"), lax.axis_index("space"))
    far_frame = frame - 1 + 2 * lax.rem(frame, 2)
    has_far = ((far_frame >= 0) & (far_frame < frames)).astype(jnp.int32).reshape(1)
    place = (frame.reshape(1), row.reshape(1))

    firsts = [sum(CHUNKS[:c]) for c in range(len(CHUNKS))]
    lse = log_sums.reshape(heads, 1, tile)
    mask = window_mask.reshape(9)
    own_kv = pack(k, v)
    near_kv = lax.ppermute(own_kv, "tm", near_pairs)
    make = lambda first, counts, source: prep(
        first, counts, width, (frames, rows), place, mask, source, g, o, lse
    )
    mine = make(0, CHUNKS[:1], q)
    theirs = {0: lax.ppermute(mine[0], "space", partner)}
    far_kv = lax.ppermute(after(own_kv, mine[0]), "tm", far_pairs)
    mine += make(firsts[1], CHUNKS[1:], after(q, mine[0]))
    frames_kv = {HERE: own_kv, NEAR: near_kv, FAR: far_kv}
    last = len(CHUNKS) - 1
    outers = {}
    sums = [{} for _ in CHUNKS]
    backs = [{} for _ in CHUNKS]
    done = []
    out = None

    def stage(c, step, *awaited):
        messages = {OUTER: outers.get(c), OWN: mine[c], PARTNER: theirs.get(c)}
        stages = LATER_STAGES if c >= DIRECT else SECOND_STAGES if c == 1 else STAGES
        work = stages[step]
        needed = {j: messages[j] for _, js in work for j in js}
        first_used = min(needed)
        arrived = [backs[i][name] for i, name in awaited]
        needed[first_used] = after(needed[first_used], *done[-1:], *arrived)
        later = {j for other in stages[step + 1 :] for _, js in other for j in js}
        slots = {slot for other in stages[step + 1 :] for slot, _ in other}
        straight = (OUTER, PARTNER) if c >= DIRECT else (OUTER,)
        final = {"q%d" % j for j in straight if j not in later}
        final |= {"kv%d" % slot for slot in (NEAR, FAR) if slot not in slots}
        joined = {}
        if c < last and step + 1 == len(stages):
            for name in JOINED:
                joined[name] = (firsts[last] * width, sums[c - 1][name] if c else None)
        sums[c] = run_stage(
            work, WEIGHTS[c][step], final, joined, firsts[c], CHUNKS[c], width, has_far, frames_kv, needed, sums[c]
        )
        done.append(sums[c]["kv%d" % work[0][0]])
        for name, axis, pairs in (
            ("q0", "space", owners if c >= DIRECT else homeward),
            ("q2", "space", partner),
            ("kv1", "tm", near_pairs),
            ("kv2", "tm", far_pairs),
        ):
            if name not in final or name not in sums[c] or name in backs[c]:
                continue
            if name in joined and (c + 1 < last or ("send", c, name) in ORDER):
                continue
            backs[c][name] = lax.ppermute(sums[c][name], axis, pairs)
            if name in joined:
                for earlier in range(c):
                    backs[earlier][name] = backs[c][name]

    def send_joined(c, name):
        axis_pairs = near_pairs if name == "kv1" else far_pairs
        joined = lax.ppermute(after(sums[c][name], *done[-1:]), "tm", axis_pairs)
        for earlier in range(c + 1):
            backs[earlier][name] = joined

    def hand_on(c):
        chain = onward_open if c == last else onward
        outers[c] = lax.ppermute(after(theirs[c], *done[-1:]), "space", chain)

    def send_back(c):
        total = sums[c]["q2"] + after(backs[c]["q0"], *done[-1:]).astype(F32)
        backs[c]["q2"] = lax.ppermute(total.astype(BF16), "space", partner)

    def complete(c, so_far):
        back = backs[c]
        own = after(sums[c]["q1"], *done[-1:])
        from_others = [back["q2"]] + ([back["q0"]] if c >= DIRECT else [])
        so_far = finish(
            firsts[c], CHUNKS[c], width, full,
            (sums[c]["kv0"], back["kv1"], back["kv2"], own, *from_others), so_far,
        )
        done.append(so_far[0])
        return so_far

    for c in range(1, len(CHUNKS)):
        theirs[c] = lax.ppermute(mine[c], "space", partner)
    for kind, c, *rest in ORDER:
        if kind == "stage":
            stage(c, *rest)
        elif kind == "hand":
            hand_on(c)
        elif kind == "back":
            send_back(c)
        elif kind == "send":
            send_joined(c, *rest)
        else:
            out = complete(c, out)
    return tuple(a.reshape(queries.shape) for a in out)


def solution(mesh):
    tile = P("tm", "space", None, None)
    return jax.shard_map(
        per_device,
        mesh=mesh,
        in_specs=(tile,) * 6 + (P("tm", "space", None),),
        out_specs=(tile,) * 3,
        check_vma=False,
    )
```

```python
import functools
import math

import jax
import jax.numpy as jnp
from jax import lax
from jax.experimental import pallas as pl
from jax.experimental.pallas import tpu as pltpu
from jax.sharding import PartitionSpec as P

F32 = jnp.float32
BF16 = jnp.bfloat16
LOG2E = math.log2(math.e)
FAR_AWAY = 1e30

OUTER, OWN, PARTNER = (0, 1, 2)
HERE, NEAR, FAR = (0, 1, 2)
CHUNKS = (4, 5, 3)
STAGES = (
    ((HERE, (OWN,)), (NEAR, (OWN,))),
    ((HERE, (PARTNER,)), (NEAR, (PARTNER,))),
    ((HERE, (OUTER,)), (NEAR, (OUTER,)), (FAR, (OWN, PARTNER, OUTER))),
)
LATER_STAGES = (
    STAGES[0],
    STAGES[1] + ((FAR, (PARTNER,)),),
    ((HERE, (OUTER,)), (NEAR, (OUTER,)), (FAR, (OWN, OUTER))),
)
SECOND_STAGES = (
    STAGES[0],
    ((FAR, (OWN,)),),
    STAGES[1],
    ((HERE, (OUTER,)), (NEAR, (OUTER,)), (FAR, (PARTNER, OUTER))),
)
DIRECT = 2
ORDER = (('stage', 0, 0), ('stage', 1, 0), ('hand', 0), ('stage', 0, 1), ('stage', 2, 0), ('stage', 1, 1), ('hand', 1), ('stage', 0, 2), ('hand', 2), ('stage', 1, 2), ('back', 0), ('stage', 1, 3), ('stage', 2, 1), ('back', 1), ('stage', 2, 2, (0, 'q2'), (0, 'kv1')), ('finish', 0), ('finish', 1), ('finish', 2))
JOINED = ('kv2',)
WEIGHTS = ((60, 60, 60), (60, 60, 30, 60), (240, 120, 60))
EXTRA = 16
TERMS = 2
VMEM_LIMIT = 20 * 1024 * 1024
GROUP = 1


def dot(a, b, dims):
    return lax.dot_general(a, b, (dims, ((), ())), preferred_element_type=F32)


def split_terms(row):
    terms = []
    for _ in range(TERMS):
        term = row.astype(BF16).astype(F32)
        terms.append(term)
        row = row - term
    return terms


def fold(row):
    lanes = 128
    return [row[:, i : i + lanes] for i in range(0, row.shape[1], lanes)]


def flag_row(frames, rows, frame, row, mask_ref, lanes):
    toward = 1 - 2 * lax.rem(row, 2)
    near = 1 - 2 * lax.rem(frame, 2)
    lane = lax.broadcasted_iota(jnp.int32, (1, lanes), 1)
    flags = jnp.zeros((1, lanes), F32)
    for role in (OUTER, OWN, PARTNER):
        for slot in (HERE, NEAR, FAR):
            row_off = (role - 1) * toward
            frame_off = (0, near, -near)[slot]
            inside = (
                (row + row_off >= 0)
                & (row + row_off < rows)
                & (frame + frame_off >= 0)
                & (frame + frame_off < frames)
            )
            index = 3 * (frame_off + 1) + row_off + 1
            on = inside & ((mask_ref[index] > 0) | (index == 4))
            flags = jnp.where(lane == 3 * role + slot, on.astype(F32), flags)
    return flags


def prep_kernel(
    counts, frames, rows, frame_ref, row_ref, mask_ref, q_ref, g_ref, o_ref, lse_ref, *outs
):
    tile = q_ref.shape[0]
    width = q_ref.shape[1] // sum(counts)
    flags = flag_row(frames, rows, frame_ref[0], row_ref[0], mask_ref, width)
    ones = jnp.ones((8, width), BF16)
    head = 0
    for out, count in zip(outs, counts):
        for h in range(count):
            source = slice(head * width, (head + 1) * width)
            cols = slice(h * width, (h + 1) * width)
            grad = g_ref[:, source]
            out[0:tile, cols] = q_ref[:, source]
            out[tile : 2 * tile, cols] = grad
            prod = grad.astype(F32) * o_ref[:, source].astype(F32)
            high = prod.astype(BF16)
            low = (prod - high.astype(F32)).astype(BF16)
            delta = dot(ones, high, ((1,), (1,))) + dot(ones, low, ((1,), (1,)))
            lines = []
            for line in (lse_ref[head] * LOG2E, delta[0:1, :]):
                for term in split_terms(line):
                    lines += fold(term)
            lines.append(flags)
            lines.append(jnp.zeros((EXTRA - len(lines), width), F32))
            extra = jnp.concatenate(lines, axis=0).astype(BF16)
            out[2 * tile : 2 * tile + EXTRA, cols] = extra
            head += 1


def prep(first, counts, head_width, sizes, place, mask, q, g, o, lse):
    tile, full = q.shape
    count = sum(counts)
    offset = first * head_width
    cols = pl.BlockSpec(
        (pl.Element(tile), pl.Element(count * head_width)), lambda i, *_: (0, offset)
    )
    shapes = [(2 * tile + EXTRA, n * head_width) for n in counts]
    return pl.pallas_call(
        functools.partial(prep_kernel, counts, *sizes),
        grid_spec=pltpu.PrefetchScalarGridSpec(
            num_scalar_prefetch=3,
            grid=(1,),
            in_specs=[
                cols,
                cols,
                cols,
                pl.BlockSpec(
                    (pl.Element(count), pl.Element(1), pl.Element(tile)),
                    lambda i, *_: (first, 0, 0),
                ),
            ],
            out_specs=[pl.BlockSpec(shape, lambda i, *_: (0, 0)) for shape in shapes],
        ),
        out_shape=[jax.ShapeDtypeStruct(shape, BF16) for shape in shapes],
        compiler_params=pltpu.CompilerParams(vmem_limit_bytes=VMEM_LIMIT),
        cost_estimate=pl.CostEstimate(
            flops=2 * tile * count * head_width,
            bytes_accessed=10 * tile * count * head_width,
            transcendentals=0,
        ),
        name="prep",
    )(*place, mask, *(pltpu.with_memory_space_constraint(a, pltpu.HBM) for a in (q, g, o)), lse)


def pack_kernel(k_ref, v_ref, out):
    out[0] = k_ref[...]
    out[1] = v_ref[...]


def pack(k, v, steps=2):
    tile, full = k.shape
    cols = pl.BlockSpec((tile, full // steps), lambda i: (0, i))
    return pl.pallas_call(
        pack_kernel,
        grid=(steps,),
        in_specs=[cols, cols],
        out_specs=pl.BlockSpec((2, tile, full // steps), lambda i: (0, 0, i)),
        out_shape=jax.ShapeDtypeStruct((2, tile, full), k.dtype),
        compiler_params=pltpu.CompilerParams(vmem_limit_bytes=VMEM_LIMIT),
        cost_estimate=pl.CostEstimate(flops=0, bytes_accessed=8 * k.size, transcendentals=0),
        name="pack",
    )(*(pltpu.with_memory_space_constraint(a, pltpu.HBM) for a in (k, v)))


def row_stats(message, tile):
    extra = message[2 * tile : 2 * tile + EXTRA, :].astype(F32)
    parts = tile // 128
    rows = []
    for base in (0, TERMS * parts):
        pieces = []
        for p in range(parts):
            first = base + p
            terms = [extra[first + i * parts : first + i * parts + 1] for i in range(TERMS)]
            pieces.append(sum(terms[1:], terms[0]))
        rows.append(jnp.concatenate(pieces, axis=1))
    return (rows[0], rows[1], extra[2 * TERMS * parts : 2 * TERMS * parts + 1])


def stage_kernel(work, names, factor, group, far_ref, *refs):
    env = dict(zip(names, refs))
    tile, wide = env["message%d" % work[0][1][0]].shape
    tile = (tile - EXTRA) // 2
    width = wide // group
    heads = [slice(i * width, (i + 1) * width) for i in range(group)]
    used = sorted({j for _, js in work for j in js})
    stats = {
        (j, i): row_stats(env["message%d" % j].at[:, cols], tile)
        for j in used
        for i, cols in enumerate(heads)
    }
    started = set()

    def add_q(j, i, term):
        name, cols = ("q%d" % j, heads[i])
        if (j, i) in started:
            env["sum_" + name][:, cols] += term
        elif "acc_" + name in env:
            env["sum_" + name][:, cols] = env["acc_" + name][:, cols] + term
        else:
            env["sum_" + name][:, cols] = term
        started.add((j, i))

    def pair_terms(slot, j, i):
        cols = heads[i]
        message, keys = (env["message%d" % j], env["keys%d" % slot])
        queries, grads = (message[0:tile, cols], message[tile : 2 * tile, cols])
        key, value = (keys[0, :, cols], keys[1, :, cols])
        shift, delta, flags = stats[j, i]
        lane = 3 * j + slot
        shift = jnp.where(flags[:, lane : lane + 1] > 0, shift, FAR_AWAY)
        scores = dot(key, queries, ((1,), (1,)))
        weights = jnp.exp2(scores * (factor * LOG2E) - shift)
        grad_prob = dot(value, grads, ((1,), (1,)))
        grad_score = (weights * (grad_prob - delta)).astype(BF16)
        term_v = dot(weights.astype(BF16), grads, ((1,), (0,)))
        term_k = dot(grad_score, queries, ((1,), (0,))) * factor
        add_q(j, i, dot(grad_score, key, ((0,), (0,))))
        return (term_k, term_v)

    def key_frames(slots_js):
        for slot, js in slots_js:
            name = "kv%d" % slot
            out = env["out_" + name]
            for i, cols in enumerate(heads):
                dk, dv = (None, None)
                if "acc_" + name in env:
                    acc = env["acc_" + name]
                    dk, dv = (acc[0, :, cols], acc[1, :, cols])
                for j in js:
                    term_k, term_v = pair_terms(slot, j, i)
                    dk = term_k if dk is None else dk + term_k
                    dv = term_v if dv is None else dv + term_v
                out[0, :, cols] = dk.astype(out.dtype)
                out[1, :, cols] = dv.astype(out.dtype)

    key_frames([(slot, js) for slot, js in work if slot != FAR])
    for slot, js in work:
        if slot == FAR:
            fresh = [j for j in js if (j, 0) not in started]
            pl.when(far_ref[0] > 0)(functools.partial(key_frames, [(slot, js)]))

            @pl.when(far_ref[0] == 0)
            def _():
                out = env["out_kv%d" % FAR]
                out[...] = jnp.zeros_like(out)
                for j in fresh:
                    name = "q%d" % j
                    env["sum_" + name][...] = env["acc_" + name][...]

    for j in used:
        out = env["out_q%d" % j]
        out[...] = (env["sum_q%d" % j][...]).astype(out.dtype)


def run_stage(work, weight, last, joined, first, count, head_width, far, keys, messages, sums):
    rows, wide = next(iter(messages.values())).shape
    tile = (rows - EXTRA) // 2
    group = math.gcd(count, GROUP) if first % math.gcd(count, GROUP) == 0 else 1
    step, begin = (group * head_width, first // group)
    one = pl.BlockSpec((tile, step), lambda h, *_: (0, h))
    two = pl.BlockSpec((2, tile, step), lambda h, *_: (0, 0, h))
    cols = pl.BlockSpec((2, tile, step), lambda h, *_: (0, 0, h + begin))
    whole = pl.BlockSpec((rows, step), lambda h, *_: (0, h))
    used = sorted({j for _, js in work for j in js})
    slots = [slot for slot, _ in work]
    names, args, specs = ([], [], [])

    def give(name, arg, spec):
        names.append(name)
        args.append(arg)
        specs.append(spec)

    for j in used:
        give("message%d" % j, messages[j], whole)
    for slot in slots:
        give("keys%d" % slot, keys[slot], cols)
    touched = [("q%d" % j, one) for j in used] + [("kv%d" % s, two) for s in slots]
    for name, spec in touched:
        if name in sums:
            give("acc_" + name, sums[name], spec)
    out_specs, out_shapes, aliases = ([], [], {})
    for name, spec in touched:
        shape = (tile, wide) if name.startswith("q") else (2, tile, wide)
        if name in last and name in joined:
            total, begun = joined[name]
            spec = cols
            shape = (2, tile, total)
            if begun is not None:
                aliases[1 + len(args)] = len(out_specs)
                give("begun_" + name, begun, pl.BlockSpec(memory_space=pl.ANY))
        out_specs.append(spec)
        out_shapes.append(jax.ShapeDtypeStruct(shape, BF16 if name in last else F32))
    names += ["out_" + name for name, _ in touched]
    names += ["sum_q%d" % j for j in used]
    pairs = count * sum(len(js) for _, js in work)
    results = pl.pallas_call(
        functools.partial(stage_kernel, work, names, head_width**-0.5, group),
        grid_spec=pltpu.PrefetchScalarGridSpec(
            num_scalar_prefetch=1,
            grid=(count // group,),
            in_specs=specs,
            out_specs=out_specs,
            scratch_shapes=[pltpu.VMEM((tile, step), F32)] * len(used),
        ),
        out_shape=out_shapes,
        input_output_aliases=aliases,
        compiler_params=pltpu.CompilerParams(vmem_limit_bytes=VMEM_LIMIT),
        cost_estimate=pl.CostEstimate(
            flops=weight * pairs * tile * tile * head_width,
            bytes_accessed=20 * tile * wide,
            transcendentals=0,
        ),
        name="pairs",
    )(far, *args)
    return {**sums, **{name: value for (name, _), value in zip(touched, results)}}


def finish_kernel(factor, backs, own_kv, near, far, own_q, *rest):
    out_q, out_k, out_v = rest[-3:]
    total = own_q[...]
    for back in rest[:backs]:
        total = total + back[...].astype(F32)
    out_q[...] = (total * factor).astype(BF16)
    sums = own_kv[...] + near[...].astype(F32) + far[...].astype(F32)
    out_k[...] = sums[0].astype(BF16)
    out_v[...] = sums[1].astype(BF16)


def finish(first, count, head_width, full, parts, so_far):
    tile = parts[0].shape[1]
    wide = count * head_width
    one = pl.BlockSpec((tile, wide), lambda i: (0, 0))
    two = pl.BlockSpec((2, tile, wide), lambda i: (0, 0, 0))

    def part(array):
        offset = first * head_width if array.shape[2] > wide else 0
        return pl.BlockSpec(
            (pl.Element(2), pl.Element(tile), pl.Element(wide)), lambda i: (0, 0, offset)
        )

    cols = pl.BlockSpec(
        (pl.Element(tile), pl.Element(wide)), lambda i: (0, first * head_width)
    )
    kept = [] if so_far is None else list(so_far)
    return pl.pallas_call(
        functools.partial(finish_kernel, head_width**-0.5, len(parts) - 4),
        grid=(1,),
        in_specs=[two, part(parts[1]), part(parts[2])] + [one] * (len(parts) - 3) + [pl.BlockSpec(memory_space=pl.ANY)] * len(kept),
        out_specs=[cols] * 3,
        out_shape=[jax.ShapeDtypeStruct((tile, full), BF16)] * 3,
        input_output_aliases={len(parts) + i: i for i in range(len(kept))},
        compiler_params=pltpu.CompilerParams(vmem_limit_bytes=VMEM_LIMIT),
        cost_estimate=pl.CostEstimate(
            flops=8 * tile * count * head_width,
            bytes_accessed=30 * tile * count * head_width,
            transcendentals=0,
        ),
        name="finish",
    )(*parts, *kept)


def after(value, *earlier):
    return lax.optimization_barrier((value, *earlier))[0]


def per_device(queries, keys, values, outputs, out_grads, log_sums, window_mask):
    tile, full = queries.shape[2:]
    heads = log_sums.shape[2]
    width = full // heads
    frames, rows = (lax.axis_size("tm"), lax.axis_size("space"))
    q, k, v, o, g = (a.reshape(tile, full) for a in (queries, keys, values, outputs, out_grads))
    partner = [(i, i ^ 1) for i in range(rows)]
    onward = [(i, (i + 2) % rows) for i in range(0, rows, 2)]
    onward += [(i, (i - 2) % rows) for i in range(1, rows, 2)]
    onward_open = [(i, i + 2) for i in range(0, rows - 2, 2)]
    onward_open += [(i, i - 2) for i in range(3, rows, 2)]
    homeward = [(i + 2, i) for i in range(0, rows - 2, 2)]
    homeward += [(i, i + 2) for i in range(1, rows - 2, 2)]
    owners = [(0, 0), (rows - 1, rows - 1)]
    for i in range(1, rows - 1, 2):
        owners += [(i, i + 1), (i + 1, i)]
    near_pairs = [(i, i ^ 1) for i in range(frames)]
    far_pairs = [(0, 0), (frames - 1, frames - 1)]
    for i in range(1, frames - 1, 2):
        far_pairs += [(i, i + 1), (i + 1, i)]

    frame, row = (lax.axis_index("tm"), lax.axis_index("space"))
    far_frame = frame - 1 + 2 * lax.rem(frame, 2)
    has_far = ((far_frame >= 0) & (far_frame < frames)).astype(jnp.int32).reshape(1)
    place = (frame.reshape(1), row.reshape(1))

    firsts = [sum(CHUNKS[:c]) for c in range(len(CHUNKS))]
    lse = log_sums.reshape(heads, 1, tile)
    mask = window_mask.reshape(9)
    own_kv = pack(k, v)
    near_kv = lax.ppermute(own_kv, "tm", near_pairs)
    make = lambda first, counts, source: prep(
        first, counts, width, (frames, rows), place, mask, source, g, o, lse
    )
    mine = make(0, CHUNKS[:1], q)
    theirs = {0: lax.ppermute(mine[0], "space", partner)}
    far_kv = lax.ppermute(after(own_kv, mine[0]), "tm", far_pairs)
    mine += make(firsts[1], CHUNKS[1:], after(q, mine[0]))
    frames_kv = {HERE: own_kv, NEAR: near_kv, FAR: far_kv}
    last = len(CHUNKS) - 1
    outers = {}
    sums = [{} for _ in CHUNKS]
    backs = [{} for _ in CHUNKS]
    done = []
    out = None

    def stage(c, step, *awaited):
        messages = {OUTER: outers.get(c), OWN: mine[c], PARTNER: theirs.get(c)}
        stages = LATER_STAGES if c >= DIRECT else SECOND_STAGES if c == 1 else STAGES
        work = stages[step]
        needed = {j: messages[j] for _, js in work for j in js}
        first_used = min(needed)
        arrived = [backs[i][name] for i, name in awaited]
        needed[first_used] = after(needed[first_used], *done[-1:], *arrived)
        later = {j for other in stages[step + 1 :] for _, js in other for j in js}
        slots = {slot for other in stages[step + 1 :] for slot, _ in other}
        straight = (OUTER, PARTNER) if c >= DIRECT else (OUTER,)
        final = {"q%d" % j for j in straight if j not in later}
        final |= {"kv%d" % slot for slot in (NEAR, FAR) if slot not in slots}
        joined = {}
        if c < last and step + 1 == len(stages):
            for name in JOINED:
                joined[name] = (firsts[last] * width, sums[c - 1][name] if c else None)
        sums[c] = run_stage(
            work, WEIGHTS[c][step], final, joined, firsts[c], CHUNKS[c], width, has_far, frames_kv, needed, sums[c]
        )
        done.append(sums[c]["kv%d" % work[0][0]])
        for name, axis, pairs in (
            ("q0", "space", owners if c >= DIRECT else homeward),
            ("q2", "space", partner),
            ("kv1", "tm", near_pairs),
            ("kv2", "tm", far_pairs),
        ):
            if name not in final or name not in sums[c] or name in backs[c]:
                continue
            if name in joined and (c + 1 < last or ("send", c, name) in ORDER):
                continue
            backs[c][name] = lax.ppermute(sums[c][name], axis, pairs)
            if name in joined:
                for earlier in range(c):
                    backs[earlier][name] = backs[c][name]

    def send_joined(c, name):
        axis_pairs = near_pairs if name == "kv1" else far_pairs
        joined = lax.ppermute(after(sums[c][name], *done[-1:]), "tm", axis_pairs)
        for earlier in range(c + 1):
            backs[earlier][name] = joined

    def hand_on(c):
        chain = onward_open if c else onward
        outers[c] = lax.ppermute(after(theirs[c], *done[-1:]), "space", chain)

    def send_back(c):
        total = sums[c]["q2"] + after(backs[c]["q0"], *done[-1:]).astype(F32)
        backs[c]["q2"] = lax.ppermute(total.astype(BF16), "space", partner)

    def complete(c, so_far):
        back = backs[c]
        own = after(sums[c]["q1"], *done[-1:])
        from_others = [back["q2"]] + ([back["q0"]] if c >= DIRECT else [])
        so_far = finish(
            firsts[c], CHUNKS[c], width, full,
            (sums[c]["kv0"], back["kv1"], back["kv2"], own, *from_others), so_far,
        )
        done.append(so_far[0])
        return so_far

    for c in range(1, len(CHUNKS)):
        theirs[c] = lax.ppermute(mine[c], "space", partner)
    for kind, c, *rest in ORDER:
        if kind == "stage":
            stage(c, *rest)
        elif kind == "hand":
            hand_on(c)
        elif kind == "back":
            send_back(c)
        elif kind == "send":
            send_joined(c, *rest)
        else:
            out = complete(c, out)
    return tuple(a.reshape(queries.shape) for a in out)


def solution(mesh):
    tile = P("tm", "space", None, None)
    return jax.shard_map(
        per_device,
        mesh=mesh,
        in_specs=(tile,) * 6 + (P("tm", "space", None),),
        out_specs=(tile,) * 3,
        check_vma=False,
    )
```
